128 devices in a mesh: gauss: 8 (over y, core), render: 16 (over x, z).
Axes of the slice: x: 4, y: 4, z: 4, core: 2. Of those that a mesh axis runs over, the one named last changes fastest.
Arguments:
- params: float32 [59, 262144], P(None, ('gauss', 'render')), as said below
- first_moment: float32 [59, 262144], P(None, ('gauss', 'render')), may hold values from -1.5 to 1.5
- second_moment: float32 [59, 262144], P(None, ('gauss', 'render')), may hold values from 0.0001 to 0.01
- target_images: float32 [4096, 3, 256], P(('gauss', 'render')), may hold values from 0 to 1
- tile_lists: int32 [4096, 512], P(('gauss', 'render')), may hold values from -1 to 16383, as said below
- send_index: int32 [128, 128, 128], P(('gauss', 'render')), may hold values from 0 to 2047, as said below
Outputs:
- images: float32 [4096, 3, 256], P(('gauss', 'render'))
- new_params: float32 [59, 262144], P(None, ('gauss', 'render'))
- new_first: float32 [59, 262144], P(None, ('gauss', 'render'))
- new_second: float32 [59, 262144], P(None, ('gauss', 'render'))
The draws below stay inside these ranges and needn't reach their ends.
Inputs may be any that keep to these rules, and one draw needn't show every extreme that they name: `tile_lists`: A live entry names slot s * 128 + j of its device's received slots: the j-th Gaussian that device s sends it. Each tile's live entries come first, at least 64 of them; every tile of some device has all 512 entries live. On one device every named slot is named by exactly one entry. send_index[s, d, j] is the local index on owner s of the Gaussian sent as slot j to renderer d; slots that no list of d names hold 0. No Gaussian is sent twice to one renderer. Some renderer uses every slot from every owner. `params`: row 6, the quaternion's real part, lies between 1 and 2.
All inputs are finite; a program needn't handle non-finite values.
Results may differ from the reference program's by a relative error of at most 0.0003.
Values sent between devices are 32-bit elements; how exact they have to be, the bound alone decides.
A program may use at most 128 MiB of HBM per device.

```python
import math
import jax
import jax.numpy as jnp
import numpy as np
from jax import lax

PARAMS = 59
PIX = 256
VIEWS = 16
TILE_COLS = 8
LIST = 512
GROUP = 4
TILE_DEV = 32
GS_DEV = 2048
DPV = 8
TPV = 256
CELLS_X = 11
CELLS = 385
CAP = 128
NG = 262144
TILES = 4096
DEVICES = 128


def layout(key):
    key_low, key_high, key_busy, key_order = jax.random.split(key, 4)
    draw_low = jax.random.randint(key_low, (CELLS,), LIST // 8, LIST + 1)
    draw_high = jax.random.randint(key_high, (CELLS,), LIST // 8, LIST + 1)
    counts = jnp.minimum(draw_low, draw_high)
    busiest = jax.random.randint(key_busy, (), 0, DEVICES)
    placed = busiest % DPV * TILE_DEV + jnp.arange(TILE_DEV)
    camera = busiest // DPV
    busy_cells = (placed // TILE_COLS + camera // 4) * CELLS_X + placed % TILE_COLS + camera % 4
    counts = counts.at[busy_cells].set(LIST)
    starts = jnp.cumsum(counts) - counts
    orders = jax.vmap(lambda subkey: jax.random.permutation(subkey, GS_DEV))(jax.random.split(key_order, DEVICES))
    return (counts.astype(jnp.int32), starts.astype(jnp.int32), orders.astype(jnp.int32))


def cell_of_tile(tiles):
    camera = tiles // TILE_DEV // DPV
    placed = tiles % TPV
    return (placed // TILE_COLS + camera // 4) * CELLS_X + placed % TILE_COLS + camera % 4


def draw_tile_lists(key, part):
    counts, starts, orders = layout(key)
    tiles = jnp.arange(TILES)
    cell_idx = cell_of_tile(tiles)
    ranks = jnp.arange(LIST)[None, :]
    ordinal = starts[cell_idx][:, None] + ranks
    source = ordinal % DEVICES
    within = (tiles % TILE_DEV)[:, None]
    slot_idx = source * CAP + within * (LIST // DEVICES) + ranks // DEVICES
    return jnp.where(ranks < counts[cell_idx][:, None], slot_idx, -1).astype(jnp.int32)


def draw_send_index(key, part):
    counts, starts, orders = layout(key)
    source = jnp.arange(DEVICES)[:, None, None]
    renderer = jnp.arange(DEVICES)[None, :, None]
    column = jnp.arange(CAP)[None, None, :]
    per_cell = LIST // DEVICES
    cell_idx = cell_of_tile(renderer * TILE_DEV + column // per_cell)
    opening = starts[cell_idx]
    ranking = (source - opening) % DEVICES + DEVICES * (column % per_cell)
    ordinal = opening + ranking
    usable = ranking < counts[cell_idx]
    local_idx = orders[source, jnp.minimum(ordinal // DEVICES, GS_DEV - 1)]
    return jnp.where(usable, local_idx, 0).astype(jnp.int32)


def draw_params(key, part):
    counts, starts, orders = layout(key)
    key = jax.random.fold_in(key, 17)
    subkeys = jax.random.split(key, 9)
    inverse = jnp.argsort(orders, axis=1).astype(jnp.int32)
    ordinal = (inverse * DEVICES + jnp.arange(DEVICES, dtype=jnp.int32)[:, None]).reshape(-1)
    total = starts[-1] + counts[-1]
    listed = ordinal < total
    home = jnp.clip(jnp.searchsorted(starts, ordinal, side='right') - 1, 0, CELLS - 1)
    cell_idx = jnp.where(listed, home, jax.random.randint(subkeys[0], (NG,), 0, CELLS))
    jitter = jax.random.uniform(subkeys[1], (3, NG), dtype=jnp.float32)
    rank_frac = (ordinal - starts[home]).astype(jnp.float32) + jitter[2]
    height = jnp.where(listed, 16.0 * (1.0 - rank_frac / counts[home].astype(jnp.float32)), 16.0 * jitter[2])
    mean_x = 16.0 * (cell_idx % CELLS_X).astype(jnp.float32) + 2.0 + 12.0 * jitter[0]
    mean_y = 16.0 * (cell_idx // CELLS_X).astype(jnp.float32) + 2.0 + 12.0 * jitter[1]
    real_part = jax.random.uniform(subkeys[2], (1, NG), minval=1.0, maxval=2.0)
    key_pick, key_solid = jax.random.split(subkeys[8], 2)
    solid = jax.random.uniform(key_pick, (1, NG)) < 0.04
    dense_logit = jax.random.uniform(key_solid, (1, NG), minval=5.5, maxval=7.5)
    log_scale = jnp.log(jax.random.uniform(subkeys[3], (3, NG), minval=1.0, maxval=3.0))
    imaginary = jnp.clip(0.5 * jax.random.normal(subkeys[4], (3, NG)), -1.5, 1.5)
    faint_logit = jnp.clip(-3.5 + 0.6 * jax.random.normal(subkeys[5], (1, NG)), -5.0, -2.0)
    harmonics = jnp.clip(0.25 * jax.random.normal(subkeys[6], (3, 16, NG)), -0.6, 0.6)
    base_colour = jnp.clip(0.9 * jax.random.normal(subkeys[7], (3, 1, NG)), -3.0, 3.0)
    opacity = jnp.where(solid, dense_logit, faint_logit)
    harmonics = jnp.concatenate([base_colour, harmonics[:, 1:]], axis=1).reshape(48, NG)
    stacked = jnp.concatenate([mean_x[None], mean_y[None], height[None], log_scale, real_part, imaginary, opacity, harmonics], axis=0)
    return stacked.astype(jnp.float32)


def block_scale(rng, extent, pieces, low, largest):
    level = 1.0
    for position, shards_of in pieces:
        heights = jax.random.uniform(jax.random.fold_in(jax.random.fold_in(rng, 6), position), (shards_of,), jnp.float32, low / len(pieces), largest / len(pieces))
        level = level * jnp.repeat(jnp.exp(heights), extent[position] // shards_of).reshape((-1,) + (1,) * (len(extent) - 1 - position))
    return level


def bell_draw(own_key, extent, scale, reach, cuts=(), kind=jnp.bfloat16):
    factor_of = block_scale(own_key, extent, cuts, -0.22, 0.18) if cuts else 1.0
    result = jax.random.normal(own_key, extent, jnp.float32) * scale * factor_of
    return jnp.minimum(jnp.maximum(result, -reach), reach).astype(kind)


def setup_inputs(seed: int = 0) -> dict:
    streams_of = jax.random.split(jax.random.key(seed), 7)
    params = draw_params(jax.random.fold_in(streams_of[6], 71), 0)
    first_moment = bell_draw(streams_of[1], (PARAMS, NG), 0.1, 1.5, ((1, 128),), jnp.float32)
    second_moment = jnp.clip(jnp.exp(math.log(0.01) - 4.6051702 * jax.random.uniform(streams_of[2], (PARAMS, NG), jnp.float32) ** block_scale(streams_of[2], (PARAMS, NG), ((1, 128),), -0.2, 0.2)), 0.0001, 0.01)
    target_images = jnp.clip(1.0 * jax.random.uniform(streams_of[3], (TILES, 3, PIX), jnp.float32) ** block_scale(streams_of[3], (TILES, 3, PIX), ((0, 128),), -0.2, 0.2), 0.0, 1.0)
    tile_lists = draw_tile_lists(jax.random.fold_in(streams_of[6], 71), 0)
    send_index = draw_send_index(jax.random.fold_in(streams_of[6], 71), 0)
    return {"params": params, "first_moment": first_moment, "second_moment": second_moment, "target_images": target_images, "tile_lists": tile_lists, "send_index": send_index}


sh_first = 0.28209479177387814
sh_second = 0.4886025119029199
sh_third = (1.0925484305920792, -1.0925484305920792, 0.31539156525252005, -1.0925484305920792, 0.5462742152960396)
sh_fourth = (-0.5900435899266435, 2.890611442640554, -0.4570457994644658, 0.3731763325901154, -0.4570457994644658, 1.445305721320277, -0.5900435899266435)
tilt_reach = 0.25
beta_one = 0.9
beta_two = 0.999
adam_epsilon = 1e-15
adam_count = 1000.0

def learning_rates():
    table = np.full((PARAMS,), 0.000125)
    table[0:3] = 0.0016
    table[3:6] = 0.005
    table[6:10] = 0.001
    table[10] = 0.05
    table[11] = 0.0025
    table[27] = 0.0025
    table[43] = 0.0025
    return jnp.asarray(table, dtype=jnp.float32)

def sh_basis(dir_x, dir_y, dir_z):
    sq_x = dir_x * dir_x
    sq_y = dir_y * dir_y
    sq_z = dir_z * dir_z
    return [sh_first * jnp.ones_like(dir_x), -sh_second * dir_y, sh_second * dir_z, -sh_second * dir_x, sh_third[0] * dir_x * dir_y, sh_third[1] * dir_y * dir_z, sh_third[2] * (2.0 * sq_z - sq_x - sq_y), sh_third[3] * dir_x * dir_z, sh_third[4] * (sq_x - sq_y), sh_fourth[0] * dir_y * (3.0 * sq_x - sq_y), sh_fourth[1] * dir_x * dir_y * dir_z, sh_fourth[2] * dir_y * (4.0 * sq_z - sq_x - sq_y), sh_fourth[3] * dir_z * (2.0 * sq_z - 3.0 * sq_x - 3.0 * sq_y), sh_fourth[4] * dir_x * (4.0 * sq_z - sq_x - sq_y), sh_fourth[5] * dir_z * (sq_x - sq_y), sh_fourth[6] * dir_x * (sq_x - 3.0 * sq_y)]

def project(raw_params, camera):
    angle = camera.astype(jnp.float32) * (2.0 * math.pi / VIEWS)
    lean_x = tilt_reach * jnp.cos(angle)
    lean_y = tilt_reach * jnp.sin(angle)
    shift_x = 16.0 * (camera % 4).astype(jnp.float32)
    shift_y = 16.0 * (camera // 4).astype(jnp.float32)
    length = jnp.sqrt(1.0 + lean_x * lean_x + lean_y * lean_y)
    basis = sh_basis(lean_x / length, lean_y / length, -1.0 / length)
    screen_x = raw_params[0] + lean_x * raw_params[2] - shift_x
    screen_y = raw_params[1] + lean_y * raw_params[2] - shift_y
    squares = [jnp.exp(2.0 * raw_params[3 + axis_position]) for axis_position in range(3)]
    quat_norm = jnp.sqrt(raw_params[6] * raw_params[6] + raw_params[7] * raw_params[7] + raw_params[8] * raw_params[8] + raw_params[9] * raw_params[9])
    q_w = raw_params[6] / quat_norm
    q_x = raw_params[7] / quat_norm
    q_y = raw_params[8] / quat_norm
    q_z = raw_params[9] / quat_norm
    rotation = [[1.0 - 2.0 * (q_y * q_y + q_z * q_z), 2.0 * (q_x * q_y - q_w * q_z), 2.0 * (q_x * q_z + q_w * q_y)], [2.0 * (q_x * q_y + q_w * q_z), 1.0 - 2.0 * (q_x * q_x + q_z * q_z), 2.0 * (q_y * q_z - q_w * q_x)], [2.0 * (q_x * q_z - q_w * q_y), 2.0 * (q_y * q_z + q_w * q_x), 1.0 - 2.0 * (q_x * q_x + q_y * q_y)]]
    footprint_spread = [[rotation[row_at][0] * rotation[col_at][0] * squares[0] + rotation[row_at][1] * rotation[col_at][1] * squares[1] + rotation[row_at][2] * rotation[col_at][2] * squares[2] for col_at in range(3)] for row_at in range(3)]
    cov_xx = footprint_spread[0][0] + 2.0 * lean_x * footprint_spread[0][2] + lean_x * lean_x * footprint_spread[2][2] + 0.3
    cov_xy = footprint_spread[0][1] + lean_x * footprint_spread[1][2] + lean_y * footprint_spread[0][2] + lean_x * lean_y * footprint_spread[2][2]
    cov_yy = footprint_spread[1][1] + 2.0 * lean_y * footprint_spread[1][2] + lean_y * lean_y * footprint_spread[2][2] + 0.3
    determinant = cov_xx * cov_yy - cov_xy * cov_xy
    opacity = jax.nn.sigmoid(raw_params[10])
    colours = [jnp.maximum(0.5 + sum((raw_params[11 + 16 * channel + term] * basis[term] for term in range(16))), 0.0) for channel in range(3)]
    screen_x, screen_y, opacity = jnp.broadcast_arrays(screen_x, screen_y, opacity)
    stacked = [screen_x, screen_y, cov_yy / determinant, -cov_xy / determinant, cov_xx / determinant, opacity] + colours
    return jnp.stack(jnp.broadcast_arrays(*stacked))

def tile_corner_points(placed):
    anchor_x = 16.0 * (placed % TILE_COLS).astype(jnp.float32)
    anchor_y = 16.0 * (placed // TILE_COLS).astype(jnp.float32)
    return (anchor_x, anchor_y)

def composite(feature_vectors, live_mask, anchor_x, anchor_y):
    pixels = jnp.arange(PIX, dtype=jnp.int32)
    offset_x = (pixels % 16).astype(jnp.float32) + 0.5
    offset_y = (pixels // 16).astype(jnp.float32) + 0.5
    delta_x = anchor_x[:, None, None] + offset_x[None, None, :] - feature_vectors[:, 0, :, None]
    delta_y = anchor_y[:, None, None] + offset_y[None, None, :] - feature_vectors[:, 1, :, None]
    exponent = -0.5 * (feature_vectors[:, 2, :, None] * delta_x * delta_x + feature_vectors[:, 4, :, None] * delta_y * delta_y) - feature_vectors[:, 3, :, None] * delta_x * delta_y
    alpha_values = jnp.minimum(feature_vectors[:, 5, :, None] * jnp.exp(exponent), 0.99) * live_mask[:, :, None]
    log_keep = jnp.log(1.0 - alpha_values)
    transmittance = jnp.exp(jnp.cumsum(log_keep, axis=1) - log_keep)
    return jnp.einsum('dwo,doy->dwy', feature_vectors[:, 6:9, :], alpha_values * transmittance, precision=lax.Precision.HIGHEST)

def render_tiles(feature_vectors, live_mask, anchor_x, anchor_y, target):
    groups = feature_vectors.shape[0] // GROUP

    def one_group(bundle):
        feats_g, live_g, tile_left_edge, top_edge, target_g = bundle
        shaded, pullback = jax.vjp(lambda values: composite(values, live_g, tile_left_edge, top_edge), feats_g)
        feat_grad, = pullback(shaded - target_g)
        return (shaded, feat_grad)
    bundle = tuple((member.reshape((groups, GROUP) + member.shape[1:]) for member in (feature_vectors, live_mask, anchor_x, anchor_y, target)))
    shaded, feat_grad = lax.map(one_group, bundle)
    return (shaded.reshape(target.shape), feat_grad.reshape(feature_vectors.shape))

def adam_step(params, first_moment, second_moment, gradient):
    rates = learning_rates()
    new_first = beta_one * first_moment + (1.0 - beta_one) * gradient
    new_second = beta_two * second_moment + (1.0 - beta_two) * gradient * gradient
    first_hat = new_first / (1.0 - beta_one ** adam_count)
    second_hat = new_second / (1.0 - beta_two ** adam_count)
    new_params = params - rates[:, None] * first_hat / (jnp.sqrt(second_hat) + adam_epsilon)
    return (new_params, new_first, new_second)

def reference(params, first_moment, second_moment, target_images, tile_lists, send_index):

    def device_block(gradient, device):
        lists_here = lax.dynamic_slice_in_dim(tile_lists, device * TILE_DEV, TILE_DEV, 0)
        target_here = lax.dynamic_slice_in_dim(target_images, device * TILE_DEV, TILE_DEV, 0)
        entry_idx = jnp.maximum(lists_here, 0)
        source = entry_idx // CAP
        column = entry_idx % CAP
        gauss_ids = (source * GS_DEV + send_index[source, device, column]).astype(jnp.int32)
        live_mask = (lists_here >= 0).astype(jnp.float32)
        camera = device // DPV
        raw_entries = params[:, gauss_ids]
        feature_vectors, pullback = jax.vjp(lambda values: project(values, camera), raw_entries)
        placed = device % DPV * TILE_DEV + jnp.arange(TILE_DEV, dtype=jnp.int32)
        anchor_x, anchor_y = tile_corner_points(placed)
        shaded, feat_grad = render_tiles(jnp.moveaxis(feature_vectors, 0, 1), live_mask, anchor_x, anchor_y, target_here)
        raw_grad, = pullback(jnp.moveaxis(feat_grad, 1, 0))
        gradient = gradient.at[:, gauss_ids].add(raw_grad)
        return (gradient, shaded)
    gradient, shaded = lax.scan(device_block, jnp.zeros((PARAMS, NG), jnp.float32), jnp.arange(DEVICES, dtype=jnp.int32))
    new_params, new_first, new_second = adam_step(params, first_moment, second_moment, gradient)
    return (shaded.reshape(TILES, 3, PIX), new_params, new_first, new_second)
```

```python
import functools
import math

import jax
import jax.numpy as jnp
import numpy as np
from jax import lax
from jax.experimental import pallas as pl
from jax.experimental.pallas import tpu as pltpu
from jax.sharding import PartitionSpec as P

PARAMS = 59
PIX = 256
VIEWS = 16
LIST = 512
TILE_DEV = 32
GS_DEV = 2048
DEVICES = 128
CAP = 128
FEATS = 9
BLOCKS = 16
PROWS = 64
LANES = 128
SLABS = 4
LOG2E = 1.4426950408889634
AXES = ("gauss", "render")
VMEM_LIMIT = 56 * 1024 * 1024

sh_first = 0.28209479177387814
sh_second = 0.4886025119029199
sh_third = (
    1.0925484305920792,
    -1.0925484305920792,
    0.31539156525252005,
    -1.0925484305920792,
    0.5462742152960396,
)
sh_fourth = (
    -0.5900435899266435,
    2.890611442640554,
    -0.4570457994644658,
    0.3731763325901154,
    -0.4570457994644658,
    1.445305721320277,
    -0.5900435899266435,
)
tilt_reach = 0.25
beta_one = 0.9
beta_two = 0.999
adam_epsilon = 1e-15
adam_count = 1000.0


def rate_table():
    table = np.full((PARAMS,), 0.000125)
    table[0:3] = 0.0016
    table[3:6] = 0.005
    table[6:10] = 0.001
    table[10] = 0.05
    table[11] = 0.0025
    table[27] = 0.0025
    table[43] = 0.0025
    return np.broadcast_to(table.astype(np.float32)[:, None], (PARAMS, LANES))


def sh_basis(dir_x, dir_y, dir_z):
    sq_x = dir_x * dir_x
    sq_y = dir_y * dir_y
    sq_z = dir_z * dir_z
    return [
        sh_first,
        -sh_second * dir_y,
        sh_second * dir_z,
        -sh_second * dir_x,
        sh_third[0] * dir_x * dir_y,
        sh_third[1] * dir_y * dir_z,
        sh_third[2] * (2.0 * sq_z - sq_x - sq_y),
        sh_third[3] * dir_x * dir_z,
        sh_third[4] * (sq_x - sq_y),
        sh_fourth[0] * dir_y * (3.0 * sq_x - sq_y),
        sh_fourth[1] * dir_x * dir_y * dir_z,
        sh_fourth[2] * dir_y * (4.0 * sq_z - sq_x - sq_y),
        sh_fourth[3] * dir_z * (2.0 * sq_z - 3.0 * sq_x - 3.0 * sq_y),
        sh_fourth[4] * dir_x * (4.0 * sq_z - sq_x - sq_y),
        sh_fourth[5] * dir_z * (sq_x - sq_y),
        sh_fourth[6] * dir_x * (sq_x - 3.0 * sq_y),
    ]


def camera_constants(camera):
    angle = camera * (2.0 * math.pi / VIEWS)
    lean_x = tilt_reach * math.cos(angle)
    lean_y = tilt_reach * math.sin(angle)
    length = math.sqrt(1.0 + lean_x * lean_x + lean_y * lean_y)
    basis = sh_basis(lean_x / length, lean_y / length, -1.0 / length)
    return (lean_x, lean_y, 16.0 * (camera % 4), 16.0 * (camera // 4), basis)


CAMERAS = [camera_constants(camera) for camera in range(VIEWS)]


def spread(log_scales, quat):
    squares = [jnp.exp(2.0 * value) for value in log_scales]
    norm = jnp.sqrt(quat[0] * quat[0] + quat[1] * quat[1] + quat[2] * quat[2] + quat[3] * quat[3])
    q_w, q_x, q_y, q_z = [part / norm for part in quat]
    rotation = [
        [
            1.0 - 2.0 * (q_y * q_y + q_z * q_z),
            2.0 * (q_x * q_y - q_w * q_z),
            2.0 * (q_x * q_z + q_w * q_y),
        ],
        [
            2.0 * (q_x * q_y + q_w * q_z),
            1.0 - 2.0 * (q_x * q_x + q_z * q_z),
            2.0 * (q_y * q_z - q_w * q_x),
        ],
        [
            2.0 * (q_x * q_z - q_w * q_y),
            2.0 * (q_y * q_z + q_w * q_x),
            1.0 - 2.0 * (q_x * q_x + q_y * q_y),
        ],
    ]
    return [
        rotation[row][0] * rotation[col][0] * squares[0]
        + rotation[row][1] * rotation[col][1] * squares[1]
        + rotation[row][2] * rotation[col][2] * squares[2]
        for row, col in ((0, 0), (0, 1), (0, 2), (1, 1), (1, 2), (2, 2))
    ]


def conic_of(sigma, lean_x, lean_y):
    s_xx, s_xy, s_xz, s_yy, s_yz, s_zz = sigma
    cov_xx = s_xx + (2.0 * lean_x) * s_xz + (lean_x * lean_x) * s_zz + 0.3
    cov_xy = s_xy + lean_x * s_yz + lean_y * s_xz + (lean_x * lean_y) * s_zz
    cov_yy = s_yy + (2.0 * lean_y) * s_yz + (lean_y * lean_y) * s_zz + 0.3
    inverse = 1.0 / (cov_xx * cov_yy - cov_xy * cov_xy)
    return cov_yy * inverse, -cov_xy * inverse, cov_xx * inverse


def raw_colour(row, basis, channel):
    total = 0.5 + row(11 + 16 * channel) * basis[0]
    for term in range(1, 16):
        total = total + row(11 + 16 * channel + term) * basis[term]
    return total


def block_rows(source, dest):
    rows = source.shape[0]
    for block in range(BLOCKS):
        dest[pl.ds(block * PROWS, rows), :] = source[:, pl.ds(block * LANES, LANES)]


def strided(ref, row):
    return ref[pl.ds(row, BLOCKS, stride=PROWS), :]


def parts_of(value, count):
    parts = []
    for step in range(count):
        part = value.astype(jnp.bfloat16)
        parts.append(part)
        if step + 1 < count:
            value = value - part.astype(jnp.float32)
    return parts


def project_kernel(params_ref, index_ref, out_ref, rows_ref, table_ref):
    block_rows(params_ref, rows_ref)
    row = functools.partial(strided, rows_ref)
    sigma = spread([row(3 + k) for k in range(3)], [row(6 + k) for k in range(4)])
    logit = row(10)
    log_opacity = -LOG2E * (jnp.maximum(-logit, 0.0) + jnp.log1p(jnp.exp(-jnp.abs(logit))))
    for camera in range(VIEWS):
        lean_x, lean_y, shift_x, shift_y, basis = CAMERAS[camera]
        height = row(2)
        features = [row(0) + lean_x * height - shift_x, row(1) + lean_y * height - shift_y]
        features += list(conic_of(sigma, lean_x, lean_y))
        features.append(log_opacity)
        features += [jnp.maximum(raw_colour(row, basis, k), 0.0) for k in range(3)]
        for f in range(FEATS):
            table_ref[pl.ds((camera * FEATS + f) * BLOCKS, BLOCKS), :] = features[f]

    @pl.loop(0, VIEWS)
    def _(camera):
        chosen = index_ref[pl.ds(pl.multiple_of(camera * 8, 8), 8), :]
        low = jnp.bitwise_and(chosen, LANES - 1)
        high = jnp.right_shift(chosen, 7)
        totals = [jnp.zeros((8, LANES), jnp.float32) for _ in range(FEATS)]
        for block in range(BLOCKS):
            here = high == block
            for f in range(FEATS):
                line = table_ref[pl.ds((camera * FEATS + f) * BLOCKS + block, 1), :]
                line = jnp.broadcast_to(line, (8, LANES))
                picked = jnp.take_along_axis(line, low, axis=1)
                totals[f] = jnp.where(here, picked, totals[f])
        for f in range(FEATS):
            out_ref[pl.ds(camera * 8 * FEATS + f, 8, stride=FEATS), :] = totals[f]


def invert_kernel(list_ref, lane_ref, row_ref):
    sublane = lax.broadcasted_iota(jnp.int32, (LANES, LANES), 0)
    lane = lax.broadcasted_iota(jnp.int32, (LANES, LANES), 1).astype(jnp.float32)

    def step(pair, total):
        owners, slots = [], []
        for member in range(2):
            line = list_ref[pl.ds(pair * 2 + member, 1), :]
            low = jnp.broadcast_to(jnp.bitwise_and(line, CAP - 1), (LANES, LANES))
            high = jnp.broadcast_to(jnp.right_shift(line, 7), (LANES, LANES))
            number = (pair * 2 + member + 1).astype(jnp.float32)
            owners.append(jnp.where(high == sublane, 1.0, 0.0).astype(jnp.bfloat16))
            same = low == sublane
            slots.append(
                jnp.concatenate([jnp.where(same, lane, 0.0), jnp.where(same, number, 0.0)], 0).astype(
                    jnp.bfloat16
                )
            )
        return total + lax.dot_general(
            jnp.concatenate(owners, 1),
            jnp.concatenate(slots, 1),
            (((1,), (1,)), ((), ())),
            preferred_element_type=jnp.float32,
        )

    total = lax.fori_loop(0, LANES // 2, step, jnp.zeros((LANES, 2 * LANES), jnp.float32), unroll=4)
    lane_ref[...] = total[:, :LANES].astype(jnp.int32)
    row_ref[...] = total[:, LANES:].astype(jnp.int32) - 1


def lane_gather(table, stride_row, stride_feature, low, high, store):
    spans = len(low)

    def step(source, totals):
        totals = list(totals)
        here = [h == source for h in high]
        for f in range(FEATS):
            line = table[pl.ds(source * stride_row + f * stride_feature, 1), :]
            line = jnp.broadcast_to(line, (8, LANES))
            for u in range(spans):
                picked = jnp.take_along_axis(line, low[u], axis=1)
                totals[f * spans + u] = jnp.where(here[u], picked, totals[f * spans + u])
        return tuple(totals)

    blank = tuple(jnp.zeros((8, LANES), jnp.float32) for _ in range(FEATS * spans))
    totals = lax.fori_loop(0, LANES, step, blank, unroll=16)
    for f in range(FEATS):
        for u in range(spans):
            store(f, u, totals[f * spans + u])


KROWS = 32
GRADS = 16
GROUP_ROWS = LIST * 8


def render_kernel(
    table_ref,
    list_ref,
    lane_ref,
    row_ref,
    target_ref,
    expand_ref,
    mono_ref,
    image_ref,
    back_ref,
    feat_ref,
    coef_ref,
    alpha_ref,
    weight_ref,
    colour_ref,
    push_ref,
    grad_ref,
    moment_ref,
):
    render = lax.axis_index(AXES[1])
    device = lax.axis_index(AXES[0]) * lax.axis_size(AXES[1]) + render
    strip = lax.rem(device, DEVICES // VIEWS)
    lane_tile = jnp.bitwise_and(lax.broadcasted_iota(jnp.int32, (8, LANES), 1), 7)
    centre_x = 16.0 * lane_tile.astype(jnp.float32) + 8.0

    @pl.loop(0, 8)
    def _(part):
        spans = [pl.ds(pl.multiple_of(part * 16 + u * 8, 8), 8) for u in range(2)]
        entries = [list_ref[span, :] for span in spans]
        low = [jnp.bitwise_and(entry, CAP - 1) for entry in entries]
        high = [jnp.right_shift(entry, 7) for entry in entries]

        def store(f, u, value):
            feat_ref[pl.ds(pl.multiple_of(f * LANES + part * 16 + u * 8, 8), 8), :] = value

        lane_gather(table_ref, FEATS, 1, low, high, store)

    zero = jnp.zeros((8, LANES), jnp.float32)

    @pl.loop(0, 16)
    def _(octet):
        base = pl.multiple_of(octet * 8, 8)
        feature = [feat_ref[pl.ds(pl.multiple_of(f * LANES + octet * 8, 8), 8), :] for f in range(FEATS)]
        live = list_ref[pl.ds(base, 8), :] >= 0
        centre_y = (16 * (strip * SLABS + octet // 4) + 8).astype(jnp.float32)
        m_x = feature[0] - centre_x
        m_y = feature[1] - centre_y
        a = (-0.5 * LOG2E) * feature[2]
        b = -LOG2E * feature[3]
        c = (-0.5 * LOG2E) * feature[4]
        to_x = 2.0 * a * m_x + b * m_y
        to_y = b * m_x + 2.0 * c * m_y
        level = a * m_x * m_x + b * m_x * m_y + c * m_y * m_y
        level = jnp.where(live, level + feature[5], -10000.0)
        values = [a, b, c, -to_x, -to_y, level] + feature[6:9]
        place = 0
        for value in values:
            for part in parts_of(value, 3):
                coef_ref[pl.ds(octet * 8 * KROWS + place, 8, stride=KROWS), :] = part.astype(jnp.float32)
                place += 1
        for rest in range(place, KROWS):
            coef_ref[pl.ds(octet * 8 * KROWS + rest, 8, stride=KROWS), :] = zero

    diagonal = lax.broadcasted_iota(jnp.int32, (8, LANES), 0) == lane_tile

    @pl.loop(0, SLABS)
    def _(group):
        @pl.loop(0, 32, unroll=2)
        def _(line):
            start = pl.multiple_of((group * 32 + line) * KROWS, KROWS)
            left = coef_ref[pl.ds(start, KROWS), :].T.astype(jnp.bfloat16)
            wide = jnp.dot(left, expand_ref[...], preferred_element_type=jnp.float32)
            out = pl.ds(pl.multiple_of(line * LANES, LANES), LANES)
            alpha_ref[out, :] = wide[:, :PIX]
            colour_ref[out, :] = wide[:, PIX:]

        def forward(block, carry):
            through = list(carry[:2])
            image = list(carry[2:])
            for u in range(16):
                here = pl.ds(pl.multiple_of(block * LANES + u * 8, 8), 8)
                shade = [colour_ref[here, pl.ds(k * LANES, LANES)] for k in range(3)]
                for half in range(2):
                    cols = pl.ds(half * LANES, LANES)
                    alpha = jnp.minimum(jnp.exp2(alpha_ref[here, cols]), 0.99)
                    weight = alpha * through[half]
                    through[half] = through[half] * (1.0 - alpha)
                    alpha_ref[here, cols] = alpha
                    weight_ref[here, cols] = weight
                    for k in range(3):
                        image[k * 2 + half] = image[k * 2 + half] + shade[k] * weight
            return tuple(through + image)

        ones = jnp.ones((8, LANES), jnp.float32)
        image = lax.fori_loop(0, 32, forward, (ones, ones) + (zero,) * 6)[2:]
        residual = []
        tiles = pl.ds(pl.multiple_of(group * 8, 8), 8)
        for k in range(3):
            for half in range(2):
                cols = pl.ds(k * PIX + half * LANES, LANES)
                image_ref[tiles, cols] = image[k * 2 + half]
                residual.append(image[k * 2 + half] - target_ref[tiles, cols])

        def backward(count, carry):
            behind = list(carry)
            block = 31 - count
            for pair in range(7, -1, -1):
                pushes = [[None, None], [None, None]]
                for member in (1, 0):
                    here = pl.ds(pl.multiple_of(block * LANES + pair * 16 + member * 8, 8), 8)
                    shade = [colour_ref[here, pl.ds(k * LANES, LANES)] for k in range(3)]
                    for half in range(2):
                        cols = pl.ds(half * LANES, LANES)
                        alpha = alpha_ref[here, cols]
                        weight = weight_ref[here, cols]
                        worth = (
                            shade[0] * residual[half]
                            + shade[1] * residual[2 + half]
                            + shade[2] * residual[4 + half]
                        )
                        gain = worth - behind[half]
                        behind[half] = behind[half] + alpha * gain
                        pushes[half][member] = jnp.where(alpha < 0.99, weight * gain, 0.0)
                rows = pl.ds(pl.multiple_of(block * LANES + pair * 16, 16), 16)
                for half in range(2):
                    value = jnp.concatenate(pushes[half], 0)
                    for which, part in enumerate(parts_of(value, 2)):
                        push_ref[which, rows, pl.ds(half * LANES, LANES)] = part
            return tuple(behind)

        lax.fori_loop(0, 32, backward, (zero, zero))
        stack = jnp.concatenate(
            [jnp.concatenate([residual[k * 2], residual[k * 2 + 1]], 1) for k in range(3)], 0
        )
        stack = jnp.concatenate(parts_of(stack, 2), 0)
        contract = (((1,), (1,)), ((), ()))

        @pl.loop(0, 8)
        def _(chunk):
            rows = pl.ds(pl.multiple_of(chunk * 512, 512), 512)
            moments = lax.dot_general(
                mono_ref[...], push_ref[0, rows, :], contract, preferred_element_type=jnp.float32
            ) + lax.dot_general(
                mono_ref[...], push_ref[1, rows, :], contract, preferred_element_type=jnp.float32
            )
            tints = 0.0
            for part in parts_of(weight_ref[rows, :], 2):
                tints = tints + lax.dot_general(stack, part, contract, preferred_element_type=jnp.float32)
            tints = tints[:24] + tints[24:]
            for line in range(4):
                cols = slice(line * LANES, (line + 1) * LANES)
                base = ((group * 32) + chunk * 4 + line) * GRADS
                moment_ref[pl.ds(pl.multiple_of(base, 8), 8), :] = moments[:8, cols]
                for k in range(3):
                    own = jnp.where(diagonal, tints[k * 8 : k * 8 + 8, cols], 0.0)
                    moment_ref[pl.ds(base + 8 + k, 1), :] = jnp.sum(own, 0, keepdims=True)

    @pl.loop(0, 16)
    def _(octet):
        feature = [feat_ref[pl.ds(pl.multiple_of(f * LANES + octet * 8, 8), 8), :] for f in range(5)]
        centre_y = (16 * (strip * SLABS + octet // 4) + 8).astype(jnp.float32)
        m_x = feature[0] - centre_x
        m_y = feature[1] - centre_y

        def moment(k):
            return moment_ref[pl.ds(octet * 8 * GRADS + k, 8, stride=GRADS), :]

        total, s_x, s_y, s_xx, s_xy, s_yy = [moment(k) for k in range(6)]
        along_x = s_x - m_x * total
        along_y = s_y - m_y * total
        results = [
            feature[2] * along_x + feature[3] * along_y,
            feature[3] * along_x + feature[4] * along_y,
            -0.5 * (s_xx - m_x * (s_x + along_x)),
            -(s_xy - m_x * s_y - m_y * along_x),
            -0.5 * (s_yy - m_y * (s_y + along_y)),
            total,
            moment(8),
            moment(9),
            moment(10),
        ]
        for f in range(FEATS):
            grad_ref[pl.ds(pl.multiple_of(f * LANES + octet * 8, 8), 8), :] = results[f]

    @pl.loop(0, 8)
    def _(part):
        spans = [pl.ds(pl.multiple_of(part * 16 + u * 8, 8), 8) for u in range(2)]
        low = [lane_ref[span, :] for span in spans]
        high = [row_ref[span, :] for span in spans]

        def store(f, u, value):
            back_ref[pl.ds((part * 16 + u * 8) * FEATS + f, 8, stride=FEATS), :] = value

        lane_gather(grad_ref, 1, LANES, low, high, store)


SUM_PARTS = 2


def update_kernel(
    back_ref, index_ref, params_ref, first_ref, second_ref, rate_ref,
    new_params_ref, new_first_ref, new_second_ref,
    rows_ref, sums_ref, slope_ref, tint_ref,
):
    block_rows(params_ref, rows_ref)
    row = functools.partial(strided, rows_ref)
    sublane = lax.broadcasted_iota(jnp.int32, (LANES, LANES), 0)
    short = lax.broadcasted_iota(jnp.int32, (BLOCKS, LANES), 0)

    @pl.loop(0, VIEWS)
    def _(camera):
        total = jnp.zeros((SUM_PARTS * FEATS * BLOCKS, LANES), jnp.float32)
        for pair in range(4):
            places, values = [], []
            for member in range(2):
                renderer = camera * 8 + pair * 2 + member
                line = index_ref[pl.ds(renderer, 1), :]
                low = jnp.broadcast_to(jnp.bitwise_and(line, LANES - 1), (LANES, LANES))
                high = jnp.broadcast_to(jnp.right_shift(line, 7), (BLOCKS, LANES))
                places.append(jnp.where(low == sublane, 1.0, 0.0).astype(jnp.bfloat16))
                here = high == short
                stacks = []
                for f in range(FEATS):
                    value = jnp.broadcast_to(back_ref[pl.ds(renderer * FEATS + f, 1), :], (BLOCKS, LANES))
                    stacks.append(jnp.where(here, value, 0.0))
                stack = jnp.concatenate(stacks, 0)
                values.append(jnp.concatenate(parts_of(stack, SUM_PARTS), 0))
            total = total + lax.dot_general(
                jnp.concatenate(values, 1),
                jnp.concatenate(places, 1),
                (((1,), (1,)), ((), ())),
                preferred_element_type=jnp.float32,
            )
        size = FEATS * BLOCKS
        merged = total[:size]
        for part in range(1, SUM_PARTS):
            merged = merged + total[part * size : (part + 1) * size]
        sums_ref[pl.ds(pl.multiple_of(camera * size, size), size), :] = merged

    logs = [row(3 + k) for k in range(3)]
    quat = [row(6 + k) for k in range(4)]
    sigma, spread_pull = jax.vjp(spread, logs, quat)
    blank = jnp.zeros((BLOCKS, LANES), jnp.float32)
    d_sigma = [blank] * 6
    d_x, d_y, d_z, d_log = blank, blank, blank, blank
    for camera in range(VIEWS):
        lean_x, lean_y, _, _, basis = CAMERAS[camera]

        def pushed(f):
            return sums_ref[pl.ds((camera * FEATS + f) * BLOCKS, BLOCKS), :]

        d_x = d_x + pushed(0)
        d_y = d_y + pushed(1)
        d_z = d_z + lean_x * pushed(0) + lean_y * pushed(1)
        _, pull = jax.vjp(lambda values: conic_of(values, lean_x, lean_y), sigma)
        (more,) = pull((pushed(2), pushed(3), pushed(4)))
        d_sigma = [old + new for old, new in zip(d_sigma, more)]
        d_log = d_log + pushed(5)
        for k in range(3):
            raw = raw_colour(row, basis, k)
            gate = jnp.where(raw > 0.0, 1.0, jnp.where(raw == 0.0, 0.5, 0.0))
            tint_ref[pl.ds((k * VIEWS + camera) * BLOCKS, BLOCKS), :] = gate * pushed(6 + k)
    d_scale, d_quat = spread_pull(d_sigma)
    slopes = [d_x, d_y, d_z] + list(d_scale) + list(d_quat) + [d_log / (1.0 + jnp.exp(row(10)))]
    for number, slope in enumerate(slopes):
        slope_ref[pl.ds(number, BLOCKS, stride=PROWS), :] = slope
    for k in range(3):
        for term in range(16):
            slope = blank
            for camera in range(VIEWS):
                tint = tint_ref[pl.ds((k * VIEWS + camera) * BLOCKS, BLOCKS), :]
                slope = slope + CAMERAS[camera][4][term] * tint
            slope_ref[pl.ds(11 + 16 * k + term, BLOCKS, stride=PROWS), :] = slope
    rates = rate_ref[...]
    for block in range(BLOCKS):
        cols = pl.ds(block * LANES, LANES)
        slope = slope_ref[pl.ds(block * PROWS, PARAMS), :]
        new_first = beta_one * first_ref[:, cols] + (1.0 - beta_one) * slope
        new_second = beta_two * second_ref[:, cols] + (1.0 - beta_two) * slope * slope
        first_hat = new_first / (1.0 - beta_one**adam_count)
        second_hat = new_second / (1.0 - beta_two**adam_count)
        new_first_ref[:, cols] = new_first
        new_second_ref[:, cols] = new_second
        new_params_ref[:, cols] = params_ref[:, cols] - rates * first_hat / (
            jnp.sqrt(second_hat) + adam_epsilon
        )


WHOLE = pl.BlockSpec(memory_space=pltpu.VMEM)


def run_kernel(kernel, shapes, scratch, *operands):
    many = isinstance(shapes, list)
    return pl.pallas_call(
        kernel,
        out_shape=shapes,
        in_specs=[WHOLE] * len(operands),
        out_specs=[WHOLE] * len(shapes) if many else WHOLE,
        scratch_shapes=scratch,
        compiler_params=pltpu.CompilerParams(vmem_limit_bytes=VMEM_LIMIT),
    )(*operands)


def table(rows, dtype=jnp.float32):
    return jax.ShapeDtypeStruct((rows, LANES), dtype)


def buffer(*shape, dtype=jnp.float32):
    return pltpu.VMEM(shape, dtype)


def expand_table():
    x = np.arange(PIX) % 16 - 7.5
    y = np.arange(PIX) // 16 - 7.5
    wide = np.zeros((KROWS, PIX + 3 * LANES), np.float32)
    for number, mono in enumerate((x * x, x * y, y * y, x, y, np.ones(PIX))):
        wide[3 * number : 3 * number + 3, :PIX] = mono
    for k in range(3):
        wide[18 + 3 * k : 21 + 3 * k, PIX + k * LANES : PIX + (k + 1) * LANES] = 1.0
    narrow = np.zeros((16, PIX), np.float32)
    for number, mono in enumerate((np.ones(PIX), x, y, x * x, x * y, y * y)):
        narrow[number] = mono
    return jnp.asarray(wide, jnp.bfloat16), jnp.asarray(narrow, jnp.bfloat16)


def owner_features(params, index):
    return run_kernel(
        project_kernel,
        table(DEVICES * FEATS),
        [buffer(BLOCKS * PROWS, LANES), buffer(VIEWS * FEATS * BLOCKS, LANES)],
        params,
        index,
    )


def ordered(tile_lists):
    return tile_lists.reshape(SLABS, 8, LIST).transpose(0, 2, 1).reshape(LANES, LANES)


def inverse_lists(entries):
    return run_kernel(invert_kernel, [table(LANES, jnp.int32)] * 2, [], entries)


def render(received, entries, lanes, rows, target):
    wide, narrow = expand_table()
    return run_kernel(
        render_kernel,
        [jax.ShapeDtypeStruct((TILE_DEV, 3 * PIX), jnp.float32), table(DEVICES * FEATS)],
        [
            buffer(FEATS * LANES, LANES),
            buffer(LANES * KROWS, LANES),
            buffer(GROUP_ROWS, PIX),
            buffer(GROUP_ROWS, PIX),
            buffer(GROUP_ROWS, 3 * LANES),
            buffer(2, GROUP_ROWS, PIX, dtype=jnp.bfloat16),
            buffer(FEATS * LANES, LANES),
            buffer(LANES * GRADS, LANES),
        ],
        received,
        entries,
        lanes,
        rows,
        target,
        wide,
        narrow,
    )


def owner_update(back, index, params, first, second):
    shape = jax.ShapeDtypeStruct(params.shape, jnp.float32)
    return run_kernel(
        update_kernel,
        [shape] * 3,
        [
            buffer(BLOCKS * PROWS, LANES),
            buffer(VIEWS * FEATS * BLOCKS, LANES),
            buffer(BLOCKS * PROWS, LANES),
            buffer(3 * VIEWS * BLOCKS, LANES),
        ],
        back,
        index,
        params,
        first,
        second,
        jnp.asarray(rate_table()),
    )


def exchange(values):
    chunks = values.reshape(DEVICES, 1, FEATS * LANES)
    arrived = lax.all_to_all(chunks, AXES, split_axis=0, concat_axis=0, tiled=True)
    return arrived.reshape(DEVICES * FEATS, LANES)


def per_device(params, first_moment, second_moment, target_images, tile_lists, send_index):
    index = send_index[0]
    outgoing = owner_features(params, index)
    entries = ordered(tile_lists)
    received = exchange(outgoing)
    lanes, rows = inverse_lists(entries)
    target = target_images.reshape(TILE_DEV, 3 * PIX)
    image, returning = render(received, entries, lanes, rows, target)
    back = exchange(returning)
    new_params, new_first, new_second = owner_update(back, index, params, first_moment, second_moment)
    return (image.reshape(target_images.shape), new_params, new_first, new_second)


def solution(mesh):
    in_specs = (
        P(None, AXES),
        P(None, AXES),
        P(None, AXES),
        P(AXES, None, None),
        P(AXES, None),
        P(AXES, None, None),
    )
    out_specs = (P(AXES, None, None), P(None, AXES), P(None, AXES), P(None, AXES))
    return jax.shard_map(
        per_device, mesh=mesh, in_specs=in_specs, out_specs=out_specs, check_vma=False
    )
```

```python
import functools
import math

import jax
import jax.numpy as jnp
import numpy as np
from jax import lax
from jax.experimental import pallas as pl
from jax.experimental.pallas import tpu as pltpu
from jax.sharding import PartitionSpec as P

PARAMS = 59
PIX = 256
VIEWS = 16
LIST = 512
TILE_DEV = 32
GS_DEV = 2048
DEVICES = 128
CAP = 128
FEATS = 9
BLOCKS = 16
PROWS = 64
LANES = 128
SLABS = 4
LOG2E = 1.4426950408889634
AXES = ("gauss", "render")
VMEM_LIMIT = 56 * 1024 * 1024

sh_first = 0.28209479177387814
sh_second = 0.4886025119029199
sh_third = (
    1.0925484305920792,
    -1.0925484305920792,
    0.31539156525252005,
    -1.0925484305920792,
    0.5462742152960396,
)
sh_fourth = (
    -0.5900435899266435,
    2.890611442640554,
    -0.4570457994644658,
    0.3731763325901154,
    -0.4570457994644658,
    1.445305721320277,
    -0.5900435899266435,
)
tilt_reach = 0.25
beta_one = 0.9
beta_two = 0.999
adam_epsilon = 1e-15
adam_count = 1000.0


def rate_table():
    table = np.full((PARAMS,), 0.000125)
    table[0:3] = 0.0016
    table[3:6] = 0.005
    table[6:10] = 0.001
    table[10] = 0.05
    table[11] = 0.0025
    table[27] = 0.0025
    table[43] = 0.0025
    return np.broadcast_to(table.astype(np.float32)[:, None], (PARAMS, LANES))


def sh_basis(dir_x, dir_y, dir_z):
    sq_x = dir_x * dir_x
    sq_y = dir_y * dir_y
    sq_z = dir_z * dir_z
    return [
        sh_first,
        -sh_second * dir_y,
        sh_second * dir_z,
        -sh_second * dir_x,
        sh_third[0] * dir_x * dir_y,
        sh_third[1] * dir_y * dir_z,
        sh_third[2] * (2.0 * sq_z - sq_x - sq_y),
        sh_third[3] * dir_x * dir_z,
        sh_third[4] * (sq_x - sq_y),
        sh_fourth[0] * dir_y * (3.0 * sq_x - sq_y),
        sh_fourth[1] * dir_x * dir_y * dir_z,
        sh_fourth[2] * dir_y * (4.0 * sq_z - sq_x - sq_y),
        sh_fourth[3] * dir_z * (2.0 * sq_z - 3.0 * sq_x - 3.0 * sq_y),
        sh_fourth[4] * dir_x * (4.0 * sq_z - sq_x - sq_y),
        sh_fourth[5] * dir_z * (sq_x - sq_y),
        sh_fourth[6] * dir_x * (sq_x - 3.0 * sq_y),
    ]


def camera_constants(camera):
    angle = camera * (2.0 * math.pi / VIEWS)
    lean_x = tilt_reach * math.cos(angle)
    lean_y = tilt_reach * math.sin(angle)
    length = math.sqrt(1.0 + lean_x * lean_x + lean_y * lean_y)
    basis = sh_basis(lean_x / length, lean_y / length, -1.0 / length)
    return (lean_x, lean_y, 16.0 * (camera % 4), 16.0 * (camera // 4), basis)


CAMERAS = [camera_constants(camera) for camera in range(VIEWS)]


def spread(log_scales, quat):
    squares = [jnp.exp(2.0 * value) for value in log_scales]
    norm = jnp.sqrt(quat[0] * quat[0] + quat[1] * quat[1] + quat[2] * quat[2] + quat[3] * quat[3])
    q_w, q_x, q_y, q_z = [part / norm for part in quat]
    rotation = [
        [
            1.0 - 2.0 * (q_y * q_y + q_z * q_z),
            2.0 * (q_x * q_y - q_w * q_z),
            2.0 * (q_x * q_z + q_w * q_y),
        ],
        [
            2.0 * (q_x * q_y + q_w * q_z),
            1.0 - 2.0 * (q_x * q_x + q_z * q_z),
            2.0 * (q_y * q_z - q_w * q_x),
        ],
        [
            2.0 * (q_x * q_z - q_w * q_y),
            2.0 * (q_y * q_z + q_w * q_x),
            1.0 - 2.0 * (q_x * q_x + q_y * q_y),
        ],
    ]
    return [
        rotation[row][0] * rotation[col][0] * squares[0]
        + rotation[row][1] * rotation[col][1] * squares[1]
        + rotation[row][2] * rotation[col][2] * squares[2]
        for row, col in ((0, 0), (0, 1), (0, 2), (1, 1), (1, 2), (2, 2))
    ]


def conic_of(sigma, lean_x, lean_y):
    s_xx, s_xy, s_xz, s_yy, s_yz, s_zz = sigma
    cov_xx = s_xx + (2.0 * lean_x) * s_xz + (lean_x * lean_x) * s_zz + 0.3
    cov_xy = s_xy + lean_x * s_yz + lean_y * s_xz + (lean_x * lean_y) * s_zz
    cov_yy = s_yy + (2.0 * lean_y) * s_yz + (lean_y * lean_y) * s_zz + 0.3
    inverse = 1.0 / (cov_xx * cov_yy - cov_xy * cov_xy)
    return cov_yy * inverse, -cov_xy * inverse, cov_xx * inverse


def raw_colour(row, basis, channel):
    total = 0.5 + row(11 + 16 * channel) * basis[0]
    for term in range(1, 16):
        total = total + row(11 + 16 * channel + term) * basis[term]
    return total


def block_rows(source, dest):
    rows = source.shape[0]
    for block in range(BLOCKS):
        dest[pl.ds(block * PROWS, rows), :] = source[:, pl.ds(block * LANES, LANES)]


def strided(ref, row):
    return ref[pl.ds(row, BLOCKS, stride=PROWS), :]


def parts_of(value, count):
    parts = []
    for step in range(count):
        part = value.astype(jnp.bfloat16)
        parts.append(part)
        if step + 1 < count:
            value = value - part.astype(jnp.float32)
    return parts


def project_kernel(params_ref, index_ref, out_ref, rows_ref, table_ref):
    block_rows(params_ref, rows_ref)
    row = functools.partial(strided, rows_ref)
    sigma = spread([row(3 + k) for k in range(3)], [row(6 + k) for k in range(4)])
    logit = row(10)
    log_opacity = -LOG2E * (jnp.maximum(-logit, 0.0) + jnp.log1p(jnp.exp(-jnp.abs(logit))))
    for camera in range(VIEWS):
        lean_x, lean_y, shift_x, shift_y, basis = CAMERAS[camera]
        height = row(2)
        features = [row(0) + lean_x * height - shift_x, row(1) + lean_y * height - shift_y]
        features += list(conic_of(sigma, lean_x, lean_y))
        features.append(log_opacity)
        features += [jnp.maximum(raw_colour(row, basis, k), 0.0) for k in range(3)]
        for f in range(FEATS):
            table_ref[pl.ds((camera * FEATS + f) * BLOCKS, BLOCKS), :] = features[f]

    @pl.loop(0, VIEWS, unroll=2)
    def _(camera):
        chosen = index_ref[pl.ds(pl.multiple_of(camera * 8, 8), 8), :]
        low = jnp.bitwise_and(chosen, LANES - 1)
        high = jnp.right_shift(chosen, 7)
        totals = [jnp.zeros((8, LANES), jnp.float32) for _ in range(FEATS)]
        for block in range(BLOCKS):
            here = high == block
            for f in range(FEATS):
                line = table_ref[pl.ds((camera * FEATS + f) * BLOCKS + block, 1), :]
                line = jnp.broadcast_to(line, (8, LANES))
                picked = jnp.take_along_axis(line, low, axis=1)
                totals[f] = jnp.where(here, picked, totals[f])
        for f in range(FEATS):
            out_ref[pl.ds(camera * 8 * FEATS + f, 8, stride=FEATS), :] = totals[f]


def invert_kernel(list_ref, lane_ref, row_ref):
    sublane = lax.broadcasted_iota(jnp.int32, (LANES, LANES), 0)
    lane = lax.broadcasted_iota(jnp.int32, (LANES, LANES), 1).astype(jnp.float32)

    def step(pair, total):
        owners, slots = [], []
        for member in range(2):
            line = list_ref[pl.ds(pair * 2 + member, 1), :]
            low = jnp.broadcast_to(jnp.bitwise_and(line, CAP - 1), (LANES, LANES))
            high = jnp.broadcast_to(jnp.right_shift(line, 7), (LANES, LANES))
            number = (pair * 2 + member + 1).astype(jnp.float32)
            owners.append(jnp.where(high == sublane, 1.0, 0.0).astype(jnp.bfloat16))
            same = low == sublane
            slots.append(
                jnp.concatenate([jnp.where(same, lane, 0.0), jnp.where(same, number, 0.0)], 0).astype(
                    jnp.bfloat16
                )
            )
        return total + lax.dot_general(
            jnp.concatenate(owners, 1),
            jnp.concatenate(slots, 1),
            (((1,), (1,)), ((), ())),
            preferred_element_type=jnp.float32,
        )

    total = lax.fori_loop(0, LANES // 2, step, jnp.zeros((LANES, 2 * LANES), jnp.float32), unroll=8)
    lane_ref[...] = total[:, :LANES].astype(jnp.int32)
    row_ref[...] = total[:, LANES:].astype(jnp.int32) - 1


def picked_lanes(table, first, low, high, base, count, totals):
    for step in range(count):
        source = base + step
        here = high == source
        for number, place in enumerate(first):
            line = jnp.broadcast_to(table[pl.ds(place(source), 1), :], (8, LANES))
            picked = jnp.take_along_axis(line, low, axis=1)
            totals[number] = jnp.where(here, picked, totals[number])
    return totals


LANE_IN = (0, 1, 5)
DOT_IN = (2, 3, 4, 6, 7, 8)
LANE_OUT = (0, 1, 5)
DOT_OUT = (2, 3, 4, 6, 7, 8)
CONTRACT = (((1,), (1,)), ((), ()))


KROWS = 32
GRADS = 16
GROUP_ROWS = LIST * 8


def render_kernel(
    table_ref,
    list_ref,
    lane_ref,
    row_ref,
    target_ref,
    expand_ref,
    mono_ref,
    image_ref,
    back_ref,
    feat_ref,
    coef_ref,
    alpha_ref,
    weight_ref,
    colour_ref,
    push_ref,
    grad_ref,
    moment_ref,
    halves_ref,
    sums_ref,
):
    render = lax.axis_index(AXES[1])
    device = lax.axis_index(AXES[0]) * lax.axis_size(AXES[1]) + render
    strip = lax.rem(device, DEVICES // VIEWS)
    lane_tile = jnp.bitwise_and(lax.broadcasted_iota(jnp.int32, (8, LANES), 1), 7)
    centre_x = 16.0 * lane_tile.astype(jnp.float32) + 8.0

    owner = lax.broadcasted_iota(jnp.int32, (LANES, 2 * LANES), 0)
    for number, f in enumerate(DOT_IN):
        value = table_ref[pl.ds(f, DEVICES, stride=FEATS), :]
        for which, part in enumerate(parts_of(value, 3)):
            halves_ref[pl.ds(number * LANES, LANES), pl.ds(which * LANES, LANES)] = part

    def collect(count, totals):
        octet = count // 4
        quarter = lax.rem(count, 4)
        span = pl.ds(pl.multiple_of(octet * 8, 8), 8)
        low = jnp.bitwise_and(list_ref[span, :], CAP - 1)
        high = jnp.right_shift(list_ref[span, :], 7)
        totals = [jnp.where(quarter == 0, 0.0, total) for total in totals]
        first = [lambda source, f=f: source * FEATS + f for f in LANE_IN]
        totals = picked_lanes(table_ref, first, low, high, quarter * 32, 32, totals)
        for number, f in enumerate(LANE_IN):
            feat_ref[pl.ds(pl.multiple_of(f * LANES + octet * 8, 8), 8), :] = totals[number]
        lines = [list_ref[pl.ds(count * 2 + member, 1), :] for member in range(2)]
        line = jnp.broadcast_to(jnp.concatenate(lines, 1), (LANES, 2 * LANES))
        slot = jnp.where(jnp.bitwise_and(line, CAP - 1) == owner, 1.0, 0.0).astype(jnp.bfloat16)
        thrice = jnp.concatenate([slot, slot, slot], 0)
        exact = jnp.dot(
            halves_ref[pl.ds(0, 3 * LANES), :], thrice, preferred_element_type=jnp.float32
        )
        other = jnp.dot(
            halves_ref[pl.ds(3 * LANES, 3 * LANES), pl.ds(0, 2 * LANES)],
            thrice[: 2 * LANES],
            preferred_element_type=jnp.float32,
        )
        found = [exact[k * LANES : (k + 1) * LANES] for k in range(3)]
        found += [other[k * LANES : (k + 1) * LANES] for k in range(3)]
        mine = jnp.right_shift(line, 7) == owner
        for number, f in enumerate(DOT_IN):
            value = jnp.where(mine, found[number], 0.0)
            value = jnp.sum(value, 0, keepdims=True)
            for member in range(2):
                feat_ref[pl.ds(f * LANES + count * 2 + member, 1), :] = value[
                    :, member * LANES : (member + 1) * LANES
                ]
        return tuple(totals)

    blank = tuple(jnp.zeros((8, LANES), jnp.float32) for _ in LANE_IN)
    lax.fori_loop(0, LANES // 2, collect, blank, unroll=8)
    zero = jnp.zeros((8, LANES), jnp.float32)

    @pl.loop(0, 16)
    def _(octet):
        base = pl.multiple_of(octet * 8, 8)
        feature = [feat_ref[pl.ds(pl.multiple_of(f * LANES + octet * 8, 8), 8), :] for f in range(FEATS)]
        live = list_ref[pl.ds(base, 8), :] >= 0
        centre_y = (16 * (strip * SLABS + octet // 4) + 8).astype(jnp.float32)
        m_x = feature[0] - centre_x
        m_y = feature[1] - centre_y
        a = (-0.5 * LOG2E) * feature[2]
        b = -LOG2E * feature[3]
        c = (-0.5 * LOG2E) * feature[4]
        to_x = 2.0 * a * m_x + b * m_y
        to_y = b * m_x + 2.0 * c * m_y
        level = a * m_x * m_x + b * m_x * m_y + c * m_y * m_y
        level = jnp.where(live, level + feature[5], -10000.0)
        values = [a, b, c, -to_x, -to_y, level] + feature[6:9]
        place = 0
        for value in values:
            for part in parts_of(value, 3):
                coef_ref[pl.ds(octet * 8 * KROWS + place, 8, stride=KROWS), :] = part.astype(jnp.float32)
                place += 1
        for rest in range(place, KROWS):
            coef_ref[pl.ds(octet * 8 * KROWS + rest, 8, stride=KROWS), :] = zero

    diagonal = lax.broadcasted_iota(jnp.int32, (8, LANES), 0) == lane_tile

    @pl.loop(0, SLABS)
    def _(group):
        @pl.loop(0, 8, unroll=4)
        def _(quad):
            lefts = []
            for sub in range(4):
                start = pl.multiple_of((group * 32 + quad * 4 + sub) * KROWS, KROWS)
                lefts.append(coef_ref[pl.ds(start, KROWS), :].T.astype(jnp.bfloat16))
            wide = jnp.dot(jnp.concatenate(lefts, 0), expand_ref[...], preferred_element_type=jnp.float32)
            out = pl.ds(pl.multiple_of(quad * 512, 512), 512)
            alpha_ref[out, :] = wide[:, :PIX]
            colour_ref[out, :] = wide[:, PIX:]

        def forward(block, carry):
            through = list(carry[:2])
            image = list(carry[2:])
            for lot in range(2):
                alphas, weights, spots = [], [], []
                for u in range(8):
                    here = pl.ds(pl.multiple_of(block * LANES + (lot * 8 + u) * 8, 8), 8)
                    spots.append(here)
                    alphas.append(
                        [
                            jnp.minimum(jnp.exp2(alpha_ref[here, pl.ds(half * LANES, LANES)]), 0.99)
                            for half in range(2)
                        ]
                    )
                for u in range(8):
                    shade = [colour_ref[spots[u], pl.ds(k * LANES, LANES)] for k in range(3)]
                    weights.append([])
                    for half in range(2):
                        weight = alphas[u][half] * through[half]
                        through[half] = through[half] * (1.0 - alphas[u][half])
                        weights[u].append(weight)
                        for k in range(3):
                            image[k * 2 + half] = image[k * 2 + half] + shade[k] * weight
                for u in range(8):
                    for half in range(2):
                        cols = pl.ds(half * LANES, LANES)
                        alpha_ref[spots[u], cols] = alphas[u][half]
                        weight_ref[spots[u], cols] = weights[u][half]
            return tuple(through + image)

        ones = jnp.ones((8, LANES), jnp.float32)
        image = lax.fori_loop(0, 32, forward, (ones, ones) + (zero,) * 6)[2:]
        residual = []
        tiles = pl.ds(pl.multiple_of(group * 8, 8), 8)
        for k in range(3):
            for half in range(2):
                cols = pl.ds(k * PIX + half * LANES, LANES)
                image_ref[tiles, cols] = image[k * 2 + half]
                residual.append(image[k * 2 + half] - target_ref[tiles, cols])

        def backward(count, carry):
            behind = list(carry)
            block = 31 - count
            for pair in range(7, -1, -1):
                pushes = [[None, None], [None, None]]
                loads = [[None, None], [None, None]]
                for member in (1, 0):
                    here = pl.ds(pl.multiple_of(block * LANES + pair * 16 + member * 8, 8), 8)
                    shade = [colour_ref[here, pl.ds(k * LANES, LANES)] for k in range(3)]
                    for half in range(2):
                        cols = pl.ds(half * LANES, LANES)
                        alpha = alpha_ref[here, cols]
                        weight = weight_ref[here, cols]
                        worth = (
                            shade[0] * residual[half]
                            + shade[1] * residual[2 + half]
                            + shade[2] * residual[4 + half]
                        )
                        loads[half][member] = weight
                        gain = worth - behind[half]
                        behind[half] = behind[half] + alpha * gain
                        pushes[half][member] = jnp.where(alpha < 0.99, weight * gain, 0.0)
                rows = pl.ds(pl.multiple_of(block * LANES + pair * 16, 16), 16)
                for half in range(2):
                    parts = parts_of(jnp.concatenate(pushes[half], 0), 2)
                    parts += parts_of(jnp.concatenate(loads[half], 0), 2)
                    for which, part in enumerate(parts):
                        push_ref[rows, pl.ds(which * PIX + half * LANES, LANES)] = part
            return tuple(behind)

        lax.fori_loop(0, 32, backward, (zero, zero))
        stack = jnp.concatenate(
            [jnp.concatenate([residual[k * 2], residual[k * 2 + 1]], 1) for k in range(3)], 0
        )
        stack = jnp.concatenate(parts_of(stack, 2), 0)
        stack = jnp.concatenate([stack, stack], 1)
        powers = jnp.concatenate([mono_ref[...], mono_ref[...]], 1)

        @pl.loop(0, 2)
        def _(chunk):
            rows = pl.ds(pl.multiple_of(chunk * 2048, 2048), 2048)
            moments = lax.dot_general(
                powers, push_ref[rows, pl.ds(0, 2 * PIX)], CONTRACT, preferred_element_type=jnp.float32
            )
            tints = lax.dot_general(
                stack, push_ref[rows, pl.ds(2 * PIX, 2 * PIX)], CONTRACT, preferred_element_type=jnp.float32
            )
            tints = tints[:24] + tints[24:]
            for line in range(16):
                cols = slice(line * LANES, (line + 1) * LANES)
                base = ((group * 32) + chunk * 16 + line) * GRADS
                moment_ref[pl.ds(pl.multiple_of(base, 8), 8), :] = moments[:8, cols]
                for k in range(3):
                    own = jnp.where(diagonal, tints[k * 8 : k * 8 + 8, cols], 0.0)
                    moment_ref[pl.ds(base + 8 + k, 1), :] = jnp.sum(own, 0, keepdims=True)

    @pl.loop(0, 16)
    def _(octet):
        feature = [feat_ref[pl.ds(pl.multiple_of(f * LANES + octet * 8, 8), 8), :] for f in range(5)]
        centre_y = (16 * (strip * SLABS + octet // 4) + 8).astype(jnp.float32)
        m_x = feature[0] - centre_x
        m_y = feature[1] - centre_y

        def moment(k):
            return moment_ref[pl.ds(octet * 8 * GRADS + k, 8, stride=GRADS), :]

        total, s_x, s_y, s_xx, s_xy, s_yy = [moment(k) for k in range(6)]
        along_x = s_x - m_x * total
        along_y = s_y - m_y * total
        results = [
            feature[2] * along_x + feature[3] * along_y,
            feature[3] * along_x + feature[4] * along_y,
            -0.5 * (s_xx - m_x * (s_x + along_x)),
            -(s_xy - m_x * s_y - m_y * along_x),
            -0.5 * (s_yy - m_y * (s_y + along_y)),
            total,
            moment(8),
            moment(9),
            moment(10),
        ]
        for f in range(FEATS):
            grad_ref[pl.ds(pl.multiple_of(f * LANES + octet * 8, 8), 8), :] = results[f]

    sums_ref[...] = jnp.zeros(sums_ref.shape, jnp.float32)
    half_owner = lax.broadcasted_iota(jnp.int32, (LANES // 2, LANES), 0)
    place = lax.broadcasted_iota(jnp.int32, (2 * LANES, LANES), 0)

    def spread_out(count, totals):
        octet = count // 4
        quarter = lax.rem(count, 4)
        span = pl.ds(pl.multiple_of(octet * 8, 8), 8)
        totals = [jnp.where(quarter == 0, 0.0, total) for total in totals]
        first = [lambda source, f=f: f * LANES + source for f in LANE_OUT]
        totals = picked_lanes(
            grad_ref, first, lane_ref[span, :], row_ref[span, :], quarter * 32, 32, totals
        )
        for number, f in enumerate(LANE_OUT):
            back_ref[pl.ds(octet * 8 * FEATS + f, 8, stride=FEATS), :] = totals[number]
        slots = []
        owners = []
        for member in range(2):
            line = list_ref[pl.ds(count * 2 + member, 1), :]
            half = jnp.bitwise_and(jnp.right_shift(line, 7), LANES // 2 - 1)
            half = jnp.where(line < 0, -1, half)
            spot = jnp.right_shift(line, 13) * LANES + jnp.bitwise_and(line, CAP - 1)
            owners.append(jnp.broadcast_to(half, (LANES // 2, LANES)) == half_owner)
            same = jnp.broadcast_to(spot, (2 * LANES, LANES)) == place
            slots.append(jnp.where(same, 1.0, 0.0).astype(jnp.bfloat16))
        rows = []
        for f in DOT_OUT:
            lines = [grad_ref[pl.ds(f * LANES + count * 2 + member, 1), :] for member in range(2)]
            tops = [line.astype(jnp.bfloat16).astype(jnp.float32) for line in lines]
            pieces = tops + [line - top for line, top in zip(lines, tops)]
            rows.append(
                jnp.concatenate(
                    [
                        jnp.where(
                            owners[number % 2], jnp.broadcast_to(piece, (LANES // 2, LANES)), 0.0
                        ).astype(jnp.bfloat16)
                        for number, piece in enumerate(pieces)
                    ],
                    1,
                )
            )
        sums_ref[...] += lax.dot_general(
            jnp.concatenate(rows, 0),
            jnp.concatenate(slots + slots, 1),
            CONTRACT,
            preferred_element_type=jnp.float32,
        )
        return tuple(totals)

    blank = tuple(jnp.zeros((8, LANES), jnp.float32) for _ in LANE_OUT)
    lax.fori_loop(0, LANES // 2, spread_out, blank, unroll=8)
    for number, f in enumerate(DOT_OUT):
        for side in range(2):
            back_ref[pl.ds(side * (LANES // 2) * FEATS + f, LANES // 2, stride=FEATS), :] = sums_ref[
                pl.ds(number * (LANES // 2), LANES // 2), pl.ds(side * LANES, LANES)
            ]


SUM_PARTS = 2


def update_kernel(
    back_ref, index_ref, params_ref, first_ref, second_ref, rate_ref,
    new_params_ref, new_first_ref, new_second_ref,
    rows_ref, sums_ref, slope_ref, tint_ref,
):
    block_rows(params_ref, rows_ref)
    row = functools.partial(strided, rows_ref)
    sublane = lax.broadcasted_iota(jnp.int32, (LANES, LANES), 0)
    short = lax.broadcasted_iota(jnp.int32, (BLOCKS, LANES), 0)

    @pl.loop(0, VIEWS, unroll=2)
    def _(camera):
        total = jnp.zeros((SUM_PARTS * FEATS * BLOCKS, LANES), jnp.float32)
        for pair in range(4):
            places, values = [], []
            for member in range(2):
                renderer = camera * 8 + pair * 2 + member
                line = index_ref[pl.ds(renderer, 1), :]
                low = jnp.broadcast_to(jnp.bitwise_and(line, LANES - 1), (LANES, LANES))
                high = jnp.broadcast_to(jnp.right_shift(line, 7), (BLOCKS, LANES))
                places.append(jnp.where(low == sublane, 1.0, 0.0).astype(jnp.bfloat16))
                here = high == short
                stacks = []
                for f in range(FEATS):
                    value = jnp.broadcast_to(back_ref[pl.ds(renderer * FEATS + f, 1), :], (BLOCKS, LANES))
                    stacks.append(jnp.where(here, value, 0.0))
                stack = jnp.concatenate(stacks, 0)
                values.append(jnp.concatenate(parts_of(stack, SUM_PARTS), 0))
            total = total + lax.dot_general(
                jnp.concatenate(values, 1),
                jnp.concatenate(places, 1),
                (((1,), (1,)), ((), ())),
                preferred_element_type=jnp.float32,
            )
        size = FEATS * BLOCKS
        merged = total[:size]
        for part in range(1, SUM_PARTS):
            merged = merged + total[part * size : (part + 1) * size]
        sums_ref[pl.ds(pl.multiple_of(camera * size, size), size), :] = merged

    logs = [row(3 + k) for k in range(3)]
    quat = [row(6 + k) for k in range(4)]
    sigma, spread_pull = jax.vjp(spread, logs, quat)
    blank = jnp.zeros((BLOCKS, LANES), jnp.float32)
    d_sigma = [blank] * 6
    d_x, d_y, d_z, d_log = blank, blank, blank, blank
    for camera in range(VIEWS):
        lean_x, lean_y, _, _, basis = CAMERAS[camera]

        def pushed(f):
            return sums_ref[pl.ds((camera * FEATS + f) * BLOCKS, BLOCKS), :]

        d_x = d_x + pushed(0)
        d_y = d_y + pushed(1)
        d_z = d_z + lean_x * pushed(0) + lean_y * pushed(1)
        _, pull = jax.vjp(lambda values: conic_of(values, lean_x, lean_y), sigma)
        (more,) = pull((pushed(2), pushed(3), pushed(4)))
        d_sigma = [old + new for old, new in zip(d_sigma, more)]
        d_log = d_log + pushed(5)
        for k in range(3):
            raw = raw_colour(row, basis, k)
            gate = jnp.where(raw > 0.0, 1.0, jnp.where(raw == 0.0, 0.5, 0.0))
            tint_ref[pl.ds((k * VIEWS + camera) * BLOCKS, BLOCKS), :] = gate * pushed(6 + k)
    d_scale, d_quat = spread_pull(d_sigma)
    slopes = [d_x, d_y, d_z] + list(d_scale) + list(d_quat) + [d_log / (1.0 + jnp.exp(row(10)))]
    for number, slope in enumerate(slopes):
        slope_ref[pl.ds(number, BLOCKS, stride=PROWS), :] = slope
    for k in range(3):
        for term in range(16):
            slope = blank
            for camera in range(VIEWS):
                tint = tint_ref[pl.ds((k * VIEWS + camera) * BLOCKS, BLOCKS), :]
                slope = slope + CAMERAS[camera][4][term] * tint
            slope_ref[pl.ds(11 + 16 * k + term, BLOCKS, stride=PROWS), :] = slope
    rates = rate_ref[...]
    for block in range(BLOCKS):
        cols = pl.ds(block * LANES, LANES)
        slope = slope_ref[pl.ds(block * PROWS, PARAMS), :]
        new_first = beta_one * first_ref[:, cols] + (1.0 - beta_one) * slope
        new_second = beta_two * second_ref[:, cols] + (1.0 - beta_two) * slope * slope
        first_hat = new_first / (1.0 - beta_one**adam_count)
        second_hat = new_second / (1.0 - beta_two**adam_count)
        new_first_ref[:, cols] = new_first
        new_second_ref[:, cols] = new_second
        new_params_ref[:, cols] = params_ref[:, cols] - rates * first_hat / (
            jnp.sqrt(second_hat) + adam_epsilon
        )


WHOLE = pl.BlockSpec(memory_space=pltpu.VMEM)


def run_kernel(kernel, shapes, scratch, *operands):
    many = isinstance(shapes, list)
    return pl.pallas_call(
        kernel,
        out_shape=shapes,
        in_specs=[WHOLE] * len(operands),
        out_specs=[WHOLE] * len(shapes) if many else WHOLE,
        scratch_shapes=scratch,
        compiler_params=pltpu.CompilerParams(vmem_limit_bytes=VMEM_LIMIT),
    )(*operands)


def table(rows, dtype=jnp.float32):
    return jax.ShapeDtypeStruct((rows, LANES), dtype)


def buffer(*shape, dtype=jnp.float32):
    return pltpu.VMEM(shape, dtype)


def expand_table():
    x = np.arange(PIX) % 16 - 7.5
    y = np.arange(PIX) // 16 - 7.5
    wide = np.zeros((KROWS, PIX + 3 * LANES), np.float32)
    for number, mono in enumerate((x * x, x * y, y * y, x, y, np.ones(PIX))):
        wide[3 * number : 3 * number + 3, :PIX] = mono
    for k in range(3):
        wide[18 + 3 * k : 21 + 3 * k, PIX + k * LANES : PIX + (k + 1) * LANES] = 1.0
    narrow = np.zeros((16, PIX), np.float32)
    for number, mono in enumerate((np.ones(PIX), x, y, x * x, x * y, y * y)):
        narrow[number] = mono
    return jnp.asarray(wide, jnp.bfloat16), jnp.asarray(narrow, jnp.bfloat16)


def owner_features(params, index):
    return run_kernel(
        project_kernel,
        table(DEVICES * FEATS),
        [buffer(BLOCKS * PROWS, LANES), buffer(VIEWS * FEATS * BLOCKS, LANES)],
        params,
        index,
    )


def ordered(tile_lists):
    return tile_lists.reshape(SLABS, 8, LIST).transpose(0, 2, 1).reshape(LANES, LANES)


def inverse_lists(entries):
    return run_kernel(invert_kernel, [table(LANES, jnp.int32)] * 2, [], entries)


def render(received, entries, lanes, rows, target):
    wide, narrow = expand_table()
    return run_kernel(
        render_kernel,
        [jax.ShapeDtypeStruct((TILE_DEV, 3 * PIX), jnp.float32), table(DEVICES * FEATS)],
        [
            buffer(FEATS * LANES, LANES),
            buffer(LANES * KROWS, LANES),
            buffer(GROUP_ROWS, PIX),
            buffer(GROUP_ROWS, PIX),
            buffer(GROUP_ROWS, 3 * LANES),
            buffer(GROUP_ROWS, 4 * PIX, dtype=jnp.bfloat16),
            buffer(FEATS * LANES, LANES),
            buffer(LANES * GRADS, LANES),
            buffer(len(DOT_IN) * LANES, 3 * LANES, dtype=jnp.bfloat16),
            buffer(len(DOT_OUT) * LANES // 2, 2 * LANES),
        ],
        received,
        entries,
        lanes,
        rows,
        target,
        wide,
        narrow,
    )


def owner_update(back, index, params, first, second):
    shape = jax.ShapeDtypeStruct(params.shape, jnp.float32)
    return run_kernel(
        update_kernel,
        [shape] * 3,
        [
            buffer(BLOCKS * PROWS, LANES),
            buffer(VIEWS * FEATS * BLOCKS, LANES),
            buffer(BLOCKS * PROWS, LANES),
            buffer(3 * VIEWS * BLOCKS, LANES),
        ],
        back,
        index,
        params,
        first,
        second,
        jnp.asarray(rate_table()),
    )


def exchange(values):
    chunks = values.reshape(DEVICES, 1, FEATS * LANES)
    arrived = lax.all_to_all(chunks, AXES, split_axis=0, concat_axis=0, tiled=True)
    return arrived.reshape(DEVICES * FEATS, LANES)


def per_device(params, first_moment, second_moment, target_images, tile_lists, send_index):
    index = send_index[0]
    outgoing = owner_features(params, index)
    entries = ordered(tile_lists)
    received = exchange(outgoing)
    lanes, rows = inverse_lists(entries)
    target = target_images.reshape(TILE_DEV, 3 * PIX)
    image, returning = render(received, entries, lanes, rows, target)
    back = exchange(returning)
    new_params, new_first, new_second = owner_update(back, index, params, first_moment, second_moment)
    return (image.reshape(target_images.shape), new_params, new_first, new_second)


def solution(mesh):
    in_specs = (
        P(None, AXES),
        P(None, AXES),
        P(None, AXES),
        P(AXES, None, None),
        P(AXES, None),
        P(AXES, None, None),
    )
    out_specs = (P(AXES, None, None), P(None, AXES), P(None, AXES), P(None, AXES))
    return jax.shard_map(
        per_device, mesh=mesh, in_specs=in_specs, out_specs=out_specs, check_vma=False
    )
```

```python
import functools
import math

import jax
import jax.numpy as jnp
import numpy as np
from jax import lax
from jax.experimental import pallas as pl
from jax.experimental.pallas import tpu as pltpu
from jax.sharding import PartitionSpec as P

PARAMS = 59
PIX = 256
VIEWS = 16
LIST = 512
TILE_DEV = 32
GS_DEV = 2048
DEVICES = 128
CAP = 128
FEATS = 9
BLOCKS = 16
PROWS = 64
LANES = 128
SLABS = 4
LOG2E = 1.4426950408889634
AXES = ("gauss", "render")
CONTRACT = (((1,), (1,)), ((), ()))
VMEM_LIMIT = 56 * 1024 * 1024

sh_first = 0.28209479177387814
sh_second = 0.4886025119029199
sh_third = (
    1.0925484305920792,
    -1.0925484305920792,
    0.31539156525252005,
    -1.0925484305920792,
    0.5462742152960396,
)
sh_fourth = (
    -0.5900435899266435,
    2.890611442640554,
    -0.4570457994644658,
    0.3731763325901154,
    -0.4570457994644658,
    1.445305721320277,
    -0.5900435899266435,
)
tilt_reach = 0.25
beta_one = 0.9
beta_two = 0.999
adam_epsilon = 1e-15
adam_count = 1000.0


def rate_table():
    table = np.full((PARAMS,), 0.000125)
    table[0:3] = 0.0016
    table[3:6] = 0.005
    table[6:10] = 0.001
    table[10] = 0.05
    table[11] = 0.0025
    table[27] = 0.0025
    table[43] = 0.0025
    return np.broadcast_to(table.astype(np.float32)[:, None], (PARAMS, LANES))


def sh_basis(dir_x, dir_y, dir_z):
    sq_x = dir_x * dir_x
    sq_y = dir_y * dir_y
    sq_z = dir_z * dir_z
    return [
        sh_first,
        -sh_second * dir_y,
        sh_second * dir_z,
        -sh_second * dir_x,
        sh_third[0] * dir_x * dir_y,
        sh_third[1] * dir_y * dir_z,
        sh_third[2] * (2.0 * sq_z - sq_x - sq_y),
        sh_third[3] * dir_x * dir_z,
        sh_third[4] * (sq_x - sq_y),
        sh_fourth[0] * dir_y * (3.0 * sq_x - sq_y),
        sh_fourth[1] * dir_x * dir_y * dir_z,
        sh_fourth[2] * dir_y * (4.0 * sq_z - sq_x - sq_y),
        sh_fourth[3] * dir_z * (2.0 * sq_z - 3.0 * sq_x - 3.0 * sq_y),
        sh_fourth[4] * dir_x * (4.0 * sq_z - sq_x - sq_y),
        sh_fourth[5] * dir_z * (sq_x - sq_y),
        sh_fourth[6] * dir_x * (sq_x - 3.0 * sq_y),
    ]


def camera_constants(camera):
    angle = camera * (2.0 * math.pi / VIEWS)
    lean_x = tilt_reach * math.cos(angle)
    lean_y = tilt_reach * math.sin(angle)
    length = math.sqrt(1.0 + lean_x * lean_x + lean_y * lean_y)
    basis = sh_basis(lean_x / length, lean_y / length, -1.0 / length)
    return (lean_x, lean_y, 16.0 * (camera % 4), 16.0 * (camera // 4), basis)


CAMERAS = [camera_constants(camera) for camera in range(VIEWS)]


def spread(log_scales, quat):
    squares = [jnp.exp(2.0 * value) for value in log_scales]
    norm = jnp.sqrt(quat[0] * quat[0] + quat[1] * quat[1] + quat[2] * quat[2] + quat[3] * quat[3])
    q_w, q_x, q_y, q_z = [part / norm for part in quat]
    rotation = [
        [
            1.0 - 2.0 * (q_y * q_y + q_z * q_z),
            2.0 * (q_x * q_y - q_w * q_z),
            2.0 * (q_x * q_z + q_w * q_y),
        ],
        [
            2.0 * (q_x * q_y + q_w * q_z),
            1.0 - 2.0 * (q_x * q_x + q_z * q_z),
            2.0 * (q_y * q_z - q_w * q_x),
        ],
        [
            2.0 * (q_x * q_z - q_w * q_y),
            2.0 * (q_y * q_z + q_w * q_x),
            1.0 - 2.0 * (q_x * q_x + q_y * q_y),
        ],
    ]
    return [
        rotation[row][0] * rotation[col][0] * squares[0]
        + rotation[row][1] * rotation[col][1] * squares[1]
        + rotation[row][2] * rotation[col][2] * squares[2]
        for row, col in ((0, 0), (0, 1), (0, 2), (1, 1), (1, 2), (2, 2))
    ]


def conic_of(sigma, lean_x, lean_y):
    s_xx, s_xy, s_xz, s_yy, s_yz, s_zz = sigma
    cov_xx = s_xx + (2.0 * lean_x) * s_xz + (lean_x * lean_x) * s_zz + 0.3
    cov_xy = s_xy + lean_x * s_yz + lean_y * s_xz + (lean_x * lean_y) * s_zz
    cov_yy = s_yy + (2.0 * lean_y) * s_yz + (lean_y * lean_y) * s_zz + 0.3
    inverse = 1.0 / (cov_xx * cov_yy - cov_xy * cov_xy)
    return cov_yy * inverse, -cov_xy * inverse, cov_xx * inverse


def raw_colour(row, basis, channel):
    total = 0.5 + row(11 + 16 * channel) * basis[0]
    for term in range(1, 16):
        total = total + row(11 + 16 * channel + term) * basis[term]
    return total


def block_rows(source, dest):
    rows = source.shape[0]
    for block in range(BLOCKS):
        dest[pl.ds(block * PROWS, rows), :] = source[:, pl.ds(block * LANES, LANES)]


def strided(ref, row):
    return ref[pl.ds(row, BLOCKS, stride=PROWS), :]


def parts_of(value, count):
    parts = []
    for step in range(count):
        part = value.astype(jnp.bfloat16)
        parts.append(part)
        if step + 1 < count:
            value = value - part.astype(jnp.float32)
    return parts


MESH = pl.DeviceIdType.MESH


def own_number():
    return lax.axis_index(AXES[0]) * lax.axis_size(AXES[1]) + lax.axis_index(AXES[1])


def coordinates(number):
    across = lax.axis_size(AXES[1])
    return (number // across, lax.rem(number, across))


def announce():
    me = own_number()
    barrier = pltpu.get_barrier_semaphore()

    def tell(step, carry):
        pl.semaphore_signal(
            barrier,
            inc=1,
            device_id=coordinates(lax.rem(me + step, DEVICES)),
            device_id_type=MESH,
        )
        return carry

    lax.fori_loop(1, DEVICES, tell, 0, unroll=True)
    return barrier


def send_chunk(target, me, send_ref, recv_ref, send_sem, recv_sem):
    pltpu.make_async_remote_copy(
        src_ref=send_ref.at[target],
        dst_ref=recv_ref.at[me],
        send_sem=send_sem,
        recv_sem=recv_sem,
        device_id=coordinates(target),
        device_id_type=MESH,
    ).start()


def all_chunks(me, send_ref, recv_ref, send_sem, recv_sem):
    most = pl.ds(0, DEVICES - 1)
    return pltpu.make_async_remote_copy(
        src_ref=send_ref.at[most],
        dst_ref=recv_ref.at[most],
        send_sem=send_sem,
        recv_sem=recv_sem,
        device_id=coordinates(me),
        device_id_type=MESH,
    )


def flatten_chunks(recv_ref, out_ref):
    for source in range(DEVICES):
        out_ref[pl.ds(source * FEATS, FEATS), :] = recv_ref[source]


def invert_lists(list_ref, lane_ref, row_ref):
    sublane = lax.broadcasted_iota(jnp.int32, (LANES, LANES), 0)
    lane = lax.broadcasted_iota(jnp.int32, (LANES, LANES), 1).astype(jnp.float32)

    def step(pair, total):
        owners, slots = [], []
        for member in range(2):
            line = list_ref[pl.ds(pair * 2 + member, 1), :]
            low = jnp.broadcast_to(jnp.bitwise_and(line, CAP - 1), (LANES, LANES))
            high = jnp.broadcast_to(jnp.right_shift(line, 7), (LANES, LANES))
            number = (pair * 2 + member + 1).astype(jnp.float32)
            owners.append(jnp.where(high == sublane, 1.0, 0.0).astype(jnp.bfloat16))
            same = low == sublane
            slots.append(
                jnp.concatenate([jnp.where(same, lane, 0.0), jnp.where(same, number, 0.0)], 0).astype(
                    jnp.bfloat16
                )
            )
        return total + lax.dot_general(
            jnp.concatenate(owners, 1),
            jnp.concatenate(slots, 1),
            CONTRACT,
            preferred_element_type=jnp.float32,
        )

    total = lax.fori_loop(0, LANES // 2, step, jnp.zeros((LANES, 2 * LANES), jnp.float32), unroll=8)
    lane_ref[...] = total[:, :LANES].astype(jnp.int32)
    row_ref[...] = total[:, LANES:].astype(jnp.int32) - 1


def deliver_kernel(
    params_ref, index_ref, list_ref,
    out_ref, lane_ref, row_ref,
    rows_ref, table_ref, flat_ref, send_ref, recv_ref, send_sem, recv_sem,
):
    me = own_number()
    barrier = announce()
    block_rows(params_ref, rows_ref)
    row = functools.partial(strided, rows_ref)
    sigma = spread([row(3 + k) for k in range(3)], [row(6 + k) for k in range(4)])
    logit = row(10)
    log_opacity = -LOG2E * (jnp.maximum(-logit, 0.0) + jnp.log1p(jnp.exp(-jnp.abs(logit))))
    for camera in range(VIEWS):
        lean_x, lean_y, shift_x, shift_y, basis = CAMERAS[camera]
        height = row(2)
        features = [row(0) + lean_x * height - shift_x, row(1) + lean_y * height - shift_y]
        features += list(conic_of(sigma, lean_x, lean_y))
        features.append(log_opacity)
        features += [jnp.maximum(raw_colour(row, basis, k), 0.0) for k in range(3)]
        for f in range(FEATS):
            table_ref[pl.ds((camera * FEATS + f) * BLOCKS, BLOCKS), :] = features[f]
    pl.semaphore_wait(barrier, DEVICES - 1)

    @pl.loop(0, VIEWS)
    def _(turn):
        camera = lax.rem(me // (DEVICES // VIEWS) + turn, VIEWS)
        chosen = index_ref[pl.ds(pl.multiple_of(camera * 8, 8), 8), :]
        low = jnp.bitwise_and(chosen, LANES - 1)
        high = jnp.right_shift(chosen, 7)
        totals = [jnp.zeros((8, LANES), jnp.float32) for _ in range(FEATS)]
        for block in range(BLOCKS):
            here = high == block
            for f in range(FEATS):
                line = table_ref[pl.ds((camera * FEATS + f) * BLOCKS + block, 1), :]
                line = jnp.broadcast_to(line, (8, LANES))
                picked = jnp.take_along_axis(line, low, axis=1)
                totals[f] = jnp.where(here, picked, totals[f])
        for f in range(FEATS):
            flat_ref[pl.ds(f, 8, stride=FEATS), :] = totals[f]
        for member in range(8):
            send_ref[camera * 8 + member] = flat_ref[pl.ds(member * FEATS, FEATS), :]
        for step in range(8):
            target = camera * 8 + lax.rem(me + step, 8)

            @pl.when(target != me)
            def _():
                send_chunk(target, me, send_ref, recv_ref, send_sem, recv_sem)

    invert_lists(list_ref, lane_ref, row_ref)
    whole = all_chunks(me, send_ref, recv_ref, send_sem, recv_sem)
    recv_ref[me] = send_ref[me]
    whole.wait_recv()
    flatten_chunks(recv_ref, out_ref)
    whole.wait_send()


def return_kernel(back_ref, out_ref, send_ref, recv_ref, send_sem, recv_sem):
    me = own_number()
    barrier = announce()
    for target in range(DEVICES):
        send_ref[target] = back_ref[pl.ds(target * FEATS, FEATS), :]
    pl.semaphore_wait(barrier, DEVICES - 1)

    def send(step, carry):
        send_chunk(lax.rem(me + step, DEVICES), me, send_ref, recv_ref, send_sem, recv_sem)
        return carry

    lax.fori_loop(1, DEVICES, send, 0, unroll=8)
    whole = all_chunks(me, send_ref, recv_ref, send_sem, recv_sem)
    recv_ref[me] = send_ref[me]
    whole.wait_recv()
    flatten_chunks(recv_ref, out_ref)
    whole.wait_send()


def picked_lanes(table, first, low, high, base, count, totals):
    for step in range(count):
        source = base + step
        here = high == source
        for number, place in enumerate(first):
            line = jnp.broadcast_to(table[pl.ds(place(source), 1), :], (8, LANES))
            picked = jnp.take_along_axis(line, low, axis=1)
            totals[number] = jnp.where(here, picked, totals[number])
    return totals


LANE_IN = (0, 1, 5)
DOT_IN = (2, 3, 4, 6, 7, 8)
LANE_OUT = (0, 1, 5)
DOT_OUT = (2, 3, 4, 6, 7, 8)
KROWS = 32
GRADS = 16
GROUP_ROWS = LIST * 8


def render_kernel(
    table_ref,
    list_ref,
    lane_ref,
    row_ref,
    target_ref,
    expand_ref,
    mono_ref,
    image_ref,
    back_ref,
    feat_ref,
    coef_ref,
    alpha_ref,
    weight_ref,
    colour_ref,
    push_ref,
    grad_ref,
    moment_ref,
    halves_ref,
    sums_ref,
):
    render = lax.axis_index(AXES[1])
    device = lax.axis_index(AXES[0]) * lax.axis_size(AXES[1]) + render
    strip = lax.rem(device, DEVICES // VIEWS)
    lane_tile = jnp.bitwise_and(lax.broadcasted_iota(jnp.int32, (8, LANES), 1), 7)
    centre_x = 16.0 * lane_tile.astype(jnp.float32) + 8.0

    owner = lax.broadcasted_iota(jnp.int32, (LANES, 2 * LANES), 0)
    for number, f in enumerate(DOT_IN):
        value = table_ref[pl.ds(f, DEVICES, stride=FEATS), :]
        for which, part in enumerate(parts_of(value, 3)):
            halves_ref[pl.ds(number * LANES, LANES), pl.ds(which * LANES, LANES)] = part

    def collect(count, totals):
        octet = count // 4
        quarter = lax.rem(count, 4)
        span = pl.ds(pl.multiple_of(octet * 8, 8), 8)
        low = jnp.bitwise_and(list_ref[span, :], CAP - 1)
        high = jnp.right_shift(list_ref[span, :], 7)
        totals = [jnp.where(quarter == 0, 0.0, total) for total in totals]
        first = [lambda source, f=f: source * FEATS + f for f in LANE_IN]
        totals = picked_lanes(table_ref, first, low, high, quarter * 32, 32, totals)
        for number, f in enumerate(LANE_IN):
            feat_ref[pl.ds(pl.multiple_of(f * LANES + octet * 8, 8), 8), :] = totals[number]
        lines = [list_ref[pl.ds(count * 2 + member, 1), :] for member in range(2)]
        line = jnp.broadcast_to(jnp.concatenate(lines, 1), (LANES, 2 * LANES))
        slot = jnp.where(jnp.bitwise_and(line, CAP - 1) == owner, 1.0, 0.0).astype(jnp.bfloat16)
        thrice = jnp.concatenate([slot, slot, slot], 0)
        exact = jnp.dot(
            halves_ref[pl.ds(0, 3 * LANES), :], thrice, preferred_element_type=jnp.float32
        )
        other = jnp.dot(
            halves_ref[pl.ds(3 * LANES, 3 * LANES), pl.ds(0, 2 * LANES)],
            thrice[: 2 * LANES],
            preferred_element_type=jnp.float32,
        )
        found = [exact[k * LANES : (k + 1) * LANES] for k in range(3)]
        found += [other[k * LANES : (k + 1) * LANES] for k in range(3)]
        mine = jnp.right_shift(line, 7) == owner
        for number, f in enumerate(DOT_IN):
            value = jnp.where(mine, found[number], 0.0)
            value = jnp.sum(value, 0, keepdims=True)
            for member in range(2):
                feat_ref[pl.ds(f * LANES + count * 2 + member, 1), :] = value[
                    :, member * LANES : (member + 1) * LANES
                ]
        return tuple(totals)

    blank = tuple(jnp.zeros((8, LANES), jnp.float32) for _ in LANE_IN)
    lax.fori_loop(0, LANES // 2, collect, blank, unroll=8)
    zero = jnp.zeros((8, LANES), jnp.float32)

    @pl.loop(0, 16)
    def _(octet):
        base = pl.multiple_of(octet * 8, 8)
        feature = [feat_ref[pl.ds(pl.multiple_of(f * LANES + octet * 8, 8), 8), :] for f in range(FEATS)]
        live = list_ref[pl.ds(base, 8), :] >= 0
        centre_y = (16 * (strip * SLABS + octet // 4) + 8).astype(jnp.float32)
        m_x = feature[0] - centre_x
        m_y = feature[1] - centre_y
        a = (-0.5 * LOG2E) * feature[2]
        b = -LOG2E * feature[3]
        c = (-0.5 * LOG2E) * feature[4]
        to_x = 2.0 * a * m_x + b * m_y
        to_y = b * m_x + 2.0 * c * m_y
        level = a * m_x * m_x + b * m_x * m_y + c * m_y * m_y
        level = jnp.where(live, level + feature[5], -10000.0)
        values = [a, b, c, -to_x, -to_y, level] + feature[6:9]
        place = 0
        for value in values:
            for part in parts_of(value, 3):
                coef_ref[pl.ds(octet * 8 * KROWS + place, 8, stride=KROWS), :] = part.astype(jnp.float32)
                place += 1
        for rest in range(place, KROWS):
            coef_ref[pl.ds(octet * 8 * KROWS + rest, 8, stride=KROWS), :] = zero

    diagonal = lax.broadcasted_iota(jnp.int32, (8, LANES), 0) == lane_tile

    @pl.loop(0, SLABS)
    def _(group):
        @pl.loop(0, 8, unroll=4)
        def _(quad):
            lefts = []
            for sub in range(4):
                start = pl.multiple_of((group * 32 + quad * 4 + sub) * KROWS, KROWS)
                lefts.append(coef_ref[pl.ds(start, KROWS), :].T.astype(jnp.bfloat16))
            wide = jnp.dot(jnp.concatenate(lefts, 0), expand_ref[...], preferred_element_type=jnp.float32)
            out = pl.ds(pl.multiple_of(quad * 512, 512), 512)
            alpha_ref[out, :] = wide[:, :PIX]
            colour_ref[out, :] = wide[:, PIX:]

        def forward(block, carry):
            through = list(carry[:2])
            image = list(carry[2:])
            for lot in range(2):
                alphas, weights, spots = [], [], []
                for u in range(8):
                    here = pl.ds(pl.multiple_of(block * LANES + (lot * 8 + u) * 8, 8), 8)
                    spots.append(here)
                    alphas.append(
                        [
                            jnp.minimum(jnp.exp2(alpha_ref[here, pl.ds(half * LANES, LANES)]), 0.99)
                            for half in range(2)
                        ]
                    )
                for u in range(8):
                    shade = [colour_ref[spots[u], pl.ds(k * LANES, LANES)] for k in range(3)]
                    weights.append([])
                    for half in range(2):
                        weight = alphas[u][half] * through[half]
                        through[half] = through[half] * (1.0 - alphas[u][half])
                        weights[u].append(weight)
                        for k in range(3):
                            image[k * 2 + half] = image[k * 2 + half] + shade[k] * weight
                for u in range(8):
                    for half in range(2):
                        cols = pl.ds(half * LANES, LANES)
                        alpha_ref[spots[u], cols] = alphas[u][half]
                        weight_ref[spots[u], cols] = weights[u][half]
            return tuple(through + image)

        ones = jnp.ones((8, LANES), jnp.float32)
        image = lax.fori_loop(0, 32, forward, (ones, ones) + (zero,) * 6)[2:]
        residual = []
        tiles = pl.ds(pl.multiple_of(group * 8, 8), 8)
        for k in range(3):
            for half in range(2):
                cols = pl.ds(k * PIX + half * LANES, LANES)
                image_ref[tiles, cols] = image[k * 2 + half]
                residual.append(image[k * 2 + half] - target_ref[tiles, cols])

        def backward(count, carry):
            behind = list(carry)
            block = 31 - count
            for pair in range(7, -1, -1):
                pushes = [[None, None], [None, None]]
                loads = [[None, None], [None, None]]
                for member in (1, 0):
                    here = pl.ds(pl.multiple_of(block * LANES + pair * 16 + member * 8, 8), 8)
                    shade = [colour_ref[here, pl.ds(k * LANES, LANES)] for k in range(3)]
                    for half in range(2):
                        cols = pl.ds(half * LANES, LANES)
                        alpha = alpha_ref[here, cols]
                        weight = weight_ref[here, cols]
                        worth = (
                            shade[0] * residual[half]
                            + shade[1] * residual[2 + half]
                            + shade[2] * residual[4 + half]
                        )
                        loads[half][member] = weight
                        gain = worth - behind[half]
                        behind[half] = behind[half] + alpha * gain
                        pushes[half][member] = jnp.where(alpha < 0.99, weight * gain, 0.0)
                rows = pl.ds(pl.multiple_of(block * LANES + pair * 16, 16), 16)
                for half in range(2):
                    parts = parts_of(jnp.concatenate(pushes[half], 0), 2)
                    parts += parts_of(jnp.concatenate(loads[half], 0), 2)
                    for which, part in enumerate(parts):
                        push_ref[rows, pl.ds(which * PIX + half * LANES, LANES)] = part
            return tuple(behind)

        lax.fori_loop(0, 32, backward, (zero, zero))
        stack = jnp.concatenate(
            [jnp.concatenate([residual[k * 2], residual[k * 2 + 1]], 1) for k in range(3)], 0
        )
        stack = jnp.concatenate(parts_of(stack, 2), 0)
        stack = jnp.concatenate([stack, stack], 1)
        powers = jnp.concatenate([mono_ref[...], mono_ref[...]], 1)

        @pl.loop(0, 2)
        def _(chunk):
            rows = pl.ds(pl.multiple_of(chunk * 2048, 2048), 2048)
            moments = lax.dot_general(
                powers, push_ref[rows, pl.ds(0, 2 * PIX)], CONTRACT, preferred_element_type=jnp.float32
            )
            tints = lax.dot_general(
                stack, push_ref[rows, pl.ds(2 * PIX, 2 * PIX)], CONTRACT, preferred_element_type=jnp.float32
            )
            tints = tints[:24] + tints[24:]
            for line in range(16):
                cols = slice(line * LANES, (line + 1) * LANES)
                base = ((group * 32) + chunk * 16 + line) * GRADS
                moment_ref[pl.ds(pl.multiple_of(base, 8), 8), :] = moments[:8, cols]
                for k in range(3):
                    own = jnp.where(diagonal, tints[k * 8 : k * 8 + 8, cols], 0.0)
                    moment_ref[pl.ds(base + 8 + k, 1), :] = jnp.sum(own, 0, keepdims=True)

    @pl.loop(0, 16)
    def _(octet):
        feature = [feat_ref[pl.ds(pl.multiple_of(f * LANES + octet * 8, 8), 8), :] for f in range(5)]
        centre_y = (16 * (strip * SLABS + octet // 4) + 8).astype(jnp.float32)
        m_x = feature[0] - centre_x
        m_y = feature[1] - centre_y

        def moment(k):
            return moment_ref[pl.ds(octet * 8 * GRADS + k, 8, stride=GRADS), :]

        total, s_x, s_y, s_xx, s_xy, s_yy = [moment(k) for k in range(6)]
        along_x = s_x - m_x * total
        along_y = s_y - m_y * total
        results = [
            feature[2] * along_x + feature[3] * along_y,
            feature[3] * along_x + feature[4] * along_y,
            -0.5 * (s_xx - m_x * (s_x + along_x)),
            -(s_xy - m_x * s_y - m_y * along_x),
            -0.5 * (s_yy - m_y * (s_y + along_y)),
            total,
            moment(8),
            moment(9),
            moment(10),
        ]
        for f in range(FEATS):
            grad_ref[pl.ds(pl.multiple_of(f * LANES + octet * 8, 8), 8), :] = results[f]

    sums_ref[...] = jnp.zeros(sums_ref.shape, jnp.float32)
    half_owner = lax.broadcasted_iota(jnp.int32, (LANES // 2, LANES), 0)
    place = lax.broadcasted_iota(jnp.int32, (2 * LANES, LANES), 0)

    def spread_out(count, totals):
        octet = count // 4
        quarter = lax.rem(count, 4)
        span = pl.ds(pl.multiple_of(octet * 8, 8), 8)
        totals = [jnp.where(quarter == 0, 0.0, total) for total in totals]
        first = [lambda source, f=f: f * LANES + source for f in LANE_OUT]
        totals = picked_lanes(
            grad_ref, first, lane_ref[span, :], row_ref[span, :], quarter * 32, 32, totals
        )
        for number, f in enumerate(LANE_OUT):
            back_ref[pl.ds(octet * 8 * FEATS + f, 8, stride=FEATS), :] = totals[number]
        slots = []
        owners = []
        for member in range(2):
            line = list_ref[pl.ds(count * 2 + member, 1), :]
            half = jnp.bitwise_and(jnp.right_shift(line, 7), LANES // 2 - 1)
            half = jnp.where(line < 0, -1, half)
            spot = jnp.right_shift(line, 13) * LANES + jnp.bitwise_and(line, CAP - 1)
            owners.append(jnp.broadcast_to(half, (LANES // 2, LANES)) == half_owner)
            same = jnp.broadcast_to(spot, (2 * LANES, LANES)) == place
            slots.append(jnp.where(same, 1.0, 0.0).astype(jnp.bfloat16))
        rows = []
        for f in DOT_OUT:
            lines = [grad_ref[pl.ds(f * LANES + count * 2 + member, 1), :] for member in range(2)]
            tops = [line.astype(jnp.bfloat16).astype(jnp.float32) for line in lines]
            pieces = tops + [line - top for line, top in zip(lines, tops)]
            rows.append(
                jnp.concatenate(
                    [
                        jnp.where(
                            owners[number % 2], jnp.broadcast_to(piece, (LANES // 2, LANES)), 0.0
                        ).astype(jnp.bfloat16)
                        for number, piece in enumerate(pieces)
                    ],
                    1,
                )
            )
        sums_ref[...] += lax.dot_general(
            jnp.concatenate(rows, 0),
            jnp.concatenate(slots + slots, 1),
            CONTRACT,
            preferred_element_type=jnp.float32,
        )
        return tuple(totals)

    blank = tuple(jnp.zeros((8, LANES), jnp.float32) for _ in LANE_OUT)
    lax.fori_loop(0, LANES // 2, spread_out, blank, unroll=8)
    for number, f in enumerate(DOT_OUT):
        for side in range(2):
            back_ref[pl.ds(side * (LANES // 2) * FEATS + f, LANES // 2, stride=FEATS), :] = sums_ref[
                pl.ds(number * (LANES // 2), LANES // 2), pl.ds(side * LANES, LANES)
            ]


SUM_PARTS = 2


def update_kernel(
    back_ref, index_ref, params_ref, first_ref, second_ref, rate_ref,
    new_params_ref, new_first_ref, new_second_ref,
    rows_ref, sums_ref, slope_ref, tint_ref,
):
    block_rows(params_ref, rows_ref)
    row = functools.partial(strided, rows_ref)
    sublane = lax.broadcasted_iota(jnp.int32, (LANES, LANES), 0)
    short = lax.broadcasted_iota(jnp.int32, (BLOCKS, LANES), 0)

    @pl.loop(0, VIEWS, unroll=2)
    def _(camera):
        total = jnp.zeros((SUM_PARTS * FEATS * BLOCKS, LANES), jnp.float32)
        for pair in range(4):
            places, values = [], []
            for member in range(2):
                renderer = camera * 8 + pair * 2 + member
                line = index_ref[pl.ds(renderer, 1), :]
                low = jnp.broadcast_to(jnp.bitwise_and(line, LANES - 1), (LANES, LANES))
                high = jnp.broadcast_to(jnp.right_shift(line, 7), (BLOCKS, LANES))
                places.append(jnp.where(low == sublane, 1.0, 0.0).astype(jnp.bfloat16))
                here = high == short
                stacks = []
                for f in range(FEATS):
                    value = jnp.broadcast_to(back_ref[pl.ds(renderer * FEATS + f, 1), :], (BLOCKS, LANES))
                    stacks.append(jnp.where(here, value, 0.0))
                stack = jnp.concatenate(stacks, 0)
                values.append(jnp.concatenate(parts_of(stack, SUM_PARTS), 0))
            total = total + lax.dot_general(
                jnp.concatenate(values, 1),
                jnp.concatenate(places, 1),
                (((1,), (1,)), ((), ())),
                preferred_element_type=jnp.float32,
            )
        size = FEATS * BLOCKS
        merged = total[:size]
        for part in range(1, SUM_PARTS):
            merged = merged + total[part * size : (part + 1) * size]
        sums_ref[pl.ds(pl.multiple_of(camera * size, size), size), :] = merged

    logs = [row(3 + k) for k in range(3)]
    quat = [row(6 + k) for k in range(4)]
    sigma, spread_pull = jax.vjp(spread, logs, quat)
    blank = jnp.zeros((BLOCKS, LANES), jnp.float32)
    d_sigma = [blank] * 6
    d_x, d_y, d_z, d_log = blank, blank, blank, blank
    for camera in range(VIEWS):
        lean_x, lean_y, _, _, basis = CAMERAS[camera]

        def pushed(f):
            return sums_ref[pl.ds((camera * FEATS + f) * BLOCKS, BLOCKS), :]

        d_x = d_x + pushed(0)
        d_y = d_y + pushed(1)
        d_z = d_z + lean_x * pushed(0) + lean_y * pushed(1)
        _, pull = jax.vjp(lambda values: conic_of(values, lean_x, lean_y), sigma)
        (more,) = pull((pushed(2), pushed(3), pushed(4)))
        d_sigma = [old + new for old, new in zip(d_sigma, more)]
        d_log = d_log + pushed(5)
        for k in range(3):
            raw = raw_colour(row, basis, k)
            gate = jnp.where(raw > 0.0, 1.0, jnp.where(raw == 0.0, 0.5, 0.0))
            tint_ref[pl.ds((k * VIEWS + camera) * BLOCKS, BLOCKS), :] = gate * pushed(6 + k)
    d_scale, d_quat = spread_pull(d_sigma)
    slopes = [d_x, d_y, d_z] + list(d_scale) + list(d_quat) + [d_log / (1.0 + jnp.exp(row(10)))]
    for number, slope in enumerate(slopes):
        slope_ref[pl.ds(number, BLOCKS, stride=PROWS), :] = slope
    for k in range(3):
        for term in range(16):
            slope = blank
            for camera in range(VIEWS):
                tint = tint_ref[pl.ds((k * VIEWS + camera) * BLOCKS, BLOCKS), :]
                slope = slope + CAMERAS[camera][4][term] * tint
            slope_ref[pl.ds(11 + 16 * k + term, BLOCKS, stride=PROWS), :] = slope
    rates = rate_ref[...]
    for block in range(BLOCKS):
        cols = pl.ds(block * LANES, LANES)
        slope = slope_ref[pl.ds(block * PROWS, PARAMS), :]
        new_first = beta_one * first_ref[:, cols] + (1.0 - beta_one) * slope
        new_second = beta_two * second_ref[:, cols] + (1.0 - beta_two) * slope * slope
        first_hat = new_first / (1.0 - beta_one**adam_count)
        second_hat = new_second / (1.0 - beta_two**adam_count)
        new_first_ref[:, cols] = new_first
        new_second_ref[:, cols] = new_second
        new_params_ref[:, cols] = params_ref[:, cols] - rates * first_hat / (
            jnp.sqrt(second_hat) + adam_epsilon
        )


WHOLE = pl.BlockSpec(memory_space=pltpu.VMEM)


def run_kernel(kernel, shapes, scratch, *operands, collective_id=None):
    many = isinstance(shapes, list)
    extra = {}
    if collective_id is not None:
        extra = dict(collective_id=collective_id, has_side_effects=True)
    return pl.pallas_call(
        kernel,
        out_shape=shapes,
        in_specs=[WHOLE] * len(operands),
        out_specs=[WHOLE] * len(shapes) if many else WHOLE,
        scratch_shapes=scratch,
        compiler_params=pltpu.CompilerParams(vmem_limit_bytes=VMEM_LIMIT, **extra),
    )(*operands)


def table(rows, dtype=jnp.float32):
    return jax.ShapeDtypeStruct((rows, LANES), dtype)


def buffer(*shape, dtype=jnp.float32):
    return pltpu.VMEM(shape, dtype)


def expand_table():
    x = np.arange(PIX) % 16 - 7.5
    y = np.arange(PIX) // 16 - 7.5
    wide = np.zeros((KROWS, PIX + 3 * LANES), np.float32)
    for number, mono in enumerate((x * x, x * y, y * y, x, y, np.ones(PIX))):
        wide[3 * number : 3 * number + 3, :PIX] = mono
    for k in range(3):
        wide[18 + 3 * k : 21 + 3 * k, PIX + k * LANES : PIX + (k + 1) * LANES] = 1.0
    narrow = np.zeros((16, PIX), np.float32)
    for number, mono in enumerate((np.ones(PIX), x, y, x * x, x * y, y * y)):
        narrow[number] = mono
    return jnp.asarray(wide, jnp.bfloat16), jnp.asarray(narrow, jnp.bfloat16)


def chunk_buffers():
    chunks = buffer(DEVICES, FEATS, LANES)
    return [chunks, chunks, pltpu.SemaphoreType.DMA, pltpu.SemaphoreType.DMA]


def deliver(params, index, entries):
    return run_kernel(
        deliver_kernel,
        [table(DEVICES * FEATS)] + [table(LANES, jnp.int32)] * 2,
        [
            buffer(BLOCKS * PROWS, LANES),
            buffer(VIEWS * FEATS * BLOCKS, LANES),
            buffer(8 * FEATS, LANES),
        ]
        + chunk_buffers(),
        params,
        index,
        entries,
        collective_id=0,
    )


def give_back(returning):
    return run_kernel(
        return_kernel, table(DEVICES * FEATS), chunk_buffers(), returning, collective_id=1
    )


def ordered(tile_lists):
    return tile_lists.reshape(SLABS, 8, LIST).transpose(0, 2, 1).reshape(LANES, LANES)


def render(received, entries, lanes, rows, target):
    wide, narrow = expand_table()
    return run_kernel(
        render_kernel,
        [jax.ShapeDtypeStruct((TILE_DEV, 3 * PIX), jnp.float32), table(DEVICES * FEATS)],
        [
            buffer(FEATS * LANES, LANES),
            buffer(LANES * KROWS, LANES),
            buffer(GROUP_ROWS, PIX),
            buffer(GROUP_ROWS, PIX),
            buffer(GROUP_ROWS, 3 * LANES),
            buffer(GROUP_ROWS, 4 * PIX, dtype=jnp.bfloat16),
            buffer(FEATS * LANES, LANES),
            buffer(LANES * GRADS, LANES),
            buffer(len(DOT_IN) * LANES, 3 * LANES, dtype=jnp.bfloat16),
            buffer(len(DOT_OUT) * LANES // 2, 2 * LANES),
        ],
        received,
        entries,
        lanes,
        rows,
        target,
        wide,
        narrow,
    )


def owner_update(back, index, params, first, second):
    shape = jax.ShapeDtypeStruct(params.shape, jnp.float32)
    return run_kernel(
        update_kernel,
        [shape] * 3,
        [
            buffer(BLOCKS * PROWS, LANES),
            buffer(VIEWS * FEATS * BLOCKS, LANES),
            buffer(BLOCKS * PROWS, LANES),
            buffer(3 * VIEWS * BLOCKS, LANES),
        ],
        back,
        index,
        params,
        first,
        second,
        jnp.asarray(rate_table()),
    )


def per_device(params, first_moment, second_moment, target_images, tile_lists, send_index):
    index = send_index[0]
    entries = ordered(tile_lists)
    received, lanes, rows = deliver(params, index, entries)
    target = target_images.reshape(TILE_DEV, 3 * PIX)
    image, returning = render(received, entries, lanes, rows, target)
    back = give_back(returning)
    new_params, new_first, new_second = owner_update(back, index, params, first_moment, second_moment)
    return (image.reshape(target_images.shape), new_params, new_first, new_second)


def solution(mesh):
    in_specs = (
        P(None, AXES),
        P(None, AXES),
        P(None, AXES),
        P(AXES, None, None),
        P(AXES, None),
        P(AXES, None, None),
    )
    out_specs = (P(AXES, None, None), P(None, AXES), P(None, AXES), P(None, AXES))
    return jax.shard_map(
        per_device, mesh=mesh, in_specs=in_specs, out_specs=out_specs, check_vma=False
    )
```

```python
import functools
import math

import jax
import jax.numpy as jnp
import numpy as np
from jax import lax
from jax.experimental import pallas as pl
from jax.experimental.pallas import tpu as pltpu
from jax.sharding import PartitionSpec as P

PARAMS = 59
PIX = 256
VIEWS = 16
LIST = 512
TILE_DEV = 32
GS_DEV = 2048
DEVICES = 128
CAP = 128
FEATS = 9
BLOCKS = 16
PROWS = 64
LANES = 128
SLABS = 4
LOG2E = 1.4426950408889634
AXES = ("gauss", "render")
CONTRACT = (((1,), (1,)), ((), ()))
VMEM_LIMIT = 56 * 1024 * 1024

sh_first = 0.28209479177387814
sh_second = 0.4886025119029199
sh_third = (
    1.0925484305920792,
    -1.0925484305920792,
    0.31539156525252005,
    -1.0925484305920792,
    0.5462742152960396,
)
sh_fourth = (
    -0.5900435899266435,
    2.890611442640554,
    -0.4570457994644658,
    0.3731763325901154,
    -0.4570457994644658,
    1.445305721320277,
    -0.5900435899266435,
)
tilt_reach = 0.25
beta_one = 0.9
beta_two = 0.999
adam_epsilon = 1e-15
adam_count = 1000.0


def rate_table():
    row = lax.broadcasted_iota(jnp.int32, (PARAMS, LANES), 0)
    rates = jnp.where((row == 11) | (row == 27) | (row == 43), 0.0025, 0.000125)
    rates = jnp.where(row == 10, 0.05, rates)
    for last, rate in ((10, 0.001), (6, 0.005), (3, 0.0016)):
        rates = jnp.where(row < last, rate, rates)
    return rates.astype(jnp.float32)


def sh_basis(dir_x, dir_y, dir_z):
    sq_x = dir_x * dir_x
    sq_y = dir_y * dir_y
    sq_z = dir_z * dir_z
    return [
        sh_first,
        -sh_second * dir_y,
        sh_second * dir_z,
        -sh_second * dir_x,
        sh_third[0] * dir_x * dir_y,
        sh_third[1] * dir_y * dir_z,
        sh_third[2] * (2.0 * sq_z - sq_x - sq_y),
        sh_third[3] * dir_x * dir_z,
        sh_third[4] * (sq_x - sq_y),
        sh_fourth[0] * dir_y * (3.0 * sq_x - sq_y),
        sh_fourth[1] * dir_x * dir_y * dir_z,
        sh_fourth[2] * dir_y * (4.0 * sq_z - sq_x - sq_y),
        sh_fourth[3] * dir_z * (2.0 * sq_z - 3.0 * sq_x - 3.0 * sq_y),
        sh_fourth[4] * dir_x * (4.0 * sq_z - sq_x - sq_y),
        sh_fourth[5] * dir_z * (sq_x - sq_y),
        sh_fourth[6] * dir_x * (sq_x - 3.0 * sq_y),
    ]


def camera_constants(camera):
    angle = camera * (2.0 * math.pi / VIEWS)
    lean_x = tilt_reach * math.cos(angle)
    lean_y = tilt_reach * math.sin(angle)
    length = math.sqrt(1.0 + lean_x * lean_x + lean_y * lean_y)
    basis = sh_basis(lean_x / length, lean_y / length, -1.0 / length)
    return (lean_x, lean_y, 16.0 * (camera % 4), 16.0 * (camera // 4), basis)


CAMERAS = [camera_constants(camera) for camera in range(VIEWS)]


def spread(log_scales, quat):
    squares = [jnp.exp(2.0 * value) for value in log_scales]
    norm = jnp.sqrt(quat[0] * quat[0] + quat[1] * quat[1] + quat[2] * quat[2] + quat[3] * quat[3])
    q_w, q_x, q_y, q_z = [part / norm for part in quat]
    rotation = [
        [
            1.0 - 2.0 * (q_y * q_y + q_z * q_z),
            2.0 * (q_x * q_y - q_w * q_z),
            2.0 * (q_x * q_z + q_w * q_y),
        ],
        [
            2.0 * (q_x * q_y + q_w * q_z),
            1.0 - 2.0 * (q_x * q_x + q_z * q_z),
            2.0 * (q_y * q_z - q_w * q_x),
        ],
        [
            2.0 * (q_x * q_z - q_w * q_y),
            2.0 * (q_y * q_z + q_w * q_x),
            1.0 - 2.0 * (q_x * q_x + q_y * q_y),
        ],
    ]
    return [
        rotation[row][0] * rotation[col][0] * squares[0]
        + rotation[row][1] * rotation[col][1] * squares[1]
        + rotation[row][2] * rotation[col][2] * squares[2]
        for row, col in ((0, 0), (0, 1), (0, 2), (1, 1), (1, 2), (2, 2))
    ]


def conic_of(sigma, lean_x, lean_y):
    s_xx, s_xy, s_xz, s_yy, s_yz, s_zz = sigma
    cov_xx = s_xx + (2.0 * lean_x) * s_xz + (lean_x * lean_x) * s_zz + 0.3
    cov_xy = s_xy + lean_x * s_yz + lean_y * s_xz + (lean_x * lean_y) * s_zz
    cov_yy = s_yy + (2.0 * lean_y) * s_yz + (lean_y * lean_y) * s_zz + 0.3
    inverse = 1.0 / (cov_xx * cov_yy - cov_xy * cov_xy)
    return cov_yy * inverse, -cov_xy * inverse, cov_xx * inverse


def raw_colour(row, basis, channel):
    total = 0.5 + row(11 + 16 * channel) * basis[0]
    for term in range(1, 16):
        total = total + row(11 + 16 * channel + term) * basis[term]
    return total


def block_rows(source, dest):
    rows = source.shape[0]
    for block in range(BLOCKS):
        dest[pl.ds(block * PROWS, rows), :] = source[:, pl.ds(block * LANES, LANES)]


def strided(ref, row):
    return ref[pl.ds(row, BLOCKS, stride=PROWS), :]


def parts_of(value, count):
    parts = []
    for step in range(count):
        part = value.astype(jnp.bfloat16)
        parts.append(part)
        if step + 1 < count:
            value = value - part.astype(jnp.float32)
    return parts


MESH = pl.DeviceIdType.MESH


def own_number():
    return lax.axis_index(AXES[0]) * lax.axis_size(AXES[1]) + lax.axis_index(AXES[1])


def coordinates(number):
    across = lax.axis_size(AXES[1])
    return (number // across, lax.rem(number, across))


def announce():
    me = own_number()
    barrier = pltpu.get_barrier_semaphore()

    def tell(step, carry):
        pl.semaphore_signal(
            barrier,
            inc=1,
            device_id=coordinates(lax.rem(me + step, DEVICES)),
            device_id_type=MESH,
        )
        return carry

    lax.fori_loop(1, DEVICES, tell, 0, unroll=True)
    return barrier


def send_chunk(target, me, send_ref, recv_ref, send_sem, recv_sem):
    pltpu.make_async_remote_copy(
        src_ref=send_ref.at[target],
        dst_ref=recv_ref.at[me],
        send_sem=send_sem,
        recv_sem=recv_sem,
        device_id=coordinates(target),
        device_id_type=MESH,
    ).start()


def all_chunks(me, send_ref, recv_ref, send_sem, recv_sem):
    most = pl.ds(0, DEVICES - 1)
    return pltpu.make_async_remote_copy(
        src_ref=send_ref.at[most],
        dst_ref=recv_ref.at[most],
        send_sem=send_sem,
        recv_sem=recv_sem,
        device_id=coordinates(me),
        device_id_type=MESH,
    )


def flatten_chunks(recv_ref, out_ref):
    for source in range(DEVICES):
        out_ref[pl.ds(source * FEATS, FEATS), :] = recv_ref[source]


def invert_lists(list_ref, lane_ref, row_ref):
    sublane = lax.broadcasted_iota(jnp.int32, (LANES, LANES), 0)
    lane = lax.broadcasted_iota(jnp.int32, (LANES, LANES), 1).astype(jnp.float32)

    def step(pair, total):
        owners, slots = [], []
        for member in range(2):
            line = list_ref[pl.ds(pair * 2 + member, 1), :]
            low = jnp.broadcast_to(jnp.bitwise_and(line, CAP - 1), (LANES, LANES))
            high = jnp.broadcast_to(jnp.right_shift(line, 7), (LANES, LANES))
            number = (pair * 2 + member + 1).astype(jnp.float32)
            owners.append(jnp.where(high == sublane, 1.0, 0.0).astype(jnp.bfloat16))
            same = low == sublane
            slots.append(
                jnp.concatenate([jnp.where(same, lane, 0.0), jnp.where(same, number, 0.0)], 0).astype(
                    jnp.bfloat16
                )
            )
        return total + lax.dot_general(
            jnp.concatenate(owners, 1),
            jnp.concatenate(slots, 1),
            CONTRACT,
            preferred_element_type=jnp.float32,
        )

    total = lax.fori_loop(0, LANES // 2, step, jnp.zeros((LANES, 2 * LANES), jnp.float32), unroll=8)
    lane_ref[...] = total[:, :LANES].astype(jnp.int32)
    row_ref[...] = total[:, LANES:].astype(jnp.int32) - 1


def deliver(
    params_ref, index_ref, list_ref,
    out_ref, lane_ref, row_ref,
    rows_ref, table_ref, flat_ref, send_ref, recv_ref, send_sem, recv_sem,
):
    me = own_number()
    barrier = announce()
    block_rows(params_ref, rows_ref)
    row = functools.partial(strided, rows_ref)
    sigma = spread([row(3 + k) for k in range(3)], [row(6 + k) for k in range(4)])
    logit = row(10)
    log_opacity = -LOG2E * (jnp.maximum(-logit, 0.0) + jnp.log1p(jnp.exp(-jnp.abs(logit))))
    for camera in range(VIEWS):
        lean_x, lean_y, shift_x, shift_y, basis = CAMERAS[camera]
        height = row(2)
        features = [row(0) + lean_x * height - shift_x, row(1) + lean_y * height - shift_y]
        features += list(conic_of(sigma, lean_x, lean_y))
        features.append(log_opacity)
        features += [jnp.maximum(raw_colour(row, basis, k), 0.0) for k in range(3)]
        for f in range(FEATS):
            table_ref[pl.ds((camera * FEATS + f) * BLOCKS, BLOCKS), :] = features[f]
    pl.semaphore_wait(barrier, DEVICES - 1)

    @pl.loop(0, VIEWS)
    def _(turn):
        camera = lax.rem(me // (DEVICES // VIEWS) + turn, VIEWS)
        chosen = index_ref[pl.ds(pl.multiple_of(camera * 8, 8), 8), :]
        low = jnp.bitwise_and(chosen, LANES - 1)
        high = jnp.right_shift(chosen, 7)
        totals = [jnp.zeros((8, LANES), jnp.float32) for _ in range(FEATS)]
        for block in range(BLOCKS):
            here = high == block
            for f in range(FEATS):
                line = table_ref[pl.ds((camera * FEATS + f) * BLOCKS + block, 1), :]
                line = jnp.broadcast_to(line, (8, LANES))
                picked = jnp.take_along_axis(line, low, axis=1)
                totals[f] = jnp.where(here, picked, totals[f])
        for f in range(FEATS):
            flat_ref[pl.ds(f, 8, stride=FEATS), :] = totals[f]
        for member in range(8):
            send_ref[camera * 8 + member] = flat_ref[pl.ds(member * FEATS, FEATS), :]
        for step in range(8):
            target = camera * 8 + lax.rem(me + step, 8)

            @pl.when(target != me)
            def _():
                send_chunk(target, me, send_ref, recv_ref, send_sem, recv_sem)

    invert_lists(list_ref, lane_ref, row_ref)
    whole = all_chunks(me, send_ref, recv_ref, send_sem, recv_sem)
    recv_ref[me] = send_ref[me]
    whole.wait_recv()
    flatten_chunks(recv_ref, out_ref)
    whole.wait_send()


def give_back(back_ref, out_ref, send_ref, recv_ref, send_sem, recv_sem):
    me = own_number()
    for target in range(DEVICES):
        send_ref[target] = back_ref[pl.ds(target * FEATS, FEATS), :]

    def send(step, carry):
        send_chunk(lax.rem(me + step, DEVICES), me, send_ref, recv_ref, send_sem, recv_sem)
        return carry

    lax.fori_loop(1, DEVICES, send, 0, unroll=8)
    whole = all_chunks(me, send_ref, recv_ref, send_sem, recv_sem)
    recv_ref[me] = send_ref[me]
    whole.wait_recv()
    flatten_chunks(recv_ref, out_ref)
    whole.wait_send()


def picked_lanes(table, first, low, high, base, count, totals):
    for step in range(count):
        source = base + step
        here = high == source
        for number, place in enumerate(first):
            line = jnp.broadcast_to(table[pl.ds(place(source), 1), :], (8, LANES))
            picked = jnp.take_along_axis(line, low, axis=1)
            totals[number] = jnp.where(here, picked, totals[number])
    return totals


LANE_IN = (0, 1, 5)
DOT_IN = (2, 3, 4, 6, 7, 8)
LANE_OUT = (0, 1, 5)
DOT_OUT = (2, 3, 4, 6, 7, 8)
KROWS = 32
GRADS = 16
GROUP_ROWS = LIST * 8


def composite(
    table_ref,
    list_ref,
    lane_ref,
    row_ref,
    target_ref,
    expand_ref,
    mono_ref,
    image_ref,
    back_ref,
    feat_ref,
    coef_ref,
    alpha_ref,
    weight_ref,
    colour_ref,
    push_ref,
    grad_ref,
    moment_ref,
    halves_ref,
    sums_ref,
):
    render = lax.axis_index(AXES[1])
    device = lax.axis_index(AXES[0]) * lax.axis_size(AXES[1]) + render
    strip = lax.rem(device, DEVICES // VIEWS)
    lane_tile = jnp.bitwise_and(lax.broadcasted_iota(jnp.int32, (8, LANES), 1), 7)
    centre_x = 16.0 * lane_tile.astype(jnp.float32) + 8.0

    owner = lax.broadcasted_iota(jnp.int32, (LANES, 2 * LANES), 0)
    for number, f in enumerate(DOT_IN):
        value = table_ref[pl.ds(f, DEVICES, stride=FEATS), :]
        for which, part in enumerate(parts_of(value, 3)):
            halves_ref[pl.ds(number * LANES, LANES), pl.ds(which * LANES, LANES)] = part

    def collect(count, totals):
        octet = count // 4
        quarter = lax.rem(count, 4)
        span = pl.ds(pl.multiple_of(octet * 8, 8), 8)
        low = jnp.bitwise_and(list_ref[span, :], CAP - 1)
        high = jnp.right_shift(list_ref[span, :], 7)
        totals = [jnp.where(quarter == 0, 0.0, total) for total in totals]
        first = [lambda source, f=f: source * FEATS + f for f in LANE_IN]
        totals = picked_lanes(table_ref, first, low, high, quarter * 32, 32, totals)
        for number, f in enumerate(LANE_IN):
            feat_ref[pl.ds(pl.multiple_of(f * LANES + octet * 8, 8), 8), :] = totals[number]
        lines = [list_ref[pl.ds(count * 2 + member, 1), :] for member in range(2)]
        line = jnp.broadcast_to(jnp.concatenate(lines, 1), (LANES, 2 * LANES))
        slot = jnp.where(jnp.bitwise_and(line, CAP - 1) == owner, 1.0, 0.0).astype(jnp.bfloat16)
        thrice = jnp.concatenate([slot, slot, slot], 0)
        exact = jnp.dot(
            halves_ref[pl.ds(0, 3 * LANES), :], thrice, preferred_element_type=jnp.float32
        )
        other = jnp.dot(
            halves_ref[pl.ds(3 * LANES, 3 * LANES), pl.ds(0, 2 * LANES)],
            thrice[: 2 * LANES],
            preferred_element_type=jnp.float32,
        )
        found = [exact[k * LANES : (k + 1) * LANES] for k in range(3)]
        found += [other[k * LANES : (k + 1) * LANES] for k in range(3)]
        mine = jnp.right_shift(line, 7) == owner
        for number, f in enumerate(DOT_IN):
            value = jnp.where(mine, found[number], 0.0)
            value = jnp.sum(value, 0, keepdims=True)
            for member in range(2):
                feat_ref[pl.ds(f * LANES + count * 2 + member, 1), :] = value[
                    :, member * LANES : (member + 1) * LANES
                ]
        return tuple(totals)

    blank = tuple(jnp.zeros((8, LANES), jnp.float32) for _ in LANE_IN)
    lax.fori_loop(0, LANES // 2, collect, blank, unroll=8)
    zero = jnp.zeros((8, LANES), jnp.float32)

    @pl.loop(0, 16)
    def _(octet):
        base = pl.multiple_of(octet * 8, 8)
        feature = [feat_ref[pl.ds(pl.multiple_of(f * LANES + octet * 8, 8), 8), :] for f in range(FEATS)]
        live = list_ref[pl.ds(base, 8), :] >= 0
        centre_y = (16 * (strip * SLABS + octet // 4) + 8).astype(jnp.float32)
        m_x = feature[0] - centre_x
        m_y = feature[1] - centre_y
        a = (-0.5 * LOG2E) * feature[2]
        b = -LOG2E * feature[3]
        c = (-0.5 * LOG2E) * feature[4]
        to_x = 2.0 * a * m_x + b * m_y
        to_y = b * m_x + 2.0 * c * m_y
        level = a * m_x * m_x + b * m_x * m_y + c * m_y * m_y
        level = jnp.where(live, level + feature[5], -10000.0)
        values = [a, b, c, -to_x, -to_y, level] + feature[6:9]
        place = 0
        for value in values:
            for part in parts_of(value, 3):
                coef_ref[pl.ds(octet * 8 * KROWS + place, 8, stride=KROWS), :] = part.astype(jnp.float32)
                place += 1
        for rest in range(place, KROWS):
            coef_ref[pl.ds(octet * 8 * KROWS + rest, 8, stride=KROWS), :] = zero

    diagonal = lax.broadcasted_iota(jnp.int32, (8, LANES), 0) == lane_tile

    @pl.loop(0, SLABS)
    def _(group):
        @pl.loop(0, 8, unroll=4)
        def _(quad):
            lefts = []
            for sub in range(4):
                start = pl.multiple_of((group * 32 + quad * 4 + sub) * KROWS, KROWS)
                lefts.append(coef_ref[pl.ds(start, KROWS), :].T.astype(jnp.bfloat16))
            wide = jnp.dot(jnp.concatenate(lefts, 0), expand_ref[...], preferred_element_type=jnp.float32)
            out = pl.ds(pl.multiple_of(quad * 512, 512), 512)
            alpha_ref[out, :] = wide[:, :PIX]
            colour_ref[out, :] = wide[:, PIX:]

        def forward(block, carry):
            through = list(carry[:2])
            image = list(carry[2:])
            for lot in range(2):
                alphas, weights, spots = [], [], []
                for u in range(8):
                    here = pl.ds(pl.multiple_of(block * LANES + (lot * 8 + u) * 8, 8), 8)
                    spots.append(here)
                    alphas.append(
                        [
                            jnp.minimum(jnp.exp2(alpha_ref[here, pl.ds(half * LANES, LANES)]), 0.99)
                            for half in range(2)
                        ]
                    )
                for u in range(8):
                    shade = [colour_ref[spots[u], pl.ds(k * LANES, LANES)] for k in range(3)]
                    weights.append([])
                    for half in range(2):
                        weight = alphas[u][half] * through[half]
                        through[half] = through[half] * (1.0 - alphas[u][half])
                        weights[u].append(weight)
                        for k in range(3):
                            image[k * 2 + half] = image[k * 2 + half] + shade[k] * weight
                for u in range(8):
                    for half in range(2):
                        cols = pl.ds(half * LANES, LANES)
                        alpha_ref[spots[u], cols] = alphas[u][half]
                        weight_ref[spots[u], cols] = weights[u][half]
            return tuple(through + image)

        ones = jnp.ones((8, LANES), jnp.float32)
        image = lax.fori_loop(0, 32, forward, (ones, ones) + (zero,) * 6)[2:]
        residual = []
        for k in range(3):
            tiles = pl.ds(pl.multiple_of(k * TILE_DEV + group * 8, 8), 8)
            for half in range(2):
                cols = pl.ds(half * LANES, LANES)
                image_ref[tiles, cols] = image[k * 2 + half]
                residual.append(image[k * 2 + half] - target_ref[tiles, cols])

        def backward(count, carry):
            behind = list(carry)
            block = 31 - count
            for pair in range(7, -1, -1):
                pushes = [[None, None], [None, None]]
                loads = [[None, None], [None, None]]
                for member in (1, 0):
                    here = pl.ds(pl.multiple_of(block * LANES + pair * 16 + member * 8, 8), 8)
                    shade = [colour_ref[here, pl.ds(k * LANES, LANES)] for k in range(3)]
                    for half in range(2):
                        cols = pl.ds(half * LANES, LANES)
                        alpha = alpha_ref[here, cols]
                        weight = weight_ref[here, cols]
                        worth = (
                            shade[0] * residual[half]
                            + shade[1] * residual[2 + half]
                            + shade[2] * residual[4 + half]
                        )
                        loads[half][member] = weight
                        gain = worth - behind[half]
                        behind[half] = behind[half] + alpha * gain
                        pushes[half][member] = jnp.where(alpha < 0.99, weight * gain, 0.0)
                rows = pl.ds(pl.multiple_of(block * LANES + pair * 16, 16), 16)
                for half in range(2):
                    parts = parts_of(jnp.concatenate(pushes[half], 0), 2)
                    parts += parts_of(jnp.concatenate(loads[half], 0), 2)
                    for which, part in enumerate(parts):
                        push_ref[rows, pl.ds(which * PIX + half * LANES, LANES)] = part
            return tuple(behind)

        lax.fori_loop(0, 32, backward, (zero, zero))
        stack = jnp.concatenate(
            [jnp.concatenate([residual[k * 2], residual[k * 2 + 1]], 1) for k in range(3)], 0
        )
        stack = jnp.concatenate(parts_of(stack, 2), 0)
        stack = jnp.concatenate([stack, stack], 1)
        powers = jnp.concatenate([mono_ref[...], mono_ref[...]], 1)

        @pl.loop(0, 2)
        def _(chunk):
            rows = pl.ds(pl.multiple_of(chunk * 2048, 2048), 2048)
            moments = lax.dot_general(
                powers, push_ref[rows, pl.ds(0, 2 * PIX)], CONTRACT, preferred_element_type=jnp.float32
            )
            tints = lax.dot_general(
                stack, push_ref[rows, pl.ds(2 * PIX, 2 * PIX)], CONTRACT, preferred_element_type=jnp.float32
            )
            tints = tints[:24] + tints[24:]
            for line in range(16):
                cols = slice(line * LANES, (line + 1) * LANES)
                base = ((group * 32) + chunk * 16 + line) * GRADS
                moment_ref[pl.ds(pl.multiple_of(base, 8), 8), :] = moments[:8, cols]
                for k in range(3):
                    own = jnp.where(diagonal, tints[k * 8 : k * 8 + 8, cols], 0.0)
                    moment_ref[pl.ds(base + 8 + k, 1), :] = jnp.sum(own, 0, keepdims=True)

    @pl.loop(0, 16)
    def _(octet):
        feature = [feat_ref[pl.ds(pl.multiple_of(f * LANES + octet * 8, 8), 8), :] for f in range(5)]
        centre_y = (16 * (strip * SLABS + octet // 4) + 8).astype(jnp.float32)
        m_x = feature[0] - centre_x
        m_y = feature[1] - centre_y

        def moment(k):
            return moment_ref[pl.ds(octet * 8 * GRADS + k, 8, stride=GRADS), :]

        total, s_x, s_y, s_xx, s_xy, s_yy = [moment(k) for k in range(6)]
        along_x = s_x - m_x * total
        along_y = s_y - m_y * total
        results = [
            feature[2] * along_x + feature[3] * along_y,
            feature[3] * along_x + feature[4] * along_y,
            -0.5 * (s_xx - m_x * (s_x + along_x)),
            -(s_xy - m_x * s_y - m_y * along_x),
            -0.5 * (s_yy - m_y * (s_y + along_y)),
            total,
            moment(8),
            moment(9),
            moment(10),
        ]
        for f in range(FEATS):
            grad_ref[pl.ds(pl.multiple_of(f * LANES + octet * 8, 8), 8), :] = results[f]

    sums_ref[...] = jnp.zeros(sums_ref.shape, jnp.float32)
    half_owner = lax.broadcasted_iota(jnp.int32, (LANES // 2, LANES), 0)
    place = lax.broadcasted_iota(jnp.int32, (2 * LANES, LANES), 0)

    def spread_out(count, totals):
        octet = count // 4
        quarter = lax.rem(count, 4)
        span = pl.ds(pl.multiple_of(octet * 8, 8), 8)
        totals = [jnp.where(quarter == 0, 0.0, total) for total in totals]
        first = [lambda source, f=f: f * LANES + source for f in LANE_OUT]
        totals = picked_lanes(
            grad_ref, first, lane_ref[span, :], row_ref[span, :], quarter * 32, 32, totals
        )
        for number, f in enumerate(LANE_OUT):
            back_ref[pl.ds(octet * 8 * FEATS + f, 8, stride=FEATS), :] = totals[number]
        slots = []
        owners = []
        for member in range(2):
            line = list_ref[pl.ds(count * 2 + member, 1), :]
            half = jnp.bitwise_and(jnp.right_shift(line, 7), LANES // 2 - 1)
            half = jnp.where(line < 0, -1, half)
            spot = jnp.right_shift(line, 13) * LANES + jnp.bitwise_and(line, CAP - 1)
            owners.append(jnp.broadcast_to(half, (LANES // 2, LANES)) == half_owner)
            same = jnp.broadcast_to(spot, (2 * LANES, LANES)) == place
            slots.append(jnp.where(same, 1.0, 0.0).astype(jnp.bfloat16))
        rows = []
        for f in DOT_OUT:
            lines = [grad_ref[pl.ds(f * LANES + count * 2 + member, 1), :] for member in range(2)]
            tops = [line.astype(jnp.bfloat16).astype(jnp.float32) for line in lines]
            pieces = tops + [line - top for line, top in zip(lines, tops)]
            rows.append(
                jnp.concatenate(
                    [
                        jnp.where(
                            owners[number % 2], jnp.broadcast_to(piece, (LANES // 2, LANES)), 0.0
                        ).astype(jnp.bfloat16)
                        for number, piece in enumerate(pieces)
                    ],
                    1,
                )
            )
        sums_ref[...] += lax.dot_general(
            jnp.concatenate(rows, 0),
            jnp.concatenate(slots + slots, 1),
            CONTRACT,
            preferred_element_type=jnp.float32,
        )
        return tuple(totals)

    blank = tuple(jnp.zeros((8, LANES), jnp.float32) for _ in LANE_OUT)
    lax.fori_loop(0, LANES // 2, spread_out, blank, unroll=8)
    for number, f in enumerate(DOT_OUT):
        for side in range(2):
            back_ref[pl.ds(side * (LANES // 2) * FEATS + f, LANES // 2, stride=FEATS), :] = sums_ref[
                pl.ds(number * (LANES // 2), LANES // 2), pl.ds(side * LANES, LANES)
            ]


def shade_kernel(params_ref, index_ref, list_ref, target_ref, expand_ref, mono_ref, image_ref, out_ref, *scratch):
    received_ref, lane_ref, row_ref, back_ref = scratch[:4]
    deliver(params_ref, index_ref, list_ref, received_ref, lane_ref, row_ref, *scratch[4:11])
    composite(
        received_ref, list_ref, lane_ref, row_ref, target_ref, expand_ref, mono_ref,
        image_ref, back_ref, *scratch[15:],
    )
    give_back(back_ref, out_ref, *scratch[11:15])


SUM_PARTS = 2


def update_kernel(
    back_ref, index_ref, params_ref, first_ref, second_ref,
    new_params_ref, new_first_ref, new_second_ref,
    rows_ref, sums_ref, slope_ref, tint_ref,
):
    block_rows(params_ref, rows_ref)
    row = functools.partial(strided, rows_ref)
    sublane = lax.broadcasted_iota(jnp.int32, (LANES, LANES), 0)
    short = lax.broadcasted_iota(jnp.int32, (BLOCKS, LANES), 0)

    @pl.loop(0, VIEWS, unroll=2)
    def _(camera):
        total = jnp.zeros((SUM_PARTS * FEATS * BLOCKS, LANES), jnp.float32)
        for pair in range(4):
            places, values = [], []
            for member in range(2):
                renderer = camera * 8 + pair * 2 + member
                line = index_ref[pl.ds(renderer, 1), :]
                low = jnp.broadcast_to(jnp.bitwise_and(line, LANES - 1), (LANES, LANES))
                high = jnp.broadcast_to(jnp.right_shift(line, 7), (BLOCKS, LANES))
                places.append(jnp.where(low == sublane, 1.0, 0.0).astype(jnp.bfloat16))
                here = high == short
                stacks = []
                for f in range(FEATS):
                    value = jnp.broadcast_to(back_ref[pl.ds(renderer * FEATS + f, 1), :], (BLOCKS, LANES))
                    stacks.append(jnp.where(here, value, 0.0))
                stack = jnp.concatenate(stacks, 0)
                values.append(jnp.concatenate(parts_of(stack, SUM_PARTS), 0))
            total = total + lax.dot_general(
                jnp.concatenate(values, 1),
                jnp.concatenate(places, 1),
                (((1,), (1,)), ((), ())),
                preferred_element_type=jnp.float32,
            )
        size = FEATS * BLOCKS
        merged = total[:size]
        for part in range(1, SUM_PARTS):
            merged = merged + total[part * size : (part + 1) * size]
        sums_ref[pl.ds(pl.multiple_of(camera * size, size), size), :] = merged

    logs = [row(3 + k) for k in range(3)]
    quat = [row(6 + k) for k in range(4)]
    sigma, spread_pull = jax.vjp(spread, logs, quat)
    blank = jnp.zeros((BLOCKS, LANES), jnp.float32)
    d_sigma = [blank] * 6
    d_x, d_y, d_z, d_log = blank, blank, blank, blank
    for camera in range(VIEWS):
        lean_x, lean_y, _, _, basis = CAMERAS[camera]

        def pushed(f):
            return sums_ref[pl.ds((camera * FEATS + f) * BLOCKS, BLOCKS), :]

        d_x = d_x + pushed(0)
        d_y = d_y + pushed(1)
        d_z = d_z + lean_x * pushed(0) + lean_y * pushed(1)
        _, pull = jax.vjp(lambda values: conic_of(values, lean_x, lean_y), sigma)
        (more,) = pull((pushed(2), pushed(3), pushed(4)))
        d_sigma = [old + new for old, new in zip(d_sigma, more)]
        d_log = d_log + pushed(5)
        for k in range(3):
            raw = raw_colour(row, basis, k)
            gate = jnp.where(raw > 0.0, 1.0, jnp.where(raw == 0.0, 0.5, 0.0))
            tint_ref[pl.ds((k * VIEWS + camera) * BLOCKS, BLOCKS), :] = gate * pushed(6 + k)
    d_scale, d_quat = spread_pull(d_sigma)
    slopes = [d_x, d_y, d_z] + list(d_scale) + list(d_quat) + [d_log / (1.0 + jnp.exp(row(10)))]
    for number, slope in enumerate(slopes):
        slope_ref[pl.ds(number, BLOCKS, stride=PROWS), :] = slope
    for k in range(3):
        for term in range(16):
            slope = blank
            for camera in range(VIEWS):
                tint = tint_ref[pl.ds((k * VIEWS + camera) * BLOCKS, BLOCKS), :]
                slope = slope + CAMERAS[camera][4][term] * tint
            slope_ref[pl.ds(11 + 16 * k + term, BLOCKS, stride=PROWS), :] = slope
    rates = rate_table()
    for block in range(BLOCKS):
        cols = pl.ds(block * LANES, LANES)
        slope = slope_ref[pl.ds(block * PROWS, PARAMS), :]
        new_first = beta_one * first_ref[:, cols] + (1.0 - beta_one) * slope
        new_second = beta_two * second_ref[:, cols] + (1.0 - beta_two) * slope * slope
        first_hat = new_first / (1.0 - beta_one**adam_count)
        second_hat = new_second / (1.0 - beta_two**adam_count)
        new_first_ref[:, cols] = new_first
        new_second_ref[:, cols] = new_second
        new_params_ref[:, cols] = params_ref[:, cols] - rates * first_hat / (
            jnp.sqrt(second_hat) + adam_epsilon
        )


WHOLE = pl.BlockSpec(memory_space=pltpu.VMEM)


def run_kernel(kernel, shapes, scratch, *operands, collective_id=None):
    many = isinstance(shapes, list)
    extra = {}
    if collective_id is not None:
        extra = dict(collective_id=collective_id, has_side_effects=True)
    return pl.pallas_call(
        kernel,
        out_shape=shapes,
        in_specs=[WHOLE] * len(operands),
        out_specs=[WHOLE] * len(shapes) if many else WHOLE,
        scratch_shapes=scratch,
        compiler_params=pltpu.CompilerParams(vmem_limit_bytes=VMEM_LIMIT, **extra),
    )(*operands)


def table(rows, dtype=jnp.float32):
    return jax.ShapeDtypeStruct((rows, LANES), dtype)


def buffer(*shape, dtype=jnp.float32):
    return pltpu.VMEM(shape, dtype)


def expand_table():
    x = np.arange(PIX) % 16 - 7.5
    y = np.arange(PIX) // 16 - 7.5
    wide = np.zeros((KROWS, PIX + 3 * LANES), np.float32)
    for number, mono in enumerate((x * x, x * y, y * y, x, y, np.ones(PIX))):
        wide[3 * number : 3 * number + 3, :PIX] = mono
    for k in range(3):
        wide[18 + 3 * k : 21 + 3 * k, PIX + k * LANES : PIX + (k + 1) * LANES] = 1.0
    narrow = np.zeros((16, PIX), np.float32)
    for number, mono in enumerate((np.ones(PIX), x, y, x * x, x * y, y * y)):
        narrow[number] = mono
    return jnp.asarray(wide, jnp.bfloat16), jnp.asarray(narrow, jnp.bfloat16)


def chunk_buffers():
    chunks = buffer(DEVICES, FEATS, LANES)
    return [chunks, chunks, pltpu.SemaphoreType.DMA, pltpu.SemaphoreType.DMA]


def ordered(tile_lists):
    return tile_lists.reshape(SLABS, 8, LIST).transpose(0, 2, 1).reshape(LANES, LANES)


def shade(params, index, entries, target):
    wide, narrow = expand_table()
    return run_kernel(
        shade_kernel,
        [jax.ShapeDtypeStruct((3 * TILE_DEV, PIX), jnp.float32), table(DEVICES * FEATS)],
        [
            buffer(DEVICES * FEATS, LANES),
            buffer(LANES, LANES, dtype=jnp.int32),
            buffer(LANES, LANES, dtype=jnp.int32),
            buffer(DEVICES * FEATS, LANES),
            buffer(BLOCKS * PROWS, LANES),
            buffer(VIEWS * FEATS * BLOCKS, LANES),
            buffer(8 * FEATS, LANES),
        ]
        + chunk_buffers()
        + chunk_buffers()
        + [
            buffer(FEATS * LANES, LANES),
            buffer(LANES * KROWS, LANES),
            buffer(GROUP_ROWS, PIX),
            buffer(GROUP_ROWS, PIX),
            buffer(GROUP_ROWS, 3 * LANES),
            buffer(GROUP_ROWS, 4 * PIX, dtype=jnp.bfloat16),
            buffer(FEATS * LANES, LANES),
            buffer(LANES * GRADS, LANES),
            buffer(len(DOT_IN) * LANES, 3 * LANES, dtype=jnp.bfloat16),
            buffer(len(DOT_OUT) * LANES // 2, 2 * LANES),
        ],
        params,
        index,
        entries,
        target,
        wide,
        narrow,
        collective_id=0,
    )


def owner_update(back, index, params, first, second):
    shape = jax.ShapeDtypeStruct(params.shape, jnp.float32)
    return run_kernel(
        update_kernel,
        [shape] * 3,
        [
            buffer(BLOCKS * PROWS, LANES),
            buffer(VIEWS * FEATS * BLOCKS, LANES),
            buffer(BLOCKS * PROWS, LANES),
            buffer(3 * VIEWS * BLOCKS, LANES),
        ],
        back,
        index,
        params,
        first,
        second,
    )


def per_device(params, first_moment, second_moment, target_images, tile_lists, send_index):
    index = send_index[0]
    entries = ordered(tile_lists)
    target = target_images.transpose(1, 0, 2).reshape(3 * TILE_DEV, PIX)
    image, back = shade(params, index, entries, target)
    new_params, new_first, new_second = owner_update(back, index, params, first_moment, second_moment)
    image = image.reshape(3, TILE_DEV, PIX).transpose(1, 0, 2)
    return (image, new_params, new_first, new_second)


def solution(mesh):
    in_specs = (
        P(None, AXES),
        P(None, AXES),
        P(None, AXES),
        P(AXES, None, None),
        P(AXES, None),
        P(AXES, None, None),
    )
    out_specs = (P(AXES, None, None), P(None, AXES), P(None, AXES), P(None, AXES))
    return jax.shard_map(
        per_device, mesh=mesh, in_specs=in_specs, out_specs=out_specs, check_vma=False
    )
```

```python
import functools
import math

import jax
import jax.numpy as jnp
import numpy as np
from jax import lax
from jax.experimental import pallas as pl
from jax.experimental.pallas import tpu as pltpu
from jax.sharding import PartitionSpec as P

PARAMS = 59
PIX = 256
VIEWS = 16
LIST = 512
TILE_DEV = 32
GS_DEV = 2048
DEVICES = 128
CAP = 128
TABLE_ROWS = 1168
FEATS = 9
BLOCKS = 16
PROWS = 65
LANES = 128
SLABS = 4
LOG2E = 1.4426950408889634
AXES = ("gauss", "render")
CONTRACT = (((1,), (1,)), ((), ()))
VMEM_LIMIT = 56 * 1024 * 1024

sh_first = 0.28209479177387814
sh_second = 0.4886025119029199
sh_third = (
    1.0925484305920792,
    -1.0925484305920792,
    0.31539156525252005,
    -1.0925484305920792,
    0.5462742152960396,
)
sh_fourth = (
    -0.5900435899266435,
    2.890611442640554,
    -0.4570457994644658,
    0.3731763325901154,
    -0.4570457994644658,
    1.445305721320277,
    -0.5900435899266435,
)
tilt_reach = 0.25
beta_one = 0.9
beta_two = 0.999
adam_epsilon = 1e-15
adam_count = 1000.0


def rate_table():
    row = lax.broadcasted_iota(jnp.int32, (PARAMS, LANES), 0)
    rates = jnp.where((row == 11) | (row == 27) | (row == 43), 0.0025, 0.000125)
    rates = jnp.where(row == 10, 0.05, rates)
    for last, rate in ((10, 0.001), (6, 0.005), (3, 0.0016)):
        rates = jnp.where(row < last, rate, rates)
    return rates.astype(jnp.float32)


def sh_basis(dir_x, dir_y, dir_z):
    sq_x = dir_x * dir_x
    sq_y = dir_y * dir_y
    sq_z = dir_z * dir_z
    return [
        sh_first,
        -sh_second * dir_y,
        sh_second * dir_z,
        -sh_second * dir_x,
        sh_third[0] * dir_x * dir_y,
        sh_third[1] * dir_y * dir_z,
        sh_third[2] * (2.0 * sq_z - sq_x - sq_y),
        sh_third[3] * dir_x * dir_z,
        sh_third[4] * (sq_x - sq_y),
        sh_fourth[0] * dir_y * (3.0 * sq_x - sq_y),
        sh_fourth[1] * dir_x * dir_y * dir_z,
        sh_fourth[2] * dir_y * (4.0 * sq_z - sq_x - sq_y),
        sh_fourth[3] * dir_z * (2.0 * sq_z - 3.0 * sq_x - 3.0 * sq_y),
        sh_fourth[4] * dir_x * (4.0 * sq_z - sq_x - sq_y),
        sh_fourth[5] * dir_z * (sq_x - sq_y),
        sh_fourth[6] * dir_x * (sq_x - 3.0 * sq_y),
    ]


def camera_constants(camera):
    angle = camera * (2.0 * math.pi / VIEWS)
    lean_x = tilt_reach * math.cos(angle)
    lean_y = tilt_reach * math.sin(angle)
    length = math.sqrt(1.0 + lean_x * lean_x + lean_y * lean_y)
    basis = sh_basis(lean_x / length, lean_y / length, -1.0 / length)
    return (lean_x, lean_y, 16.0 * (camera % 4), 16.0 * (camera // 4), basis)


CAMERAS = [camera_constants(camera) for camera in range(VIEWS)]


def spread(log_scales, quat):
    squares = [jnp.exp(2.0 * value) for value in log_scales]
    norm = jnp.sqrt(quat[0] * quat[0] + quat[1] * quat[1] + quat[2] * quat[2] + quat[3] * quat[3])
    q_w, q_x, q_y, q_z = [part / norm for part in quat]
    rotation = [
        [
            1.0 - 2.0 * (q_y * q_y + q_z * q_z),
            2.0 * (q_x * q_y - q_w * q_z),
            2.0 * (q_x * q_z + q_w * q_y),
        ],
        [
            2.0 * (q_x * q_y + q_w * q_z),
            1.0 - 2.0 * (q_x * q_x + q_z * q_z),
            2.0 * (q_y * q_z - q_w * q_x),
        ],
        [
            2.0 * (q_x * q_z - q_w * q_y),
            2.0 * (q_y * q_z + q_w * q_x),
            1.0 - 2.0 * (q_x * q_x + q_y * q_y),
        ],
    ]
    return [
        rotation[row][0] * rotation[col][0] * squares[0]
        + rotation[row][1] * rotation[col][1] * squares[1]
        + rotation[row][2] * rotation[col][2] * squares[2]
        for row, col in ((0, 0), (0, 1), (0, 2), (1, 1), (1, 2), (2, 2))
    ]


def conic_of(sigma, lean_x, lean_y):
    s_xx, s_xy, s_xz, s_yy, s_yz, s_zz = sigma
    cov_xx = s_xx + (2.0 * lean_x) * s_xz + (lean_x * lean_x) * s_zz + 0.3
    cov_xy = s_xy + lean_x * s_yz + lean_y * s_xz + (lean_x * lean_y) * s_zz
    cov_yy = s_yy + (2.0 * lean_y) * s_yz + (lean_y * lean_y) * s_zz + 0.3
    inverse = 1.0 / (cov_xx * cov_yy - cov_xy * cov_xy)
    return cov_yy * inverse, -cov_xy * inverse, cov_xx * inverse


def raw_colour(row, basis, channel):
    total = 0.5 + row(11 + 16 * channel) * basis[0]
    for term in range(1, 16):
        total = total + row(11 + 16 * channel + term) * basis[term]
    return total


def block_rows(source, dest):
    rows = source.shape[0]
    for block in range(BLOCKS):
        dest[pl.ds(block * PROWS, rows), :] = source[:, pl.ds(block * LANES, LANES)]


def strided(ref, row):
    return ref[pl.ds(row, BLOCKS, stride=PROWS), :]


def parts_of(value, count):
    parts = []
    for step in range(count):
        part = value.astype(jnp.bfloat16)
        parts.append(part)
        if step + 1 < count:
            value = value - part.astype(jnp.float32)
    return parts


MESH = pl.DeviceIdType.MESH


def own_number():
    return lax.axis_index(AXES[0]) * lax.axis_size(AXES[1]) + lax.axis_index(AXES[1])


def coordinates(number):
    across = lax.axis_size(AXES[1])
    return (number // across, lax.rem(number, across))


def announce():
    me = own_number()
    barrier = pltpu.get_barrier_semaphore()

    def tell(step, carry):
        pl.semaphore_signal(
            barrier,
            inc=1,
            device_id=coordinates(lax.rem(me + step, DEVICES)),
            device_id_type=MESH,
        )
        return carry

    lax.fori_loop(1, DEVICES, tell, 0, unroll=True)
    return barrier


def send_chunk(target, me, send_ref, recv_ref, send_sem, recv_sem):
    pltpu.make_async_remote_copy(
        src_ref=send_ref.at[target],
        dst_ref=recv_ref.at[me],
        send_sem=send_sem,
        recv_sem=recv_sem,
        device_id=coordinates(target),
        device_id_type=MESH,
    ).start()


def all_chunks(me, send_ref, recv_ref, send_sem, recv_sem):
    most = pl.ds(0, DEVICES - 1)
    return pltpu.make_async_remote_copy(
        src_ref=send_ref.at[most],
        dst_ref=recv_ref.at[most],
        send_sem=send_sem,
        recv_sem=recv_sem,
        device_id=coordinates(me),
        device_id_type=MESH,
    )


def flatten_chunks(recv_ref, out_ref):
    for source in range(DEVICES):
        out_ref[pl.ds(source * FEATS, FEATS), :] = recv_ref[source]


def order_lists(tile_ref, turned_ref, list_ref):
    gap = jnp.zeros((LANES - 8, LANES), jnp.float32)
    for slab in range(SLABS):
        for block in range(LIST // LANES):
            part = tile_ref[pl.ds(slab * 8, 8), pl.ds(block * LANES, LANES)].astype(jnp.float32)
            turned_ref[pl.ds(block * LANES, LANES), :] = jnp.concatenate([part, gap], 0).T
        total = turned_ref[pl.ds(0, 32, stride=16), :]
        for place in range(1, 16):
            total = total + pltpu.roll(turned_ref[pl.ds(place, 32, stride=16), :], 8 * place, axis=1)
        list_ref[pl.ds(slab * 32, 32), :] = total.astype(jnp.int32)


def invert_lists(list_ref, lane_ref, row_ref):
    sublane = lax.broadcasted_iota(jnp.int32, (LANES, LANES), 0)
    lane = lax.broadcasted_iota(jnp.int32, (LANES, LANES), 1).astype(jnp.float32)

    def step(pair, total):
        owners, slots = [], []
        for member in range(2):
            line = list_ref[pl.ds(pair * 2 + member, 1), :]
            low = jnp.broadcast_to(jnp.bitwise_and(line, CAP - 1), (LANES, LANES))
            high = jnp.broadcast_to(jnp.right_shift(line, 7), (LANES, LANES))
            number = (pair * 2 + member + 1).astype(jnp.float32)
            owners.append(jnp.where(high == sublane, 1.0, 0.0).astype(jnp.bfloat16))
            same = low == sublane
            slots.append(
                jnp.concatenate([jnp.where(same, lane, 0.0), jnp.where(same, number, 0.0)], 0).astype(
                    jnp.bfloat16
                )
            )
        return total + lax.dot_general(
            jnp.concatenate(owners, 1),
            jnp.concatenate(slots, 1),
            CONTRACT,
            preferred_element_type=jnp.float32,
        )

    total = lax.fori_loop(0, LANES // 2, step, jnp.zeros((LANES, 2 * LANES), jnp.float32), unroll=8)
    lane_ref[...] = total[:, :LANES].astype(jnp.int32)
    row_ref[...] = total[:, LANES:].astype(jnp.int32) - 1


def deliver(
    params_ref, index_ref, tile_ref, turned_ref, list_ref,
    out_ref, lane_ref, row_ref,
    rows_ref, table_ref, flat_ref, send_ref, recv_ref, send_sem, recv_sem,
):
    me = own_number()
    barrier = announce()
    block_rows(params_ref, rows_ref)
    row = functools.partial(strided, rows_ref)
    sigma = spread([row(3 + k) for k in range(3)], [row(6 + k) for k in range(4)])
    logit = row(10)
    log_opacity = -LOG2E * (jnp.maximum(-logit, 0.0) + jnp.log1p(jnp.exp(-jnp.abs(logit))))
    for camera in range(VIEWS):
        lean_x, lean_y, shift_x, shift_y, basis = CAMERAS[camera]
        height = row(2)
        features = [row(0) + lean_x * height - shift_x, row(1) + lean_y * height - shift_y]
        features += list(conic_of(sigma, lean_x, lean_y))
        features.append(log_opacity)
        features += [jnp.maximum(raw_colour(row, basis, k), 0.0) for k in range(3)]
        for f in range(FEATS):
            table_ref[pl.ds((camera * FEATS + f) * BLOCKS, BLOCKS), :] = features[f]
    pl.semaphore_wait(barrier, DEVICES - 1)

    @pl.loop(0, VIEWS)
    def _(turn):
        camera = lax.rem(me // (DEVICES // VIEWS) + turn, VIEWS)
        chosen = index_ref[pl.ds(pl.multiple_of(camera * 8, 8), 8), :]
        low = jnp.bitwise_and(chosen, LANES - 1)
        high = jnp.right_shift(chosen, 7)
        totals = [jnp.zeros((8, LANES), jnp.float32) for _ in range(FEATS)]
        for block in range(BLOCKS):
            here = high == block
            for f in range(FEATS):
                line = table_ref[pl.ds((camera * FEATS + f) * BLOCKS + block, 1), :]
                line = jnp.broadcast_to(line, (8, LANES))
                picked = jnp.take_along_axis(line, low, axis=1)
                totals[f] = jnp.where(here, picked, totals[f])
        for f in range(FEATS):
            flat_ref[pl.ds(f, 8, stride=FEATS), :] = totals[f]
        for member in range(8):
            send_ref[camera * 8 + member] = flat_ref[pl.ds(member * FEATS, FEATS), :]
        for step in range(8):
            target = camera * 8 + lax.rem(me + step, 8)

            @pl.when(target != me)
            def _():
                send_chunk(target, me, send_ref, recv_ref, send_sem, recv_sem)

    order_lists(tile_ref, turned_ref, list_ref)
    invert_lists(list_ref, lane_ref, row_ref)
    whole = all_chunks(me, send_ref, recv_ref, send_sem, recv_sem)
    recv_ref[me] = send_ref[me]
    whole.wait_recv()
    flatten_chunks(recv_ref, out_ref)
    whole.wait_send()


def give_back(back_ref, out_ref, send_ref, recv_ref, send_sem, recv_sem):
    me = own_number()
    for target in range(DEVICES):
        send_ref[target] = back_ref[pl.ds(target * FEATS, FEATS), :]

    def send(step, carry):
        send_chunk(lax.rem(me + step, DEVICES), me, send_ref, recv_ref, send_sem, recv_sem)
        return carry

    lax.fori_loop(1, DEVICES, send, 0, unroll=8)
    whole = all_chunks(me, send_ref, recv_ref, send_sem, recv_sem)
    recv_ref[me] = send_ref[me]
    whole.wait_recv()
    flatten_chunks(recv_ref, out_ref)
    whole.wait_send()


def picked_lanes(table, first, low, high, base, count, totals):
    for step in range(count):
        source = base + step
        here = high == source
        for number, place in enumerate(first):
            line = jnp.broadcast_to(table[pl.ds(place(source), 1), :], (8, LANES))
            picked = jnp.take_along_axis(line, low, axis=1)
            totals[number] = jnp.where(here, picked, totals[number])
    return totals


LANE_IN = (0, 1, 5)
DOT_IN = (2, 3, 4, 6, 7, 8)
LANE_OUT = (0, 1, 5)
DOT_OUT = (2, 3, 4, 6, 7, 8)
KROWS = 32
KPITCH = 40
GRADS = 24
GROUP_ROWS = LIST * 8


def composite(
    table_ref,
    list_ref,
    lane_ref,
    row_ref,
    target_ref,
    expand_ref,
    mono_ref,
    image_ref,
    back_ref,
    feat_ref,
    coef_ref,
    alpha_ref,
    weight_ref,
    colour_ref,
    push_ref,
    grad_ref,
    moment_ref,
    halves_ref,
    sums_ref,
):
    render = lax.axis_index(AXES[1])
    device = lax.axis_index(AXES[0]) * lax.axis_size(AXES[1]) + render
    strip = lax.rem(device, DEVICES // VIEWS)
    lane_tile = jnp.bitwise_and(lax.broadcasted_iota(jnp.int32, (8, LANES), 1), 7)
    centre_x = 16.0 * lane_tile.astype(jnp.float32) + 8.0

    owner = lax.broadcasted_iota(jnp.int32, (LANES, 2 * LANES), 0)
    for number, f in enumerate(DOT_IN):
        value = table_ref[pl.ds(f, DEVICES, stride=FEATS), :]
        for which, part in enumerate(parts_of(value, 3)):
            halves_ref[pl.ds(number * LANES, LANES), pl.ds(which * LANES, LANES)] = part

    def collect(count, totals):
        octet = count // 4
        quarter = lax.rem(count, 4)
        span = pl.ds(pl.multiple_of(octet * 8, 8), 8)
        low = jnp.bitwise_and(list_ref[span, :], CAP - 1)
        high = jnp.right_shift(list_ref[span, :], 7)
        totals = [jnp.where(quarter == 0, 0.0, total) for total in totals]
        first = [lambda source, f=f: source * FEATS + f for f in LANE_IN]
        totals = picked_lanes(table_ref, first, low, high, quarter * 32, 32, totals)
        for number, f in enumerate(LANE_IN):
            feat_ref[pl.ds(pl.multiple_of(f * LANES + octet * 8, 8), 8), :] = totals[number]
        lines = [list_ref[pl.ds(count * 2 + member, 1), :] for member in range(2)]
        line = jnp.broadcast_to(jnp.concatenate(lines, 1), (LANES, 2 * LANES))
        slot = jnp.where(jnp.bitwise_and(line, CAP - 1) == owner, 1.0, 0.0).astype(jnp.bfloat16)
        thrice = jnp.concatenate([slot, slot, slot], 0)
        exact = jnp.dot(
            halves_ref[pl.ds(0, 3 * LANES), :], thrice, preferred_element_type=jnp.float32
        )
        other = jnp.dot(
            halves_ref[pl.ds(3 * LANES, 3 * LANES), pl.ds(0, 2 * LANES)],
            thrice[: 2 * LANES],
            preferred_element_type=jnp.float32,
        )
        found = [exact[k * LANES : (k + 1) * LANES] for k in range(3)]
        found += [other[k * LANES : (k + 1) * LANES] for k in range(3)]
        mine = jnp.right_shift(line, 7) == owner
        for number, f in enumerate(DOT_IN):
            value = jnp.where(mine, found[number], 0.0)
            value = jnp.sum(value, 0, keepdims=True)
            for member in range(2):
                feat_ref[pl.ds(f * LANES + count * 2 + member, 1), :] = value[
                    :, member * LANES : (member + 1) * LANES
                ]
        return tuple(totals)

    blank = tuple(jnp.zeros((8, LANES), jnp.float32) for _ in LANE_IN)
    lax.fori_loop(0, LANES // 2, collect, blank, unroll=8)
    zero = jnp.zeros((8, LANES), jnp.float32)

    @pl.loop(0, 16)
    def _(octet):
        base = pl.multiple_of(octet * 8, 8)
        feature = [feat_ref[pl.ds(pl.multiple_of(f * LANES + octet * 8, 8), 8), :] for f in range(FEATS)]
        live = list_ref[pl.ds(base, 8), :] >= 0
        centre_y = (16 * (strip * SLABS + octet // 4) + 8).astype(jnp.float32)
        m_x = feature[0] - centre_x
        m_y = feature[1] - centre_y
        a = (-0.5 * LOG2E) * feature[2]
        b = -LOG2E * feature[3]
        c = (-0.5 * LOG2E) * feature[4]
        to_x = 2.0 * a * m_x + b * m_y
        to_y = b * m_x + 2.0 * c * m_y
        level = a * m_x * m_x + b * m_x * m_y + c * m_y * m_y
        level = jnp.where(live, level + feature[5], -10000.0)
        values = [a, b, c, -to_x, -to_y, level] + feature[6:9]
        place = 0
        for value in values:
            for part in parts_of(value, 3):
                coef_ref[pl.ds(octet * 8 * KPITCH + place, 8, stride=KPITCH), :] = part.astype(jnp.float32)
                place += 1
        for rest in range(place, KROWS):
            coef_ref[pl.ds(octet * 8 * KPITCH + rest, 8, stride=KPITCH), :] = zero

    diagonal = lax.broadcasted_iota(jnp.int32, (8, LANES), 0) == lane_tile

    @pl.loop(0, SLABS)
    def _(group):
        @pl.loop(0, 8, unroll=4)
        def _(quad):
            lefts = []
            for sub in range(4):
                start = pl.multiple_of((group * 32 + quad * 4 + sub) * KPITCH, 8)
                lefts.append(coef_ref[pl.ds(start, KROWS), :].T.astype(jnp.bfloat16))
            wide = jnp.dot(jnp.concatenate(lefts, 0), expand_ref[...], preferred_element_type=jnp.float32)
            out = pl.ds(pl.multiple_of(quad * 512, 512), 512)
            alpha_ref[out, :] = wide[:, :PIX]
            colour_ref[out, :] = wide[:, PIX:]

        def forward(block, carry):
            through = list(carry[:2])
            image = list(carry[2:])
            for lot in range(2):
                alphas, weights, spots = [], [], []
                for u in range(8):
                    here = pl.ds(pl.multiple_of(block * LANES + (lot * 8 + u) * 8, 8), 8)
                    spots.append(here)
                    alphas.append(
                        [
                            jnp.minimum(jnp.exp2(alpha_ref[here, pl.ds(half * LANES, LANES)]), 0.99)
                            for half in range(2)
                        ]
                    )
                for u in range(8):
                    shade = [colour_ref[spots[u], pl.ds(k * LANES, LANES)] for k in range(3)]
                    weights.append([])
                    for half in range(2):
                        weight = alphas[u][half] * through[half]
                        through[half] = through[half] * (1.0 - alphas[u][half])
                        weights[u].append(weight)
                        for k in range(3):
                            image[k * 2 + half] = image[k * 2 + half] + shade[k] * weight
                for u in range(8):
                    for half in range(2):
                        cols = pl.ds(half * LANES, LANES)
                        alpha_ref[spots[u], cols] = alphas[u][half]
                        weight_ref[spots[u], cols] = weights[u][half]
            return tuple(through + image)

        ones = jnp.ones((8, LANES), jnp.float32)
        image = lax.fori_loop(0, 32, forward, (ones, ones) + (zero,) * 6)[2:]
        residual = []
        for k in range(3):
            tiles = pl.ds(pl.multiple_of(k * TILE_DEV + group * 8, 8), 8)
            for half in range(2):
                cols = pl.ds(half * LANES, LANES)
                image_ref[tiles, cols] = image[k * 2 + half]
                residual.append(image[k * 2 + half] - target_ref[tiles, cols])

        def backward(count, carry):
            behind = list(carry)
            block = 31 - count
            for pair in range(7, -1, -1):
                pushes = [[None, None], [None, None]]
                loads = [[None, None], [None, None]]
                for member in (1, 0):
                    here = pl.ds(pl.multiple_of(block * LANES + pair * 16 + member * 8, 8), 8)
                    shade = [colour_ref[here, pl.ds(k * LANES, LANES)] for k in range(3)]
                    for half in range(2):
                        cols = pl.ds(half * LANES, LANES)
                        alpha = alpha_ref[here, cols]
                        weight = weight_ref[here, cols]
                        worth = (
                            shade[0] * residual[half]
                            + shade[1] * residual[2 + half]
                            + shade[2] * residual[4 + half]
                        )
                        loads[half][member] = weight
                        gain = worth - behind[half]
                        behind[half] = behind[half] + alpha * gain
                        pushes[half][member] = jnp.where(alpha < 0.99, weight * gain, 0.0)
                rows = pl.ds(pl.multiple_of(block * LANES + pair * 16, 16), 16)
                for half in range(2):
                    parts = parts_of(jnp.concatenate(pushes[half], 0), 2)
                    parts += parts_of(jnp.concatenate(loads[half], 0), 2)
                    for which, part in enumerate(parts):
                        push_ref[rows, pl.ds(which * PIX + half * LANES, LANES)] = part
            return tuple(behind)

        lax.fori_loop(0, 32, backward, (zero, zero))
        stack = jnp.concatenate(
            [jnp.concatenate([residual[k * 2], residual[k * 2 + 1]], 1) for k in range(3)], 0
        )
        stack = jnp.concatenate(parts_of(stack, 2), 0)
        stack = jnp.concatenate([stack, stack], 1)
        powers = jnp.concatenate([mono_ref[...], mono_ref[...]], 1)

        @pl.loop(0, 2)
        def _(chunk):
            rows = pl.ds(pl.multiple_of(chunk * 2048, 2048), 2048)
            moments = lax.dot_general(
                powers, push_ref[rows, pl.ds(0, 2 * PIX)], CONTRACT, preferred_element_type=jnp.float32
            )
            tints = lax.dot_general(
                stack, push_ref[rows, pl.ds(2 * PIX, 2 * PIX)], CONTRACT, preferred_element_type=jnp.float32
            )
            tints = tints[:24] + tints[24:]
            for line in range(16):
                cols = slice(line * LANES, (line + 1) * LANES)
                base = ((group * 32) + chunk * 16 + line) * GRADS
                moment_ref[pl.ds(pl.multiple_of(base, 8), 8), :] = moments[:8, cols]
                for k in range(3):
                    own = jnp.where(diagonal, tints[k * 8 : k * 8 + 8, cols], 0.0)
                    moment_ref[pl.ds(base + 8 + k, 1), :] = jnp.sum(own, 0, keepdims=True)

    @pl.loop(0, 16)
    def _(octet):
        feature = [feat_ref[pl.ds(pl.multiple_of(f * LANES + octet * 8, 8), 8), :] for f in range(5)]
        centre_y = (16 * (strip * SLABS + octet // 4) + 8).astype(jnp.float32)
        m_x = feature[0] - centre_x
        m_y = feature[1] - centre_y

        def moment(k):
            return moment_ref[pl.ds(octet * 8 * GRADS + k, 8, stride=GRADS), :]

        total, s_x, s_y, s_xx, s_xy, s_yy = [moment(k) for k in range(6)]
        along_x = s_x - m_x * total
        along_y = s_y - m_y * total
        results = [
            feature[2] * along_x + feature[3] * along_y,
            feature[3] * along_x + feature[4] * along_y,
            -0.5 * (s_xx - m_x * (s_x + along_x)),
            -(s_xy - m_x * s_y - m_y * along_x),
            -0.5 * (s_yy - m_y * (s_y + along_y)),
            total,
            moment(8),
            moment(9),
            moment(10),
        ]
        for f in range(FEATS):
            grad_ref[pl.ds(pl.multiple_of(f * LANES + octet * 8, 8), 8), :] = results[f]

    sums_ref[...] = jnp.zeros(sums_ref.shape, jnp.float32)
    half_owner = lax.broadcasted_iota(jnp.int32, (LANES // 2, LANES), 0)
    place = lax.broadcasted_iota(jnp.int32, (2 * LANES, LANES), 0)

    def spread_out(count, totals):
        octet = count // 4
        quarter = lax.rem(count, 4)
        span = pl.ds(pl.multiple_of(octet * 8, 8), 8)
        totals = [jnp.where(quarter == 0, 0.0, total) for total in totals]
        first = [lambda source, f=f: f * LANES + source for f in LANE_OUT]
        totals = picked_lanes(
            grad_ref, first, lane_ref[span, :], row_ref[span, :], quarter * 32, 32, totals
        )
        for number, f in enumerate(LANE_OUT):
            back_ref[pl.ds(octet * 8 * FEATS + f, 8, stride=FEATS), :] = totals[number]
        slots = []
        owners = []
        for member in range(2):
            line = list_ref[pl.ds(count * 2 + member, 1), :]
            half = jnp.bitwise_and(jnp.right_shift(line, 7), LANES // 2 - 1)
            half = jnp.where(line < 0, -1, half)
            spot = jnp.right_shift(line, 13) * LANES + jnp.bitwise_and(line, CAP - 1)
            owners.append(jnp.broadcast_to(half, (LANES // 2, LANES)) == half_owner)
            same = jnp.broadcast_to(spot, (2 * LANES, LANES)) == place
            slots.append(jnp.where(same, 1.0, 0.0).astype(jnp.bfloat16))
        rows = []
        for f in DOT_OUT:
            lines = [grad_ref[pl.ds(f * LANES + count * 2 + member, 1), :] for member in range(2)]
            tops = [line.astype(jnp.bfloat16).astype(jnp.float32) for line in lines]
            pieces = tops + [line - top for line, top in zip(lines, tops)]
            rows.append(
                jnp.concatenate(
                    [
                        jnp.where(
                            owners[number % 2], jnp.broadcast_to(piece, (LANES // 2, LANES)), 0.0
                        ).astype(jnp.bfloat16)
                        for number, piece in enumerate(pieces)
                    ],
                    1,
                )
            )
        sums_ref[...] += lax.dot_general(
            jnp.concatenate(rows, 0),
            jnp.concatenate(slots + slots, 1),
            CONTRACT,
            preferred_element_type=jnp.float32,
        )
        return tuple(totals)

    blank = tuple(jnp.zeros((8, LANES), jnp.float32) for _ in LANE_OUT)
    lax.fori_loop(0, LANES // 2, spread_out, blank, unroll=8)
    for number, f in enumerate(DOT_OUT):
        for side in range(2):
            back_ref[pl.ds(side * (LANES // 2) * FEATS + f, LANES // 2, stride=FEATS), :] = sums_ref[
                pl.ds(number * (LANES // 2), LANES // 2), pl.ds(side * LANES, LANES)
            ]


def shade_kernel(params_ref, index_ref, tile_ref, target_ref, expand_ref, mono_ref, image_ref, out_ref, *scratch):
    turned_ref, list_ref = scratch[:2]
    scratch = scratch[2:]
    received_ref, lane_ref, row_ref, back_ref = scratch[:4]
    deliver(params_ref, index_ref, tile_ref, turned_ref, list_ref, received_ref, lane_ref, row_ref, *scratch[4:11])
    composite(
        received_ref, list_ref, lane_ref, row_ref, target_ref, expand_ref, mono_ref,
        image_ref, back_ref, *scratch[15:],
    )
    give_back(back_ref, out_ref, *scratch[11:15])


SUM_PARTS = 2


def update_kernel(
    back_ref, index_ref, params_ref, first_ref, second_ref,
    new_params_ref, new_first_ref, new_second_ref,
    rows_ref, sums_ref, slope_ref, tint_ref,
):
    block_rows(params_ref, rows_ref)
    row = functools.partial(strided, rows_ref)
    sublane = lax.broadcasted_iota(jnp.int32, (LANES, LANES), 0)
    short = lax.broadcasted_iota(jnp.int32, (BLOCKS, LANES), 0)

    @pl.loop(0, VIEWS, unroll=4)
    def _(camera):
        total = jnp.zeros((SUM_PARTS * FEATS * BLOCKS, LANES), jnp.float32)
        for pair in range(4):
            places, values = [], []
            for member in range(2):
                renderer = camera * 8 + pair * 2 + member
                line = index_ref[pl.ds(renderer, 1), :]
                low = jnp.broadcast_to(jnp.bitwise_and(line, LANES - 1), (LANES, LANES))
                high = jnp.broadcast_to(jnp.right_shift(line, 7), (BLOCKS, LANES))
                places.append(jnp.where(low == sublane, 1.0, 0.0).astype(jnp.bfloat16))
                here = high == short
                stacks = []
                for f in range(FEATS):
                    value = jnp.broadcast_to(back_ref[pl.ds(renderer * FEATS + f, 1), :], (BLOCKS, LANES))
                    stacks.append(jnp.where(here, value, 0.0))
                stack = jnp.concatenate(stacks, 0)
                values.append(jnp.concatenate(parts_of(stack, SUM_PARTS), 0))
            total = total + lax.dot_general(
                jnp.concatenate(values, 1),
                jnp.concatenate(places, 1),
                (((1,), (1,)), ((), ())),
                preferred_element_type=jnp.float32,
            )
        size = FEATS * BLOCKS
        merged = total[:size]
        for part in range(1, SUM_PARTS):
            merged = merged + total[part * size : (part + 1) * size]
        sums_ref[pl.ds(pl.multiple_of(camera * size, size), size), :] = merged

    logs = [row(3 + k) for k in range(3)]
    quat = [row(6 + k) for k in range(4)]
    sigma, spread_pull = jax.vjp(spread, logs, quat)
    blank = jnp.zeros((BLOCKS, LANES), jnp.float32)
    d_sigma = [blank] * 6
    d_x, d_y, d_z, d_log = blank, blank, blank, blank
    for camera in range(VIEWS):
        lean_x, lean_y, _, _, basis = CAMERAS[camera]

        def pushed(f):
            return sums_ref[pl.ds((camera * FEATS + f) * BLOCKS, BLOCKS), :]

        d_x = d_x + pushed(0)
        d_y = d_y + pushed(1)
        d_z = d_z + lean_x * pushed(0) + lean_y * pushed(1)
        _, pull = jax.vjp(lambda values: conic_of(values, lean_x, lean_y), sigma)
        (more,) = pull((pushed(2), pushed(3), pushed(4)))
        d_sigma = [old + new for old, new in zip(d_sigma, more)]
        d_log = d_log + pushed(5)
        for k in range(3):
            raw = raw_colour(row, basis, k)
            gate = jnp.where(raw > 0.0, 1.0, jnp.where(raw == 0.0, 0.5, 0.0))
            tint_ref[pl.ds((k * VIEWS + camera) * BLOCKS, BLOCKS), :] = gate * pushed(6 + k)
    d_scale, d_quat = spread_pull(d_sigma)
    slopes = [d_x, d_y, d_z] + list(d_scale) + list(d_quat) + [d_log / (1.0 + jnp.exp(row(10)))]
    for number, slope in enumerate(slopes):
        slope_ref[pl.ds(number, BLOCKS, stride=PROWS), :] = slope
    for k in range(3):
        for term in range(16):
            slope = blank
            for camera in range(VIEWS):
                tint = tint_ref[pl.ds((k * VIEWS + camera) * BLOCKS, BLOCKS), :]
                slope = slope + CAMERAS[camera][4][term] * tint
            slope_ref[pl.ds(11 + 16 * k + term, BLOCKS, stride=PROWS), :] = slope
    rates = rate_table()
    for block in range(BLOCKS):
        cols = pl.ds(block * LANES, LANES)
        slope = slope_ref[pl.ds(block * PROWS, PARAMS), :]
        new_first = beta_one * first_ref[:, cols] + (1.0 - beta_one) * slope
        new_second = beta_two * second_ref[:, cols] + (1.0 - beta_two) * slope * slope
        first_hat = new_first * (1.0 / (1.0 - beta_one**adam_count))
        second_hat = new_second * (1.0 / (1.0 - beta_two**adam_count))
        new_first_ref[:, cols] = new_first
        new_second_ref[:, cols] = new_second
        new_params_ref[:, cols] = params_ref[:, cols] - rates * first_hat / (
            jnp.sqrt(second_hat) + adam_epsilon
        )


WHOLE = pl.BlockSpec(memory_space=pltpu.VMEM)


def run_kernel(kernel, shapes, scratch, *operands, collective_id=None):
    many = isinstance(shapes, list)
    extra = {}
    if collective_id is not None:
        extra = dict(collective_id=collective_id, has_side_effects=True)
    return pl.pallas_call(
        kernel,
        out_shape=shapes,
        in_specs=[WHOLE] * len(operands),
        out_specs=[WHOLE] * len(shapes) if many else WHOLE,
        scratch_shapes=scratch,
        compiler_params=pltpu.CompilerParams(vmem_limit_bytes=VMEM_LIMIT, **extra),
    )(*operands)


def table(rows, dtype=jnp.float32):
    return jax.ShapeDtypeStruct((rows, LANES), dtype)


def buffer(*shape, dtype=jnp.float32):
    return pltpu.VMEM(shape, dtype)


def expand_table():
    x = np.arange(PIX) % 16 - 7.5
    y = np.arange(PIX) // 16 - 7.5
    wide = np.zeros((KROWS, PIX + 3 * LANES), np.float32)
    for number, mono in enumerate((x * x, x * y, y * y, x, y, np.ones(PIX))):
        wide[3 * number : 3 * number + 3, :PIX] = mono
    for k in range(3):
        wide[18 + 3 * k : 21 + 3 * k, PIX + k * LANES : PIX + (k + 1) * LANES] = 1.0
    narrow = np.zeros((16, PIX), np.float32)
    for number, mono in enumerate((np.ones(PIX), x, y, x * x, x * y, y * y)):
        narrow[number] = mono
    return jnp.asarray(wide, jnp.bfloat16), jnp.asarray(narrow, jnp.bfloat16)


def chunk_buffers():
    chunks = buffer(DEVICES, FEATS, LANES)
    return [chunks, chunks, pltpu.SemaphoreType.DMA, pltpu.SemaphoreType.DMA]


def shade(params, index, tile_lists, target):
    wide, narrow = expand_table()
    return run_kernel(
        shade_kernel,
        [jax.ShapeDtypeStruct((3 * TILE_DEV, PIX), jnp.float32), table(TABLE_ROWS)],
        [
            buffer(LIST, LANES),
            buffer(LANES, LANES, dtype=jnp.int32),
            buffer(TABLE_ROWS, LANES),
            buffer(LANES, LANES, dtype=jnp.int32),
            buffer(LANES, LANES, dtype=jnp.int32),
            buffer(TABLE_ROWS, LANES),
            buffer(BLOCKS * PROWS, LANES),
            buffer(VIEWS * FEATS * BLOCKS, LANES),
            buffer(80, LANES),
        ]
        + chunk_buffers()
        + chunk_buffers()
        + [
            buffer(FEATS * LANES, LANES),
            buffer(LANES * KPITCH, LANES),
            buffer(GROUP_ROWS, PIX),
            buffer(GROUP_ROWS, PIX),
            buffer(GROUP_ROWS, 3 * LANES),
            buffer(GROUP_ROWS, 4 * PIX, dtype=jnp.bfloat16),
            buffer(FEATS * LANES, LANES),
            buffer(LANES * GRADS, LANES),
            buffer(len(DOT_IN) * LANES, 3 * LANES, dtype=jnp.bfloat16),
            buffer(len(DOT_OUT) * LANES // 2, 2 * LANES),
        ],
        params,
        index,
        tile_lists,
        target,
        wide,
        narrow,
        collective_id=0,
    )


def owner_update(back, index, params, first, second):
    shape = jax.ShapeDtypeStruct(params.shape, jnp.float32)
    return run_kernel(
        update_kernel,
        [shape] * 3,
        [
            buffer(BLOCKS * PROWS, LANES),
            buffer(VIEWS * FEATS * BLOCKS, LANES),
            buffer(BLOCKS * PROWS, LANES),
            buffer(3 * VIEWS * BLOCKS, LANES),
        ],
        back,
        index,
        params,
        first,
        second,
    )


def per_device(params, first_moment, second_moment, target_images, tile_lists, send_index):
    index = send_index[0]
    target = target_images.transpose(1, 0, 2).reshape(3 * TILE_DEV, PIX)
    image, back = shade(params, index, tile_lists, target)
    new_params, new_first, new_second = owner_update(back, index, params, first_moment, second_moment)
    image = image.reshape(3, TILE_DEV, PIX).transpose(1, 0, 2)
    return (image, new_params, new_first, new_second)


def solution(mesh):
    in_specs = (
        P(None, AXES),
        P(None, AXES),
        P(None, AXES),
        P(AXES, None, None),
        P(AXES, None),
        P(AXES, None, None),
    )
    out_specs = (P(AXES, None, None), P(None, AXES), P(None, AXES), P(None, AXES))
    return jax.shard_map(
        per_device, mesh=mesh, in_specs=in_specs, out_specs=out_specs, check_vma=False
    )
```

```python
import functools
import math

import jax
import jax.numpy as jnp
import numpy as np
from jax import lax
from jax.experimental import pallas as pl
from jax.experimental.pallas import tpu as pltpu
from jax.sharding import PartitionSpec as P

PARAMS = 59
PIX = 256
VIEWS = 16
LIST = 512
TILE_DEV = 32
GS_DEV = 2048
DEVICES = 128
CAP = 128
TABLE_ROWS = 1168
FEATS = 9
BLOCKS = 16
PROWS = 65
LANES = 128
SLABS = 4
LOG2E = 1.4426950408889634
AXES = ("gauss", "render")
CONTRACT = (((1,), (1,)), ((), ()))
VMEM_LIMIT = 56 * 1024 * 1024

sh_first = 0.28209479177387814
sh_second = 0.4886025119029199
sh_third = (
    1.0925484305920792,
    -1.0925484305920792,
    0.31539156525252005,
    -1.0925484305920792,
    0.5462742152960396,
)
sh_fourth = (
    -0.5900435899266435,
    2.890611442640554,
    -0.4570457994644658,
    0.3731763325901154,
    -0.4570457994644658,
    1.445305721320277,
    -0.5900435899266435,
)
tilt_reach = 0.25
beta_one = 0.9
beta_two = 0.999
adam_epsilon = 1e-15
adam_count = 1000.0


def rate_table():
    row = lax.broadcasted_iota(jnp.int32, (PARAMS, LANES), 0)
    rates = jnp.where((row == 11) | (row == 27) | (row == 43), 0.0025, 0.000125)
    rates = jnp.where(row == 10, 0.05, rates)
    for last, rate in ((10, 0.001), (6, 0.005), (3, 0.0016)):
        rates = jnp.where(row < last, rate, rates)
    return rates.astype(jnp.float32)


def sh_basis(dir_x, dir_y, dir_z):
    sq_x = dir_x * dir_x
    sq_y = dir_y * dir_y
    sq_z = dir_z * dir_z
    return [
        sh_first,
        -sh_second * dir_y,
        sh_second * dir_z,
        -sh_second * dir_x,
        sh_third[0] * dir_x * dir_y,
        sh_third[1] * dir_y * dir_z,
        sh_third[2] * (2.0 * sq_z - sq_x - sq_y),
        sh_third[3] * dir_x * dir_z,
        sh_third[4] * (sq_x - sq_y),
        sh_fourth[0] * dir_y * (3.0 * sq_x - sq_y),
        sh_fourth[1] * dir_x * dir_y * dir_z,
        sh_fourth[2] * dir_y * (4.0 * sq_z - sq_x - sq_y),
        sh_fourth[3] * dir_z * (2.0 * sq_z - 3.0 * sq_x - 3.0 * sq_y),
        sh_fourth[4] * dir_x * (4.0 * sq_z - sq_x - sq_y),
        sh_fourth[5] * dir_z * (sq_x - sq_y),
        sh_fourth[6] * dir_x * (sq_x - 3.0 * sq_y),
    ]


def camera_constants(camera):
    angle = camera * (2.0 * math.pi / VIEWS)
    lean_x = tilt_reach * math.cos(angle)
    lean_y = tilt_reach * math.sin(angle)
    length = math.sqrt(1.0 + lean_x * lean_x + lean_y * lean_y)
    basis = sh_basis(lean_x / length, lean_y / length, -1.0 / length)
    return (lean_x, lean_y, 16.0 * (camera % 4), 16.0 * (camera // 4), basis)


CAMERAS = [camera_constants(camera) for camera in range(VIEWS)]


def spread(log_scales, quat):
    squares = [jnp.exp(2.0 * value) for value in log_scales]
    norm = jnp.sqrt(quat[0] * quat[0] + quat[1] * quat[1] + quat[2] * quat[2] + quat[3] * quat[3])
    q_w, q_x, q_y, q_z = [part / norm for part in quat]
    rotation = [
        [
            1.0 - 2.0 * (q_y * q_y + q_z * q_z),
            2.0 * (q_x * q_y - q_w * q_z),
            2.0 * (q_x * q_z + q_w * q_y),
        ],
        [
            2.0 * (q_x * q_y + q_w * q_z),
            1.0 - 2.0 * (q_x * q_x + q_z * q_z),
            2.0 * (q_y * q_z - q_w * q_x),
        ],
        [
            2.0 * (q_x * q_z - q_w * q_y),
            2.0 * (q_y * q_z + q_w * q_x),
            1.0 - 2.0 * (q_x * q_x + q_y * q_y),
        ],
    ]
    return [
        rotation[row][0] * rotation[col][0] * squares[0]
        + rotation[row][1] * rotation[col][1] * squares[1]
        + rotation[row][2] * rotation[col][2] * squares[2]
        for row, col in ((0, 0), (0, 1), (0, 2), (1, 1), (1, 2), (2, 2))
    ]


def conic_of(sigma, lean_x, lean_y):
    s_xx, s_xy, s_xz, s_yy, s_yz, s_zz = sigma
    cov_xx = s_xx + (2.0 * lean_x) * s_xz + (lean_x * lean_x) * s_zz + 0.3
    cov_xy = s_xy + lean_x * s_yz + lean_y * s_xz + (lean_x * lean_y) * s_zz
    cov_yy = s_yy + (2.0 * lean_y) * s_yz + (lean_y * lean_y) * s_zz + 0.3
    inverse = 1.0 / (cov_xx * cov_yy - cov_xy * cov_xy)
    return cov_yy * inverse, -cov_xy * inverse, cov_xx * inverse


def raw_colour(row, basis, channel):
    total = 0.5 + row(11 + 16 * channel) * basis[0]
    for term in range(1, 16):
        total = total + row(11 + 16 * channel + term) * basis[term]
    return total


def block_rows(source, dest):
    rows = source.shape[0]
    for block in range(BLOCKS):
        dest[pl.ds(block * PROWS, rows), :] = source[:, pl.ds(block * LANES, LANES)]


def strided(ref, row):
    return ref[pl.ds(row, BLOCKS, stride=PROWS), :]


def parts_of(value, count):
    parts = []
    for step in range(count):
        part = value.astype(jnp.bfloat16)
        parts.append(part)
        if step + 1 < count:
            value = value - part.astype(jnp.float32)
    return parts


MESH = pl.DeviceIdType.MESH


def own_number():
    return lax.axis_index(AXES[0]) * lax.axis_size(AXES[1]) + lax.axis_index(AXES[1])


def coordinates(number):
    across = lax.axis_size(AXES[1])
    return (number // across, lax.rem(number, across))


def announce():
    me = own_number()
    barrier = pltpu.get_barrier_semaphore()

    def tell(step, carry):
        pl.semaphore_signal(
            barrier,
            inc=1,
            device_id=coordinates(lax.rem(me + step, DEVICES)),
            device_id_type=MESH,
        )
        return carry

    lax.fori_loop(1, DEVICES, tell, 0, unroll=True)
    return barrier


def send_chunk(target, me, send_ref, recv_ref, send_sem, recv_sem):
    pltpu.make_async_remote_copy(
        src_ref=send_ref.at[target],
        dst_ref=recv_ref.at[me],
        send_sem=send_sem,
        recv_sem=recv_sem,
        device_id=coordinates(target),
        device_id_type=MESH,
    ).start()


def all_chunks(me, send_ref, recv_ref, send_sem, recv_sem):
    most = pl.ds(0, DEVICES - 1)
    return pltpu.make_async_remote_copy(
        src_ref=send_ref.at[most],
        dst_ref=recv_ref.at[most],
        send_sem=send_sem,
        recv_sem=recv_sem,
        device_id=coordinates(me),
        device_id_type=MESH,
    )


def flatten_chunks(recv_ref, out_ref):
    for source in range(DEVICES):
        out_ref[pl.ds(source * FEATS, FEATS), :] = recv_ref[source]


def order_lists(tile_ref, turned_ref, list_ref):
    gap = jnp.zeros((LANES - 8, LANES), jnp.float32)
    for slab in range(SLABS):
        for block in range(LIST // LANES):
            part = tile_ref[pl.ds(slab * 8, 8), pl.ds(block * LANES, LANES)].astype(jnp.float32)
            turned_ref[pl.ds(block * LANES, LANES), :] = jnp.concatenate([part, gap], 0).T
        total = turned_ref[pl.ds(0, 32, stride=16), :]
        for place in range(1, 16):
            total = total + pltpu.roll(turned_ref[pl.ds(place, 32, stride=16), :], 8 * place, axis=1)
        list_ref[pl.ds(slab * 32, 32), :] = total.astype(jnp.int32)


def invert_lists(list_ref, lane_ref, row_ref):
    sublane = lax.broadcasted_iota(jnp.int32, (LANES, LANES), 0)
    lane = lax.broadcasted_iota(jnp.int32, (LANES, LANES), 1).astype(jnp.float32)

    def step(pair, total):
        owners, slots = [], []
        for member in range(2):
            line = list_ref[pl.ds(pair * 2 + member, 1), :]
            low = jnp.broadcast_to(jnp.bitwise_and(line, CAP - 1), (LANES, LANES))
            high = jnp.broadcast_to(jnp.right_shift(line, 7), (LANES, LANES))
            number = (pair * 2 + member + 1).astype(jnp.float32)
            owners.append(jnp.where(high == sublane, 1.0, 0.0).astype(jnp.bfloat16))
            same = low == sublane
            slots.append(
                jnp.concatenate([jnp.where(same, lane, 0.0), jnp.where(same, number, 0.0)], 0).astype(
                    jnp.bfloat16
                )
            )
        return total + lax.dot_general(
            jnp.concatenate(owners, 1),
            jnp.concatenate(slots, 1),
            CONTRACT,
            preferred_element_type=jnp.float32,
        )

    total = lax.fori_loop(0, LANES // 2, step, jnp.zeros((LANES, 2 * LANES), jnp.float32), unroll=8)
    lane_ref[...] = total[:, :LANES].astype(jnp.int32)
    row_ref[...] = total[:, LANES:].astype(jnp.int32) - 1


def deliver(
    params_ref, index_ref, tile_ref, turned_ref, list_ref,
    out_ref, lane_ref, row_ref,
    rows_ref, table_ref, flat_ref, send_ref, recv_ref, send_sem, recv_sem,
):
    me = own_number()
    barrier = announce()
    block_rows(params_ref, rows_ref)
    row = functools.partial(strided, rows_ref)
    sigma = spread([row(3 + k) for k in range(3)], [row(6 + k) for k in range(4)])
    logit = row(10)
    log_opacity = -LOG2E * (jnp.maximum(-logit, 0.0) + jnp.log1p(jnp.exp(-jnp.abs(logit))))
    for camera in range(VIEWS):
        lean_x, lean_y, shift_x, shift_y, basis = CAMERAS[camera]
        height = row(2)
        features = [row(0) + lean_x * height - shift_x, row(1) + lean_y * height - shift_y]
        features += list(conic_of(sigma, lean_x, lean_y))
        features.append(log_opacity)
        features += [jnp.maximum(raw_colour(row, basis, k), 0.0) for k in range(3)]
        for f in range(FEATS):
            table_ref[pl.ds((camera * FEATS + f) * BLOCKS, BLOCKS), :] = features[f]
    pl.semaphore_wait(barrier, DEVICES - 1)

    @pl.loop(0, VIEWS)
    def _(turn):
        camera = lax.rem(me // (DEVICES // VIEWS) + turn, VIEWS)
        chosen = index_ref[pl.ds(pl.multiple_of(camera * 8, 8), 8), :]
        low = jnp.bitwise_and(chosen, LANES - 1)
        high = jnp.right_shift(chosen, 7)
        totals = [jnp.zeros((8, LANES), jnp.float32) for _ in range(FEATS)]
        for block in range(BLOCKS):
            here = high == block
            for f in range(FEATS):
                line = table_ref[pl.ds((camera * FEATS + f) * BLOCKS + block, 1), :]
                line = jnp.broadcast_to(line, (8, LANES))
                picked = jnp.take_along_axis(line, low, axis=1)
                totals[f] = jnp.where(here, picked, totals[f])
        for f in range(FEATS):
            flat_ref[pl.ds(f, 8, stride=FEATS), :] = totals[f]
        for member in range(8):
            send_ref[camera * 8 + member] = flat_ref[pl.ds(member * FEATS, FEATS), :]
        for step in range(8):
            target = camera * 8 + lax.rem(me + step, 8)

            @pl.when(target != me)
            def _():
                send_chunk(target, me, send_ref, recv_ref, send_sem, recv_sem)

    order_lists(tile_ref, turned_ref, list_ref)
    invert_lists(list_ref, lane_ref, row_ref)
    whole = all_chunks(me, send_ref, recv_ref, send_sem, recv_sem)
    recv_ref[me] = send_ref[me]
    whole.wait_recv()
    flatten_chunks(recv_ref, out_ref)
    whole.wait_send()


def give_back(back_ref, out_ref, send_ref, recv_ref, send_sem, recv_sem):
    me = own_number()
    for target in range(DEVICES):
        send_ref[target] = back_ref[pl.ds(target * FEATS, FEATS), :]

    def send(step, carry):
        send_chunk(lax.rem(me + step, DEVICES), me, send_ref, recv_ref, send_sem, recv_sem)
        return carry

    lax.fori_loop(1, DEVICES, send, 0, unroll=8)
    whole = all_chunks(me, send_ref, recv_ref, send_sem, recv_sem)
    recv_ref[me] = send_ref[me]
    whole.wait_recv()
    flatten_chunks(recv_ref, out_ref)
    whole.wait_send()


def picked_lanes(table, first, low, high, base, count, totals):
    for step in range(count):
        source = base + step
        here = high == source
        for number, place in enumerate(first):
            line = jnp.broadcast_to(table[pl.ds(place(source), 1), :], (8, LANES))
            picked = jnp.take_along_axis(line, low, axis=1)
            totals[number] = jnp.where(here, picked, totals[number])
    return totals


LANE_IN = (0, 1, 5)
DOT_IN = (2, 3, 4, 6, 7, 8)
LANE_OUT = (0, 1, 5)
DOT_OUT = (2, 3, 4, 6, 7, 8)
KROWS = 32
KPITCH = 40
GRADS = 24
GROUP_ROWS = LIST * 8


def composite(
    table_ref,
    list_ref,
    lane_ref,
    row_ref,
    target_ref,
    expand_ref,
    mono_ref,
    image_ref,
    back_ref,
    feat_ref,
    coef_ref,
    alpha_ref,
    weight_ref,
    colour_ref,
    push_ref,
    grad_ref,
    moment_ref,
    halves_ref,
    sums_ref,
):
    render = lax.axis_index(AXES[1])
    device = lax.axis_index(AXES[0]) * lax.axis_size(AXES[1]) + render
    strip = lax.rem(device, DEVICES // VIEWS)
    lane_tile = jnp.bitwise_and(lax.broadcasted_iota(jnp.int32, (8, LANES), 1), 7)
    centre_x = 16.0 * lane_tile.astype(jnp.float32) + 8.0

    owner = lax.broadcasted_iota(jnp.int32, (LANES, 2 * LANES), 0)
    for number, f in enumerate(DOT_IN):
        value = table_ref[pl.ds(f, DEVICES, stride=FEATS), :]
        for which, part in enumerate(parts_of(value, 3)):
            halves_ref[pl.ds(number * LANES, LANES), pl.ds(which * LANES, LANES)] = part

    def collect(count, totals):
        octet = count // 4
        quarter = lax.rem(count, 4)
        span = pl.ds(pl.multiple_of(octet * 8, 8), 8)
        low = jnp.bitwise_and(list_ref[span, :], CAP - 1)
        high = jnp.right_shift(list_ref[span, :], 7)
        totals = [jnp.where(quarter == 0, 0.0, total) for total in totals]
        first = [lambda source, f=f: source * FEATS + f for f in LANE_IN]
        totals = picked_lanes(table_ref, first, low, high, quarter * 32, 32, totals)
        for number, f in enumerate(LANE_IN):
            feat_ref[pl.ds(pl.multiple_of(f * LANES + octet * 8, 8), 8), :] = totals[number]
        lines = [list_ref[pl.ds(count * 2 + member, 1), :] for member in range(2)]
        line = jnp.broadcast_to(jnp.concatenate(lines, 1), (LANES, 2 * LANES))
        slot = jnp.where(jnp.bitwise_and(line, CAP - 1) == owner, 1.0, 0.0).astype(jnp.bfloat16)
        thrice = jnp.concatenate([slot, slot, slot], 0)
        exact = jnp.dot(
            halves_ref[pl.ds(0, 3 * LANES), :], thrice, preferred_element_type=jnp.float32
        )
        other = jnp.dot(
            halves_ref[pl.ds(3 * LANES, 3 * LANES), pl.ds(0, 2 * LANES)],
            thrice[: 2 * LANES],
            preferred_element_type=jnp.float32,
        )
        found = [exact[k * LANES : (k + 1) * LANES] for k in range(3)]
        found += [other[k * LANES : (k + 1) * LANES] for k in range(3)]
        mine = jnp.right_shift(line, 7) == owner
        for number, f in enumerate(DOT_IN):
            value = jnp.where(mine, found[number], 0.0)
            value = jnp.sum(value, 0, keepdims=True)
            for member in range(2):
                feat_ref[pl.ds(f * LANES + count * 2 + member, 1), :] = value[
                    :, member * LANES : (member + 1) * LANES
                ]
        return tuple(totals)

    blank = tuple(jnp.zeros((8, LANES), jnp.float32) for _ in LANE_IN)
    lax.fori_loop(0, LANES // 2, collect, blank, unroll=8)
    zero = jnp.zeros((8, LANES), jnp.float32)

    @pl.loop(0, 16)
    def _(octet):
        base = pl.multiple_of(octet * 8, 8)
        feature = [feat_ref[pl.ds(pl.multiple_of(f * LANES + octet * 8, 8), 8), :] for f in range(FEATS)]
        live = list_ref[pl.ds(base, 8), :] >= 0
        centre_y = (16 * (strip * SLABS + octet // 4) + 8).astype(jnp.float32)
        m_x = feature[0] - centre_x
        m_y = feature[1] - centre_y
        a = (-0.5 * LOG2E) * feature[2]
        b = -LOG2E * feature[3]
        c = (-0.5 * LOG2E) * feature[4]
        to_x = 2.0 * a * m_x + b * m_y
        to_y = b * m_x + 2.0 * c * m_y
        level = a * m_x * m_x + b * m_x * m_y + c * m_y * m_y
        level = jnp.where(live, level + feature[5], -10000.0)
        values = [a, b, c, -to_x, -to_y, level] + feature[6:9]
        place = 0
        for value in values:
            for part in parts_of(value, 3):
                coef_ref[pl.ds(octet * 8 * KPITCH + place, 8, stride=KPITCH), :] = part.astype(jnp.float32)
                place += 1
        for rest in range(place, KROWS):
            coef_ref[pl.ds(octet * 8 * KPITCH + rest, 8, stride=KPITCH), :] = zero

    diagonal = lax.broadcasted_iota(jnp.int32, (8, LANES), 0) == lane_tile

    @pl.loop(0, SLABS)
    def _(group):
        @pl.loop(0, 8, unroll=8)
        def _(quad):
            lefts = []
            for sub in range(4):
                start = pl.multiple_of((group * 32 + quad * 4 + sub) * KPITCH, 8)
                lefts.append(coef_ref[pl.ds(start, KROWS), :].T.astype(jnp.bfloat16))
            wide = jnp.dot(jnp.concatenate(lefts, 0), expand_ref[...], preferred_element_type=jnp.float32)
            out = pl.ds(pl.multiple_of(quad * 512, 512), 512)
            alpha_ref[out, :] = wide[:, :PIX]
            colour_ref[out, :] = wide[:, PIX:]

        def forward(block, carry):
            through = list(carry[:2])
            image = list(carry[2:])
            for lot in range(2):
                alphas, weights, spots = [], [], []
                for u in range(8):
                    here = pl.ds(pl.multiple_of(block * LANES + (lot * 8 + u) * 8, 8), 8)
                    spots.append(here)
                    alphas.append(
                        [
                            jnp.minimum(jnp.exp2(alpha_ref[here, pl.ds(half * LANES, LANES)]), 0.99)
                            for half in range(2)
                        ]
                    )
                for u in range(8):
                    shade = [colour_ref[spots[u], pl.ds(k * LANES, LANES)] for k in range(3)]
                    weights.append([])
                    for half in range(2):
                        weight = alphas[u][half] * through[half]
                        through[half] = through[half] * (1.0 - alphas[u][half])
                        weights[u].append(weight)
                        for k in range(3):
                            image[k * 2 + half] = image[k * 2 + half] + shade[k] * weight
                for u in range(8):
                    for half in range(2):
                        cols = pl.ds(half * LANES, LANES)
                        alpha_ref[spots[u], cols] = alphas[u][half]
                        weight_ref[spots[u], cols] = weights[u][half]
            return tuple(through + image)

        ones = jnp.ones((8, LANES), jnp.float32)
        image = lax.fori_loop(0, 32, forward, (ones, ones) + (zero,) * 6, unroll=2)[2:]
        residual = []
        for k in range(3):
            tiles = pl.ds(pl.multiple_of(k * TILE_DEV + group * 8, 8), 8)
            for half in range(2):
                cols = pl.ds(half * LANES, LANES)
                image_ref[tiles, cols] = image[k * 2 + half]
                residual.append(image[k * 2 + half] - target_ref[tiles, cols])

        def backward(count, carry):
            behind = list(carry)
            block = 31 - count
            for pair in range(7, -1, -1):
                pushes = [[None, None], [None, None]]
                loads = [[None, None], [None, None]]
                for member in (1, 0):
                    here = pl.ds(pl.multiple_of(block * LANES + pair * 16 + member * 8, 8), 8)
                    shade = [colour_ref[here, pl.ds(k * LANES, LANES)] for k in range(3)]
                    for half in range(2):
                        cols = pl.ds(half * LANES, LANES)
                        alpha = alpha_ref[here, cols]
                        weight = weight_ref[here, cols]
                        worth = (
                            shade[0] * residual[half]
                            + shade[1] * residual[2 + half]
                            + shade[2] * residual[4 + half]
                        )
                        loads[half][member] = weight
                        gain = worth - behind[half]
                        behind[half] = behind[half] + alpha * gain
                        pushes[half][member] = jnp.where(alpha < 0.99, weight * gain, 0.0)
                rows = pl.ds(pl.multiple_of(block * LANES + pair * 16, 16), 16)
                for half in range(2):
                    parts = parts_of(jnp.concatenate(pushes[half], 0), 2)
                    parts += parts_of(jnp.concatenate(loads[half], 0), 2)
                    for which, part in enumerate(parts):
                        push_ref[rows, pl.ds(which * PIX + half * LANES, LANES)] = part
            return tuple(behind)

        lax.fori_loop(0, 32, backward, (zero, zero))
        stack = jnp.concatenate(
            [jnp.concatenate([residual[k * 2], residual[k * 2 + 1]], 1) for k in range(3)], 0
        )
        stack = jnp.concatenate(parts_of(stack, 2), 0)
        stack = jnp.concatenate([stack, stack], 1)
        powers = jnp.concatenate([mono_ref[...], mono_ref[...]], 1)

        @pl.loop(0, 1)
        def _(chunk):
            rows = pl.ds(pl.multiple_of(chunk * 4096, 4096), 4096)
            moments = lax.dot_general(
                powers, push_ref[rows, pl.ds(0, 2 * PIX)], CONTRACT, preferred_element_type=jnp.float32
            )
            tints = lax.dot_general(
                stack, push_ref[rows, pl.ds(2 * PIX, 2 * PIX)], CONTRACT, preferred_element_type=jnp.float32
            )
            tints = tints[:24] + tints[24:]
            for line in range(32):
                cols = slice(line * LANES, (line + 1) * LANES)
                base = ((group * 32) + chunk * 32 + line) * GRADS
                moment_ref[pl.ds(pl.multiple_of(base, 8), 8), :] = moments[:8, cols]
                for k in range(3):
                    own = jnp.where(diagonal, tints[k * 8 : k * 8 + 8, cols], 0.0)
                    moment_ref[pl.ds(base + 8 + k, 1), :] = jnp.sum(own, 0, keepdims=True)

    @pl.loop(0, 16)
    def _(octet):
        feature = [feat_ref[pl.ds(pl.multiple_of(f * LANES + octet * 8, 8), 8), :] for f in range(5)]
        centre_y = (16 * (strip * SLABS + octet // 4) + 8).astype(jnp.float32)
        m_x = feature[0] - centre_x
        m_y = feature[1] - centre_y

        def moment(k):
            return moment_ref[pl.ds(octet * 8 * GRADS + k, 8, stride=GRADS), :]

        total, s_x, s_y, s_xx, s_xy, s_yy = [moment(k) for k in range(6)]
        along_x = s_x - m_x * total
        along_y = s_y - m_y * total
        results = [
            feature[2] * along_x + feature[3] * along_y,
            feature[3] * along_x + feature[4] * along_y,
            -0.5 * (s_xx - m_x * (s_x + along_x)),
            -(s_xy - m_x * s_y - m_y * along_x),
            -0.5 * (s_yy - m_y * (s_y + along_y)),
            total,
            moment(8),
            moment(9),
            moment(10),
        ]
        for f in range(FEATS):
            grad_ref[pl.ds(pl.multiple_of(f * LANES + octet * 8, 8), 8), :] = results[f]

    sums_ref[...] = jnp.zeros(sums_ref.shape, jnp.float32)
    half_owner = lax.broadcasted_iota(jnp.int32, (LANES // 2, LANES), 0)
    place = lax.broadcasted_iota(jnp.int32, (2 * LANES, LANES), 0)

    def spread_out(count, totals):
        octet = count // 4
        quarter = lax.rem(count, 4)
        span = pl.ds(pl.multiple_of(octet * 8, 8), 8)
        totals = [jnp.where(quarter == 0, 0.0, total) for total in totals]
        first = [lambda source, f=f: f * LANES + source for f in LANE_OUT]
        totals = picked_lanes(
            grad_ref, first, lane_ref[span, :], row_ref[span, :], quarter * 32, 32, totals
        )
        for number, f in enumerate(LANE_OUT):
            back_ref[pl.ds(octet * 8 * FEATS + f, 8, stride=FEATS), :] = totals[number]
        slots = []
        owners = []
        for member in range(2):
            line = list_ref[pl.ds(count * 2 + member, 1), :]
            half = jnp.bitwise_and(jnp.right_shift(line, 7), LANES // 2 - 1)
            half = jnp.where(line < 0, -1, half)
            spot = jnp.right_shift(line, 13) * LANES + jnp.bitwise_and(line, CAP - 1)
            owners.append(jnp.broadcast_to(half, (LANES // 2, LANES)) == half_owner)
            same = jnp.broadcast_to(spot, (2 * LANES, LANES)) == place
            slots.append(jnp.where(same, 1.0, 0.0).astype(jnp.bfloat16))
        rows = []
        for f in DOT_OUT:
            lines = [grad_ref[pl.ds(f * LANES + count * 2 + member, 1), :] for member in range(2)]
            tops = [line.astype(jnp.bfloat16).astype(jnp.float32) for line in lines]
            pieces = tops + [line - top for line, top in zip(lines, tops)]
            rows.append(
                jnp.concatenate(
                    [
                        jnp.where(
                            owners[number % 2], jnp.broadcast_to(piece, (LANES // 2, LANES)), 0.0
                        ).astype(jnp.bfloat16)
                        for number, piece in enumerate(pieces)
                    ],
                    1,
                )
            )
        sums_ref[...] += lax.dot_general(
            jnp.concatenate(rows, 0),
            jnp.concatenate(slots + slots, 1),
            CONTRACT,
            preferred_element_type=jnp.float32,
        )
        return tuple(totals)

    blank = tuple(jnp.zeros((8, LANES), jnp.float32) for _ in LANE_OUT)
    lax.fori_loop(0, LANES // 2, spread_out, blank, unroll=8)
    for number, f in enumerate(DOT_OUT):
        for side in range(2):
            back_ref[pl.ds(side * (LANES // 2) * FEATS + f, LANES // 2, stride=FEATS), :] = sums_ref[
                pl.ds(number * (LANES // 2), LANES // 2), pl.ds(side * LANES, LANES)
            ]


def shade_kernel(params_ref, index_ref, tile_ref, target_ref, expand_ref, mono_ref, image_ref, out_ref, *scratch):
    turned_ref, list_ref = scratch[:2]
    scratch = scratch[2:]
    received_ref, lane_ref, row_ref, back_ref = scratch[:4]
    deliver(params_ref, index_ref, tile_ref, turned_ref, list_ref, received_ref, lane_ref, row_ref, *scratch[4:11])
    composite(
        received_ref, list_ref, lane_ref, row_ref, target_ref, expand_ref, mono_ref,
        image_ref, back_ref, *scratch[15:],
    )
    give_back(back_ref, out_ref, *scratch[11:15])


SUM_PARTS = 2


def update_kernel(
    back_ref, index_ref, params_ref, first_ref, second_ref,
    new_params_ref, new_first_ref, new_second_ref,
    rows_ref, sums_ref, slope_ref, tint_ref,
):
    block_rows(params_ref, rows_ref)
    row = functools.partial(strided, rows_ref)
    sublane = lax.broadcasted_iota(jnp.int32, (LANES, LANES), 0)
    short = lax.broadcasted_iota(jnp.int32, (BLOCKS, LANES), 0)

    @pl.loop(0, VIEWS, unroll=4)
    def _(camera):
        total = jnp.zeros((SUM_PARTS * FEATS * BLOCKS, LANES), jnp.float32)
        for pair in range(4):
            places, values = [], []
            for member in range(2):
                renderer = camera * 8 + pair * 2 + member
                line = index_ref[pl.ds(renderer, 1), :]
                low = jnp.broadcast_to(jnp.bitwise_and(line, LANES - 1), (LANES, LANES))
                high = jnp.broadcast_to(jnp.right_shift(line, 7), (BLOCKS, LANES))
                places.append(jnp.where(low == sublane, 1.0, 0.0).astype(jnp.bfloat16))
                here = high == short
                stacks = []
                for f in range(FEATS):
                    value = jnp.broadcast_to(back_ref[pl.ds(renderer * FEATS + f, 1), :], (BLOCKS, LANES))
                    stacks.append(jnp.where(here, value, 0.0))
                stack = jnp.concatenate(stacks, 0)
                values.append(jnp.concatenate(parts_of(stack, SUM_PARTS), 0))
            total = total + lax.dot_general(
                jnp.concatenate(values, 1),
                jnp.concatenate(places, 1),
                (((1,), (1,)), ((), ())),
                preferred_element_type=jnp.float32,
            )
        size = FEATS * BLOCKS
        merged = total[:size]
        for part in range(1, SUM_PARTS):
            merged = merged + total[part * size : (part + 1) * size]
        sums_ref[pl.ds(pl.multiple_of(camera * size, size), size), :] = merged

    logs = [row(3 + k) for k in range(3)]
    quat = [row(6 + k) for k in range(4)]
    sigma, spread_pull = jax.vjp(spread, logs, quat)
    blank = jnp.zeros((BLOCKS, LANES), jnp.float32)
    d_sigma = [blank] * 6
    d_x, d_y, d_z, d_log = blank, blank, blank, blank
    for camera in range(VIEWS):
        lean_x, lean_y, _, _, basis = CAMERAS[camera]

        def pushed(f):
            return sums_ref[pl.ds((camera * FEATS + f) * BLOCKS, BLOCKS), :]

        d_x = d_x + pushed(0)
        d_y = d_y + pushed(1)
        d_z = d_z + lean_x * pushed(0) + lean_y * pushed(1)
        _, pull = jax.vjp(lambda values: conic_of(values, lean_x, lean_y), sigma)
        (more,) = pull((pushed(2), pushed(3), pushed(4)))
        d_sigma = [old + new for old, new in zip(d_sigma, more)]
        d_log = d_log + pushed(5)
        for k in range(3):
            raw = raw_colour(row, basis, k)
            gate = jnp.where(raw > 0.0, 1.0, jnp.where(raw == 0.0, 0.5, 0.0))
            tint_ref[pl.ds((k * VIEWS + camera) * BLOCKS, BLOCKS), :] = gate * pushed(6 + k)
    d_scale, d_quat = spread_pull(d_sigma)
    slopes = [d_x, d_y, d_z] + list(d_scale) + list(d_quat) + [d_log / (1.0 + jnp.exp(row(10)))]
    for number, slope in enumerate(slopes):
        slope_ref[pl.ds(number, BLOCKS, stride=PROWS), :] = slope
    for k in range(3):
        for term in range(16):
            slope = blank
            for camera in range(VIEWS):
                tint = tint_ref[pl.ds((k * VIEWS + camera) * BLOCKS, BLOCKS), :]
                slope = slope + CAMERAS[camera][4][term] * tint
            slope_ref[pl.ds(11 + 16 * k + term, BLOCKS, stride=PROWS), :] = slope
    rates = rate_table()
    for block in range(BLOCKS):
        cols = pl.ds(block * LANES, LANES)
        slope = slope_ref[pl.ds(block * PROWS, PARAMS), :]
        new_first = beta_one * first_ref[:, cols] + (1.0 - beta_one) * slope
        new_second = beta_two * second_ref[:, cols] + (1.0 - beta_two) * slope * slope
        first_hat = new_first * (1.0 / (1.0 - beta_one**adam_count))
        second_hat = new_second * (1.0 / (1.0 - beta_two**adam_count))
        new_first_ref[:, cols] = new_first
        new_second_ref[:, cols] = new_second
        new_params_ref[:, cols] = params_ref[:, cols] - rates * first_hat / (
            jnp.sqrt(second_hat) + adam_epsilon
        )


WHOLE = pl.BlockSpec(memory_space=pltpu.VMEM)


def run_kernel(kernel, shapes, scratch, *operands, collective_id=None):
    many = isinstance(shapes, list)
    extra = {}
    if collective_id is not None:
        extra = dict(collective_id=collective_id, has_side_effects=True)
    return pl.pallas_call(
        kernel,
        out_shape=shapes,
        in_specs=[WHOLE] * len(operands),
        out_specs=[WHOLE] * len(shapes) if many else WHOLE,
        scratch_shapes=scratch,
        compiler_params=pltpu.CompilerParams(vmem_limit_bytes=VMEM_LIMIT, **extra),
    )(*operands)


def table(rows, dtype=jnp.float32):
    return jax.ShapeDtypeStruct((rows, LANES), dtype)


def buffer(*shape, dtype=jnp.float32):
    return pltpu.VMEM(shape, dtype)


def expand_table():
    x = np.arange(PIX) % 16 - 7.5
    y = np.arange(PIX) // 16 - 7.5
    wide = np.zeros((KROWS, PIX + 3 * LANES), np.float32)
    for number, mono in enumerate((x * x, x * y, y * y, x, y, np.ones(PIX))):
        wide[3 * number : 3 * number + 3, :PIX] = mono
    for k in range(3):
        wide[18 + 3 * k : 21 + 3 * k, PIX + k * LANES : PIX + (k + 1) * LANES] = 1.0
    narrow = np.zeros((16, PIX), np.float32)
    for number, mono in enumerate((np.ones(PIX), x, y, x * x, x * y, y * y)):
        narrow[number] = mono
    return jnp.asarray(wide, jnp.bfloat16), jnp.asarray(narrow, jnp.bfloat16)


def chunk_buffers():
    chunks = buffer(DEVICES, FEATS, LANES)
    return [chunks, chunks, pltpu.SemaphoreType.DMA, pltpu.SemaphoreType.DMA]


def shade(params, index, tile_lists, target):
    wide, narrow = expand_table()
    return run_kernel(
        shade_kernel,
        [jax.ShapeDtypeStruct((3 * TILE_DEV, PIX), jnp.float32), table(TABLE_ROWS)],
        [
            buffer(LIST, LANES),
            buffer(LANES, LANES, dtype=jnp.int32),
            buffer(TABLE_ROWS, LANES),
            buffer(LANES, LANES, dtype=jnp.int32),
            buffer(LANES, LANES, dtype=jnp.int32),
            buffer(TABLE_ROWS, LANES),
            buffer(BLOCKS * PROWS, LANES),
            buffer(VIEWS * FEATS * BLOCKS, LANES),
            buffer(80, LANES),
        ]
        + chunk_buffers()
        + chunk_buffers()
        + [
            buffer(FEATS * LANES, LANES),
            buffer(LANES * KPITCH, LANES),
            buffer(GROUP_ROWS, PIX),
            buffer(GROUP_ROWS, PIX),
            buffer(GROUP_ROWS, 3 * LANES),
            buffer(GROUP_ROWS, 4 * PIX, dtype=jnp.bfloat16),
            buffer(FEATS * LANES, LANES),
            buffer(LANES * GRADS, LANES),
            buffer(len(DOT_IN) * LANES, 3 * LANES, dtype=jnp.bfloat16),
            buffer(len(DOT_OUT) * LANES // 2, 2 * LANES),
        ],
        params,
        index,
        tile_lists,
        target,
        wide,
        narrow,
        collective_id=0,
    )


def owner_update(back, index, params, first, second):
    shape = jax.ShapeDtypeStruct(params.shape, jnp.float32)
    return run_kernel(
        update_kernel,
        [shape] * 3,
        [
            buffer(BLOCKS * PROWS, LANES),
            buffer(VIEWS * FEATS * BLOCKS, LANES),
            buffer(BLOCKS * PROWS, LANES),
            buffer(3 * VIEWS * BLOCKS, LANES),
        ],
        back,
        index,
        params,
        first,
        second,
    )


def per_device(params, first_moment, second_moment, target_images, tile_lists, send_index):
    index = send_index[0]
    target = target_images.transpose(1, 0, 2).reshape(3 * TILE_DEV, PIX)
    image, back = shade(params, index, tile_lists, target)
    new_params, new_first, new_second = owner_update(back, index, params, first_moment, second_moment)
    image = image.reshape(3, TILE_DEV, PIX).transpose(1, 0, 2)
    return (image, new_params, new_first, new_second)


def solution(mesh):
    in_specs = (
        P(None, AXES),
        P(None, AXES),
        P(None, AXES),
        P(AXES, None, None),
        P(AXES, None),
        P(AXES, None, None),
    )
    out_specs = (P(AXES, None, None), P(None, AXES), P(None, AXES), P(None, AXES))
    return jax.shard_map(
        per_device, mesh=mesh, in_specs=in_specs, out_specs=out_specs, check_vma=False
    )
```
